32 devices in a mesh: dp: 8 (over z, y), mp: 4 (over x, core).
Axes of the slice: x: 2, y: 2, z: 4, core: 2. Of those that a mesh axis runs over, the one named last changes fastest.
Arguments:
- tokens: bfloat16 [16384, 1024], P(('dp', 'mp')), may hold values from -6 to 6
- lengths: int32 [8, 8], P('dp'), may hold values from 0 to 2048, as said below
- norm1_gain: float32 [1024], replicated, may hold values from 0.5 to 1.5
- norm1_shift: float32 [1024], replicated, may hold values from -1.8 to 1.8
- query_weight: bfloat16 [1024, 1024], P(None, 'mp'), may hold values from -0.1875 to 0.1875
- query_bias: float32 [1024], P('mp'), may hold values from -1.8 to 1.8
- key_weight: bfloat16 [1024, 1024], P(None, 'mp'), may hold values from -0.1875 to 0.1875
- value_weight: bfloat16 [1024, 1024], P(None, 'mp'), may hold values from -0.1875 to 0.1875
- value_bias: float32 [1024], P('mp'), may hold values from -1.8 to 1.8
- head_scale: float32 [16], P('mp'), may hold values from 0.1 to 1.9
- output_weight: bfloat16 [1024, 1024], P('mp'), may hold values from -0.75 to 0.75
- output_bias: float32 [1024], replicated, may hold values from -1.8 to 1.8
- norm2_gain: float32 [1024], replicated, may hold values from 0.5 to 1.5
- norm2_shift: float32 [1024], replicated, may hold values from -1.8 to 1.8
- norm3_gain: float32 [1024], replicated, may hold values from 0.5 to 1.5
- norm3_shift: float32 [1024], replicated, may hold values from -1.8 to 1.8
- fc1_weight: bfloat16 [1024, 4096], P(None, 'mp'), may hold values from -0.1875 to 0.1875
- fc1_bias: float32 [4096], P('mp'), may hold values from -1.8 to 1.8
- mid_gain: float32 [4096], P('mp'), may hold values from 0.5 to 1.5
- mid_shift: float32 [4096], P('mp'), may hold values from -1.8 to 1.8
- fc2_weight: bfloat16 [4096, 1024], P('mp'), may hold values from -0.09375 to 0.09375
- fc2_bias: float32 [1024], replicated, may hold values from -1.8 to 1.8
- out_grad: bfloat16 [16384, 1024], P(('dp', 'mp')), may hold values from -6 to 6
Outputs:
- output: bfloat16 [16384, 1024], P(('dp', 'mp'))
- token_grad: float32 [16384, 1024], P(('dp', 'mp'))
- grad_norm1_gain: float32 [1024], replicated
- grad_norm1_shift: float32 [1024], replicated
- grad_query_weight: float32 [1024, 1024], P(None, 'mp')
- grad_query_bias: float32 [1024], P('mp')
- grad_key_weight: float32 [1024, 1024], P(None, 'mp')
- grad_value_weight: float32 [1024, 1024], P(None, 'mp')
- grad_value_bias: float32 [1024], P('mp')
- grad_head_scale: float32 [16], P('mp')
- grad_output_weight: float32 [1024, 1024], P('mp')
- grad_output_bias: float32 [1024], replicated
- grad_norm2_gain: float32 [1024], replicated
- grad_norm2_shift: float32 [1024], replicated
- grad_norm3_gain: float32 [1024], replicated
- grad_norm3_shift: float32 [1024], replicated
- grad_fc1_weight: float32 [1024, 4096], P(None, 'mp')
- grad_fc1_bias: float32 [4096], P('mp')
- grad_mid_gain: float32 [4096], P('mp')
- grad_mid_shift: float32 [4096], P('mp')
- grad_fc2_weight: float32 [4096, 1024], P('mp')
- grad_fc2_bias: float32 [1024], replicated
The draws below stay inside these ranges and needn't reach their ends.
Inputs may be any that keep to these rules, and one draw needn't show every extreme that they name: Each row's 8 lengths sum to at most 2048; the rest of the row is padding. Some rows hold a single sequence of exactly 2048 tokens in every draw.
All inputs are finite; a program needn't handle non-finite values.
Results may differ from the reference program's by a relative error of at most 0.023.
Values may be sent and summed in bfloat16 or wider, within the bound.
No kernel may reach another device: no remote copies, remote signals or barrier semaphores. Data moves between devices by JAX's collectives and lax.ppermute only.
A program may use at most 192 MiB of HBM per device.

```python
import jax
import jax.numpy as jnp
from jax import lax

D = 1024
HEADS = 16
HEAD_DIM = 64
FF = 4096
ROW = 2048
QBLOCK = 512
SLOTS = 8
NROWS = 8
TOKENS = 16384


def draw_lengths(key, part):
    key_fill = jax.random.fold_in(key, 11)
    key_cut = jax.random.fold_in(key, 23)
    padding = jax.random.randint(key_fill, (NROWS,), 0, ROW // 4 + 1)
    filled = ROW - padding
    cut_points = jax.random.randint(key_cut, (NROWS, SLOTS - 1), 0, filled[:, None] + 1)
    cut_points = jnp.sort(cut_points, axis=1)
    bounds = jnp.concatenate([jnp.zeros((NROWS, 1), jnp.int32), cut_points.astype(jnp.int32), filled[:, None].astype(jnp.int32)], axis=1)
    pieces = bounds[:, 1:] - bounds[:, :-1]
    whole_rows = jnp.arange(NROWS) % 8 == 0
    single = jnp.where(jnp.arange(SLOTS)[None, :] == 0, ROW, 0) * jnp.ones((NROWS, 1), jnp.int32)
    return jnp.where(whole_rows[:, None], single, pieces).astype(jnp.int32)


def steps_of(stream_key, shape, split, smallest, top_value):
    factor_of = 1.0
    for position, blocks in split:
        heights = jax.random.uniform(jax.random.fold_in(jax.random.fold_in(stream_key, 6), position), (blocks,), jnp.float32, smallest / len(split), top_value / len(split))
        factor_of = factor_of * jnp.repeat(jnp.exp(heights), shape[position] // blocks).reshape((-1,) + (1,) * (len(shape) - 1 - position))
    return factor_of


def scatter_about(stream_key, shape, deviation, bound, cuts=(), held_as=jnp.bfloat16):
    factor_of = steps_of(stream_key, shape, cuts, -0.22, 0.18) if cuts else 1.0
    values = jax.random.normal(stream_key, shape, jnp.float32) * deviation * factor_of
    return jnp.minimum(jnp.maximum(values, -bound), bound).astype(held_as)


def setup_inputs(seed: int = 0) -> dict:
    keys = jax.random.split(jax.random.key(seed), 24)
    tokens = scatter_about(keys[0], (TOKENS, D), 1.0, 6.0, ((0, 32),))
    lengths = draw_lengths(jax.random.fold_in(keys[23], 71), 0)
    norm1_gain = jnp.clip(1.0 + 0.1 * jax.random.normal(keys[2], (D,), jnp.float32), 0.5, 1.5)
    norm1_shift = scatter_about(keys[3], (D,), 0.3, 1.8, (), jnp.float32)
    query_weight = scatter_about(keys[4], (D, D), D ** -0.5, 0.1875, ((1, 4),))
    query_bias = scatter_about(keys[5], (D,), 0.3, 1.8, ((0, 4),), jnp.float32)
    key_weight = scatter_about(keys[6], (D, D), D ** -0.5, 0.1875, ((1, 4),))
    value_weight = scatter_about(keys[7], (D, D), D ** -0.5, 0.1875, ((1, 4),))
    value_bias = scatter_about(keys[8], (D,), 0.3, 1.8, ((0, 4),), jnp.float32)
    head_scale = jnp.clip(1.0 + 0.18 * jax.random.normal(keys[9], (HEADS,), jnp.float32), 0.1, 1.9)
    output_weight = scatter_about(keys[10], (D, D), (D // 16) ** -0.5, 0.75, ((0, 4),))
    output_bias = scatter_about(keys[11], (D,), 0.3, 1.8, (), jnp.float32)
    norm2_gain = jnp.clip(1.0 + 0.1 * jax.random.normal(keys[12], (D,), jnp.float32), 0.5, 1.5)
    norm2_shift = scatter_about(keys[13], (D,), 0.3, 1.8, (), jnp.float32)
    norm3_gain = jnp.clip(1.0 + 0.1 * jax.random.normal(keys[14], (D,), jnp.float32), 0.5, 1.5)
    norm3_shift = scatter_about(keys[15], (D,), 0.3, 1.8, (), jnp.float32)
    fc1_weight = scatter_about(keys[16], (D, FF), D ** -0.5, 0.1875, ((1, 4),))
    fc1_bias = scatter_about(keys[17], (FF,), 0.3, 1.8, ((0, 4),), jnp.float32)
    mid_gain = jnp.clip(1.0 + 0.1 * jax.random.normal(keys[18], (FF,), jnp.float32), 0.5, 1.5)
    mid_shift = scatter_about(keys[19], (FF,), 0.3, 1.8, ((0, 4),), jnp.float32)
    fc2_weight = scatter_about(keys[20], (FF, D), FF ** -0.5, 0.09375, ((0, 4),))
    fc2_bias = scatter_about(keys[21], (D,), 0.3, 1.8, (), jnp.float32)
    out_grad = scatter_about(keys[22], (TOKENS, D), 1.0, 6.0, ((0, 32),))
    return dict(tokens=tokens, lengths=lengths, norm1_gain=norm1_gain, norm1_shift=norm1_shift, query_weight=query_weight, query_bias=query_bias, key_weight=key_weight, value_weight=value_weight, value_bias=value_bias, head_scale=head_scale, output_weight=output_weight, output_bias=output_bias, norm2_gain=norm2_gain, norm2_shift=norm2_shift, norm3_gain=norm3_gain, norm3_shift=norm3_shift, fc1_weight=fc1_weight, fc1_bias=fc1_bias, mid_gain=mid_gain, mid_shift=mid_shift, fc2_weight=fc2_weight, fc2_bias=fc2_bias, out_grad=out_grad)


EPSILON = 1e-05
MASKED = -1000000000.0

@jax.custom_vjp
def low(v):
    return lax.optimization_barrier(v.astype(jnp.bfloat16)).astype(jnp.float32)

@jax.custom_vjp
def low_back(v):
    return v

def low_keep(v):
    return (low(v), None)

def low_pass(kept, grad):
    return (grad,)

def back_keep(v):
    return (v, None)

def back_low(kept, grad):
    return (low(grad),)
low.defvjp(low_keep, low_pass)
low_back.defvjp(back_keep, back_low)

def normalize(inputs, scales, shifts):
    center = inputs - lax.optimization_barrier(jnp.mean(inputs, -1, keepdims=True))
    spread = lax.optimization_barrier(jnp.mean(center * center, -1, keepdims=True))
    return center * lax.rsqrt(spread + EPSILON) * scales + shifts

def matmul(left, right):
    return jnp.dot(left, right, precision=lax.Precision.HIGHEST)

def segments_of(lengths):
    seq_ends = jnp.cumsum(lengths, axis=-1).astype(jnp.int32)
    places = jnp.arange(ROW, dtype=jnp.int32)
    return lax.optimization_barrier(jnp.sum((places[None, :, None] >= seq_ends[:, None, :]).astype(jnp.int32), -1)).astype(jnp.int32)

def row_forward(weights_all, token_rows, seg_row):
    norm1_gain, norm1_shift, query_weight, query_bias, key_weight, value_weight, value_bias, head_scale, output_weight, output_bias, norm2_gain, norm2_shift, norm3_gain, norm3_shift, fc1_weight, fc1_bias, mid_gain, mid_shift, fc2_weight, fc2_bias = weights_all
    normed = low(normalize(token_rows, norm1_gain, norm1_shift))
    queries_all = low_back(low(matmul(normed, query_weight) + query_bias)).reshape(ROW, HEADS, HEAD_DIM)
    keys_all = low_back(low(matmul(normed, key_weight))).reshape(ROW, HEADS, HEAD_DIM)
    values_all = low_back(low(matmul(normed, value_weight) + value_bias)).reshape(ROW, HEADS, HEAD_DIM)
    places = jnp.arange(ROW, dtype=jnp.int32)

    def attend_block(block_index):
        offset = block_index * QBLOCK
        q_blk = lax.dynamic_slice_in_dim(queries_all, offset, QBLOCK, 0)
        seg_q = lax.dynamic_slice_in_dim(seg_row, offset, QBLOCK, 0)
        pos_q = offset + jnp.arange(QBLOCK, dtype=jnp.int32)
        raw_scores = jnp.einsum('qhd,khd->hqk', q_blk, keys_all, precision=lax.Precision.HIGHEST) * HEAD_DIM ** (-0.5)
        raw_scores = low_back(raw_scores)
        allowed = (seg_q[:, None] == seg_row[None, :]) & (places[None, :] <= pos_q[:, None])
        scores = jnp.where(allowed[None], raw_scores, MASKED)
        row_max = lax.optimization_barrier(jnp.max(scores, -1, keepdims=True))
        exp_scores = jnp.exp(scores - row_max)
        attn_prob = low(exp_scores / lax.optimization_barrier(jnp.sum(exp_scores, -1, keepdims=True)))
        return jnp.einsum('hqk,khd->qhd', attn_prob, values_all, precision=lax.Precision.HIGHEST)
    block_outs = lax.map(jax.checkpoint(attend_block), jnp.arange(ROW // QBLOCK, dtype=jnp.int32))
    attended = block_outs.reshape(ROW, HEADS, HEAD_DIM)
    mixed_heads = low(low_back(attended) * head_scale[None, :, None]).reshape(ROW, HEADS * HEAD_DIM)
    branch = low_back(matmul(mixed_heads, output_weight) + output_bias)
    residual = token_rows + normalize(branch, norm2_gain, norm2_shift)
    ffn_in = low(normalize(residual, norm3_gain, norm3_shift))
    fc1_out = low_back(matmul(ffn_in, fc1_weight) + fc1_bias)
    active = jax.nn.gelu(fc1_out, approximate=True)
    hidden = low(normalize(active, mid_gain, mid_shift))
    ffn_out = low_back(matmul(hidden, fc2_weight) + fc2_bias)
    return residual + ffn_out

def reference(tokens, lengths, norm1_gain, norm1_shift, query_weight, query_bias, key_weight, value_weight, value_bias, head_scale, output_weight, output_bias, norm2_gain, norm2_shift, norm3_gain, norm3_shift, fc1_weight, fc1_bias, mid_gain, mid_shift, fc2_weight, fc2_bias, out_grad):
    weights_all = tuple((weight_arg.astype(jnp.float32) for weight_arg in (norm1_gain, norm1_shift, query_weight, query_bias, key_weight, value_weight, value_bias, head_scale, output_weight, output_bias, norm2_gain, norm2_shift, norm3_gain, norm3_shift, fc1_weight, fc1_bias, mid_gain, mid_shift, fc2_weight, fc2_bias)))
    segments = segments_of(lengths)
    token_rows = tokens.astype(jnp.float32).reshape(NROWS, ROW, D)
    valid_rows = (segments < SLOTS).astype(jnp.float32)
    cotangents = out_grad.astype(jnp.float32).reshape(NROWS, ROW, D) * valid_rows[:, :, None]

    def row_step(totals, row_item):
        token_row, seg_row, cotangent = row_item
        output_row, pull_back = jax.vjp(lambda weight_set, token_set: row_forward(weight_set, token_set, seg_row), weights_all, token_row)
        weight_grads, token_grad = pull_back(cotangent)
        totals = jax.tree.map(jnp.add, totals, weight_grads)
        return (totals, (output_row, token_grad))
    zero_grads = jax.tree.map(jnp.zeros_like, weights_all)
    totals, (outputs, token_grads) = lax.scan(row_step, zero_grads, (token_rows, segments, cotangents))
    return (outputs.reshape(TOKENS, D).astype(jnp.bfloat16), token_grads.reshape(TOKENS, D), totals[0], totals[1], totals[2], totals[3], totals[4], totals[5], totals[6], totals[7], totals[8], totals[9], totals[10], totals[11], totals[12], totals[13], totals[14], totals[15], totals[16], totals[17], totals[18], totals[19])
```

```python
import functools
import math

import jax
import jax.numpy as jnp
from jax import lax
from jax.experimental import pallas as pl
from jax.experimental.pallas import tpu as pltpu
from jax.sharding import PartitionSpec as P

HEAD_DIM = 64
FF = 4096
ROW = 2048
EPSILON = 1e-05
MASKED = -1000000000.0
LOG2E = math.log2(math.e)
VMEM_LIMIT = 56 * 2**20
SMEM_SPEC = pl.BlockSpec(memory_space=pltpu.SMEM)

def dot(a,b,ca=1,cb=0,prec=None):
    return lax.dot_general(a,b,(((ca,),(cb,)),((),())),preferred_element_type=jnp.float32,precision=prec)

def spread_heads(block, heads):
    lane=lax.broadcasted_iota(jnp.int32,(1,block.shape[1]),1)//HEAD_DIM
    zero=jnp.zeros_like(block)
    return jnp.concatenate([jnp.where(lane==h,block,zero) for h in range(heads)],axis=0)

def seq_ends(len_ref):
    ends=[]; total=jnp.int32(0)
    for j in range(len_ref.shape[-1]):
        total=total+len_ref[0,j]; ends.append(total)
    return ends

def start_of(ends,pos):
    first=jnp.zeros_like(pos)
    for e in ends: first=jnp.maximum(first,jnp.where(e<=pos,e,0))
    return first

def end_of(ends,pos):
    last=jnp.full_like(pos,ROW)
    for e in reversed(ends): last=jnp.where(e>pos,jnp.minimum(last,e),last)
    return last

def slot_row(pos,me,tok):
    return pl.multiple_of(((pos//tok)^me)*tok+pos%tok,128)

def query_positions(q0,qb,heads):
    lane=lax.broadcasted_iota(jnp.int32,(1,qb),1)+q0
    return jnp.concatenate([lane]*heads,axis=1)

def tile_mask(k0,kb,pos,first):
    key=lax.broadcasted_iota(jnp.int32,(kb,pos.shape[1]),0)+k0
    return (key>=first)&(key<=pos)

def forward_kernel(heads,tok,qb,kb,me_ref,len_ref,qkv_ref,hs_ref,att_ref,mix_ref,lse_ref,vt_ref):
    width=heads*HEAD_DIM
    me=me_ref[0]; ends=seq_ends(len_ref)
    scale=LOG2E*HEAD_DIM**-0.5
    @pl.loop(0,ROW//256)
    def _(b):
        rows=pl.ds(pl.multiple_of(b*256,256),256)
        vt_ref[b]=qkv_ref[rows,2*width:].astype(jnp.float32).T.astype(jnp.bfloat16)
    sub=kb//256
    def values_t(row):
        b=row//256
        if sub==1: return vt_ref[b]
        return jnp.concatenate([vt_ref[b+i] for i in range(sub)],axis=1)
    @pl.loop(0,ROW//qb)
    def _(qi):
        q0=qi*qb
        qrow=slot_row(q0,me,tok)
        q4=spread_heads(qkv_ref[pl.ds(qrow,qb),:width],heads)
        pos=query_positions(q0,qb,heads)
        first=start_of(ends,pos)
        def tile(k0,state,masked):
            krow=slot_row(k0,me,tok)
            s=dot(qkv_ref[pl.ds(krow,kb),width:2*width],q4,1,1)*scale
            if masked: s=jnp.where(tile_mask(k0,kb,pos,first),s,MASKED)
            top=jnp.max(s,0,keepdims=True)
            vt=values_t(krow)
            if state is not None:
                m,l,acc=state
                top=jnp.maximum(top,m)
            p=jnp.exp2(s-top)
            add=jnp.sum(p,0,keepdims=True)
            pb=p.astype(jnp.bfloat16)
            out=jnp.concatenate([dot(vt[h*HEAD_DIM:(h+1)*HEAD_DIM],pb[:,h*qb:(h+1)*qb]) for h in range(heads)],axis=1)
            if state is not None:
                fade=jnp.exp2(m-top)
                add=add+l*fade
                out=out+acc*fade
            return top,add,out
        state=None
        for d in range(qb//kb):
            state=tile(q0+d*kb,state,True)
        k_from=start_of(ends,q0)//kb
        whole=(start_of(ends,q0+qb-1)+kb-1)//kb
        diag=q0//kb
        whole=jnp.minimum(whole,diag)
        state=lax.fori_loop(k_from,whole,lambda ki,st: tile(ki*kb,st,True),state)
        m,l,acc=lax.fori_loop(whole,diag,lambda ki,st: tile(ki*kb,st,False),state)
        o=acc/l
        o=jnp.concatenate([o[:,h*qb:(h+1)*qb] for h in range(heads)],axis=0).T
        rows=pl.ds(qrow,qb)
        att_ref[rows,:]=o
        mix_ref[rows,:]=(o*hs_ref[...]).astype(jnp.bfloat16)
        lse_ref[qi]=m+jnp.log2(l)

def attend_forward(qkv,lengths,me,head_scale_lanes,tok,qb=256,kb=256):
    width=qkv.shape[1]//3; heads=width//HEAD_DIM
    smem=pl.BlockSpec(memory_space=pltpu.SMEM); vmem=pl.BlockSpec(memory_space=pltpu.VMEM)
    return pl.pallas_call(
        functools.partial(forward_kernel,heads,tok,qb,kb),
        out_shape=(jax.ShapeDtypeStruct((ROW,width),jnp.float32),jax.ShapeDtypeStruct((ROW,width),jnp.bfloat16),
                   jax.ShapeDtypeStruct((ROW//qb,1,heads*qb),jnp.float32)),
        in_specs=[smem,smem,vmem,vmem],out_specs=(vmem,vmem,vmem),
        scratch_shapes=[pltpu.VMEM((ROW//256,width,256),jnp.bfloat16)],
        compiler_params=pltpu.CompilerParams(vmem_limit_bytes=VMEM_LIMIT),
        cost_estimate=pl.CostEstimate(flops=2*2*heads*ROW*ROW*HEAD_DIM*4,bytes_accessed=8*2**20,transcendentals=heads*ROW*ROW//2),
        name="attend_forward",
    )(me,lengths,qkv,head_scale_lanes)

def backward_kernel(heads,tok,qb,kb,me_ref,len_ref,qkv_ref,do_ref,att_ref,lse_ref,dqkv_ref,sum_ref,q4_ref,do4_ref,dqt_ref,delta_ref):
    width=heads*HEAD_DIM
    me=me_ref[0]; ends=seq_ends(len_ref)
    scale=LOG2E*HEAD_DIM**-0.5
    nq=ROW//qb
    sum_ref[...]=jnp.zeros_like(sum_ref)
    pick=(lax.broadcasted_iota(jnp.int32,(8,width),1)//HEAD_DIM==lax.broadcasted_iota(jnp.int32,(8,width),0)).astype(jnp.float32)
    @pl.loop(0,nq)
    def _(qi):
        rows=pl.ds(slot_row(qi*qb,me,tok),qb)
        q4_ref[qi]=spread_heads(qkv_ref[rows,:width],heads)
        do=do_ref[rows,:]
        do4_ref[qi]=spread_heads(do,heads)
        both=do.astype(jnp.float32)*att_ref[rows,:]
        d=dot(pick,both,1,1,lax.Precision.HIGHEST)
        sum_ref[:,3*width:]+=jnp.sum(both,0,keepdims=True)
        delta_ref[qi]=jnp.concatenate([d[h:h+1] for h in range(heads)],axis=1)
        dqt_ref[qi]=jnp.zeros(dqt_ref.shape[1:],jnp.float32)
    @pl.loop(0,ROW//kb)
    def _(ki):
        k0=ki*kb
        krow=slot_row(k0,me,tok)
        rows=pl.ds(krow,kb)
        k=qkv_ref[rows,width:2*width]; v=qkv_ref[rows,2*width:]
        kt=k.astype(jnp.float32).T.astype(jnp.bfloat16)
        def tile(qi,state,masked):
            q4=q4_ref[qi]; do4=do4_ref[qi]
            s=dot(k,q4,1,1)*scale
            if masked:
                pos=query_positions(qi*qb,qb,heads)
                s=jnp.where(tile_mask(k0,kb,pos,start_of(ends,pos)),s,MASKED)
            p=jnp.exp2(s-lse_ref[qi])
            dp=dot(v,do4,1,1)
            ds=(p*(dp-delta_ref[qi])).astype(jnp.bfloat16)
            dv=dot(p.astype(jnp.bfloat16),do4)
            dk=dot(ds,q4)
            dqt_ref[qi]+=jnp.concatenate([dot(kt[h*HEAD_DIM:(h+1)*HEAD_DIM],ds[:,h*qb:(h+1)*qb]) for h in range(heads)],axis=1)
            if state is None: return dk,dv
            return state[0]+dk,state[1]+dv
        state=None
        qd=k0//qb
        for d in range(max(1,kb//qb)):
            state=tile(qd+d,state,True)
        q_from=qd+max(1,kb//qb)
        q_to=(end_of(ends,k0+kb-1)+qb-1)//qb
        whole=jnp.clip(end_of(ends,k0)//qb,q_from,q_to)
        state=lax.fori_loop(q_from,whole,lambda qi,st: tile(qi,st,False),state)
        dk,dv=lax.fori_loop(whole,q_to,lambda qi,st: tile(qi,st,True),state)
        dqkv_ref[rows,width:2*width]=(dk*HEAD_DIM**-0.5).astype(jnp.bfloat16)
        dqkv_ref[rows,2*width:]=dv.astype(jnp.bfloat16)
    @pl.loop(0,nq)
    def _(qi):
        o=dqt_ref[qi]
        o=jnp.concatenate([o[:,h*qb:(h+1)*qb] for h in range(heads)],axis=0).T
        rows=pl.ds(slot_row(qi*qb,me,tok),qb)
        dqkv_ref[rows,:width]=(o*HEAD_DIM**-0.5).astype(jnp.bfloat16)
        sum_ref[:,:3*width]+=jnp.sum(dqkv_ref[rows,:].astype(jnp.float32),0,keepdims=True)

def attend_backward(qkv,lengths,me,att_grad,att,lse,tok,qb=256,kb=256):
    width=qkv.shape[1]//3; heads=width//HEAD_DIM
    smem=pl.BlockSpec(memory_space=pltpu.SMEM); vmem=pl.BlockSpec(memory_space=pltpu.VMEM)
    nq=ROW//qb
    return pl.pallas_call(
        functools.partial(backward_kernel,heads,tok,qb,kb),
        out_shape=(jax.ShapeDtypeStruct((ROW,3*width),jnp.bfloat16),jax.ShapeDtypeStruct((1,4*width),jnp.float32)),
        in_specs=[smem,smem,vmem,vmem,vmem,vmem],out_specs=(vmem,vmem),
        scratch_shapes=[pltpu.VMEM((nq,heads*qb,width),jnp.bfloat16),pltpu.VMEM((nq,heads*qb,width),jnp.bfloat16),
                        pltpu.VMEM((nq,HEAD_DIM,heads*qb),jnp.float32),pltpu.VMEM((nq,1,heads*qb),jnp.float32)],
        compiler_params=pltpu.CompilerParams(vmem_limit_bytes=VMEM_LIMIT),
        cost_estimate=pl.CostEstimate(flops=2*5*heads*ROW*ROW*HEAD_DIM*4,bytes_accessed=12*2**20,transcendentals=heads*ROW*ROW//2),
        name="attend_backward",
    )(me,lengths,qkv,att_grad,att,lse)


def gelu_parts(u):
    k = math.sqrt(2 / math.pi)
    square = u * u
    t = jnp.tanh(u * (k + (k * 0.044715) * square))
    half = 0.5 + 0.5 * t
    return half, t, square


def ffn_first_kernel(x_ref, c_ref, w1_ref, b1_ref, gain_ref, w2_ref, u_ref, hg_ref, stat_ref):
    units = u_ref.shape[1]
    u = dot(x_ref[...], w1_ref[...]) + b1_ref[...]
    u_ref[...] = u
    half, _, _ = gelu_parts(u)
    a = u * half
    total = jnp.sum(a, 1, keepdims=True)
    d = a - total * (1.0 / units)
    hg = dot(c_ref[...], w2_ref[...], 1, 1)
    hg_ref[...] = hg
    sg = hg * gain_ref[...]
    cols = [
        total,
        jnp.sum(d * d, 1, keepdims=True),
        jnp.sum(sg, 1, keepdims=True),
        jnp.sum(sg * d, 1, keepdims=True),
    ]
    lane = lax.broadcasted_iota(jnp.int32, (u.shape[0], 128), 1)
    wide = jnp.zeros(lane.shape, jnp.float32)
    for j, col in enumerate(cols):
        wide = jnp.where(lane == j, col, wide)
    stat_ref[...] = wide.T[:8]


def ffn_first(x, cot, w1, b1, gain, w2, tile=256):
    rows, d = x.shape
    units = w1.shape[1]
    tile = min(tile, rows)
    return pl.pallas_call(
        ffn_first_kernel,
        grid=(rows // tile,),
        in_specs=[
            pl.BlockSpec((tile, d), lambda t: (t, 0)),
            pl.BlockSpec((tile, d), lambda t: (t, 0)),
            pl.BlockSpec((d, units), lambda t: (0, 0)),
            pl.BlockSpec((1, units), lambda t: (0, 0)),
            pl.BlockSpec((1, units), lambda t: (0, 0)),
            pl.BlockSpec((units, d), lambda t: (0, 0)),
        ],
        out_specs=(
            pl.BlockSpec((tile, units), lambda t: (t, 0)),
            pl.BlockSpec((tile, units), lambda t: (t, 0)),
            pl.BlockSpec((8, tile), lambda t: (0, t)),
        ),
        out_shape=(
            jax.ShapeDtypeStruct((rows, units), jnp.float32),
            jax.ShapeDtypeStruct((rows, units), jnp.float32),
            jax.ShapeDtypeStruct((8, rows), jnp.float32),
        ),
        compiler_params=pltpu.CompilerParams(vmem_limit_bytes=VMEM_LIMIT),
        cost_estimate=pl.CostEstimate(
            flops=4 * rows * d * units, bytes_accessed=rows * units * 8, transcendentals=rows * units
        ),
        name="ffn_first",
    )(x, cot, w1, b1, gain, w2)


def ffn_second_kernel(ndev, *refs):
    u_ref, hg_ref, gain_ref, shift_ref, w1_ref = refs[:5]
    stats = [r[...] for r in refs[5 : 5 + ndev]]
    hid_ref, fg_ref, back_ref, sum_ref = refs[-4:]
    units = u_ref.shape[1]
    mean = sum(s[0:1] for s in stats) * (1.0 / FF)
    spread = jnp.zeros_like(mean)
    total = jnp.zeros_like(mean)
    cross = jnp.zeros_like(mean)
    for s in stats:
        gap = s[0:1] * (1.0 / units) - mean
        spread += s[1:2] + units * (gap * gap)
        total += s[2:3]
        cross += s[3:4] + gap * s[2:3]
    inv = lax.rsqrt(spread * (1.0 / FF) + EPSILON)
    packed = jnp.concatenate(
        [mean, inv, total * (1.0 / FF), cross * inv * (1.0 / FF)] + [jnp.zeros_like(mean)] * 4, axis=0
    ).T
    mean, inv, total, cross = (packed[:, j : j + 1] for j in range(4))
    u = u_ref[...]
    hg = hg_ref[...]
    half, t, square = gelu_parts(u)
    unit = (u * half - mean) * inv
    gain = gain_ref[...]
    hid_ref[...] = (unit * gain + shift_ref[...]).astype(jnp.bfloat16)
    k = math.sqrt(2 / math.pi)
    slope = half + (0.5 * u) * ((1.0 - t * t) * (k + (3 * k * 0.044715) * square))
    fg = (inv * (hg * gain - total - unit * cross) * slope).astype(jnp.bfloat16)
    fg_ref[...] = fg
    back_ref[...] = dot(fg, w1_ref[...], 1, 1).astype(jnp.bfloat16)

    @pl.when(pl.program_id(0) == 0)
    def _():
        sum_ref[...] = jnp.zeros_like(sum_ref)

    sums = jnp.concatenate(
        [
            jnp.sum(hg * unit, 0, keepdims=True),
            jnp.sum(hg, 0, keepdims=True),
            jnp.sum(fg.astype(jnp.float32), 0, keepdims=True),
            jnp.zeros((5, units), jnp.float32),
        ],
        axis=0,
    )
    sum_ref[...] += sums


def ffn_second(u, hg, gain, shift, w1, stats, tok, base, earlier=None, tile=256):
    rows, units = u.shape
    d = w1.shape[0]
    tile = min(tile, tok)
    per = tok // tile
    ndev = len(stats)

    def stat_place(s):
        return lambda t: (0, (((t // per) + base) ^ s) * per + t % per)

    skip = base * per
    in_specs = [
        pl.BlockSpec((tile, units), lambda t: (t, 0)),
        pl.BlockSpec((tile, units), lambda t: (t, 0)),
        pl.BlockSpec((1, units), lambda t: (0, 0)),
        pl.BlockSpec((1, units), lambda t: (0, 0)),
        pl.BlockSpec((d, units), lambda t: (0, 0)),
    ] + [pl.BlockSpec((8, tile), stat_place(s)) for s in range(ndev)]
    args = [u, hg, gain, shift, w1, *stats]
    aliases = {}
    if earlier is not None:
        in_specs += [pl.BlockSpec(memory_space=pl.ANY)] * 2
        aliases = {len(args): 0, len(args) + 1: 1}
        args += list(earlier)
    return pl.pallas_call(
        functools.partial(ffn_second_kernel, ndev),
        grid=(rows // tile,),
        in_specs=in_specs,
        out_specs=(
            pl.BlockSpec((tile, units), lambda t: (t + skip, 0)),
            pl.BlockSpec((tile, units), lambda t: (t + skip, 0)),
            pl.BlockSpec((tile, d), lambda t: (t, 0)),
            pl.BlockSpec((8, units), lambda t: (0, 0)),
        ),
        out_shape=(
            jax.ShapeDtypeStruct((ROW, units), jnp.bfloat16),
            jax.ShapeDtypeStruct((ROW, units), jnp.bfloat16),
            jax.ShapeDtypeStruct((rows, d), jnp.bfloat16),
            jax.ShapeDtypeStruct((8, units), jnp.float32),
        ),
        input_output_aliases=aliases,
        compiler_params=pltpu.CompilerParams(vmem_limit_bytes=VMEM_LIMIT),
        cost_estimate=pl.CostEstimate(
            flops=2 * rows * d * units, bytes_accessed=rows * units * 12, transcendentals=rows * units
        ),
        name="ffn_second",
    )(*args)


def normalize(inputs, scales, shifts):
    center = inputs - jnp.mean(inputs, -1, keepdims=True)
    spread = jnp.mean(center * center, -1, keepdims=True)
    return center * lax.rsqrt(spread + EPSILON) * scales + shifts


def contract_rows(left, right):
    return dot(left, right, 0, 0)


def swap(value, axis, size, bit):
    return lax.ppermute(value, axis, [(i, i ^ bit) for i in range(size)])


def bits_of(size):
    return [1 << b for b in range(size.bit_length() - 1)]


def gather_slots(value, axis, size):
    slots = {0: value}
    for bit in reversed(bits_of(size)):
        slots.update({s | bit: swap(v, axis, size, bit) for s, v in slots.items()})
    return [slots[s] for s in range(size)]


def direct_slots(value, axis, size):
    return [value] + [swap(value, axis, size, s) for s in range(1, size)]


def add_low(left, right):
    return left.astype(jnp.float32) + right.astype(jnp.float32)


def scatter_slots(parts, axis, size):
    held = dict(enumerate(parts))
    for bit in bits_of(size):
        came = {
            s ^ bit: swap(held[s].astype(jnp.bfloat16), axis, size, bit)
            for s in sorted(held, reverse=True)
            if s & bit
        }
        held = {s: add_low(held[s], v) for s, v in came.items()}
    return held[0]


def all_sum(value, axes):
    for axis, size in axes:
        for bit in bits_of(size):
            value = value + swap(value, axis, size, bit)
    return value


def group_sum(value, axis, size, order):
    index = lax.axis_index(axis)
    cur = value.astype(jnp.bfloat16)
    for bit in order:
        upper = (index & bit) != 0
        half = cur.shape[0] // 2
        low, high = cur[:half], cur[half:]
        came = swap(jnp.where(upper, low, high), axis, size, bit)
        cur = add_low(jnp.where(upper, high, low), came).astype(jnp.bfloat16)
    for bit in reversed(order):
        upper = (index & bit) != 0
        came = swap(cur, axis, size, bit)
        cur = jnp.concatenate([jnp.where(upper, came, cur), jnp.where(upper, cur, came)], axis=0)
    return cur.astype(jnp.float32)


def on_device(
    dp,
    mp,
    tokens,
    lengths,
    norm1_gain,
    norm1_shift,
    query_weight,
    query_bias,
    key_weight,
    value_weight,
    value_bias,
    head_scale,
    output_weight,
    output_bias,
    norm2_gain,
    norm2_shift,
    norm3_gain,
    norm3_shift,
    fc1_weight,
    fc1_bias,
    mid_gain,
    mid_shift,
    fc2_weight,
    fc2_bias,
    out_grad,
):
    tok = tokens.shape[0]
    width = query_weight.shape[1]
    heads = width // HEAD_DIM
    me = lax.axis_index("mp").astype(jnp.int32)
    me_arr = me[None]
    block = min(512, tok)
    bf16 = jnp.bfloat16
    token_f = tokens.astype(jnp.float32)
    place = me * tok + lax.broadcasted_iota(jnp.int32, (tok, 1), 0)
    cotangent = jnp.where(place < jnp.sum(lengths), out_grad.astype(jnp.float32), 0.0)

    normed_own = normalize(token_f, norm1_gain, norm1_shift).astype(bf16)
    normed = jnp.concatenate(gather_slots(normed_own, "mp", mp))
    cot_low = cotangent.astype(bf16)
    cot_slots = gather_slots(cot_low, "mp", mp)
    out_rows = jnp.concatenate(gather_slots(output_weight, "mp", mp))
    scale_lanes = jnp.repeat(head_scale, HEAD_DIM)[None]
    scale_slots = jnp.concatenate(direct_slots(scale_lanes, "mp", mp), axis=1)

    w_qkv = jnp.concatenate([query_weight, key_weight, value_weight], axis=1)
    bias_qkv = jnp.concatenate([query_bias, jnp.zeros_like(query_bias), value_bias])
    qkv = (dot(normed, w_qkv) + bias_qkv).astype(bf16)
    attended, mixed, lse = attend_forward(qkv, lengths, me_arr, scale_lanes, tok, block, block)
    mixed = mixed.reshape(mp, tok, width)
    mixed_own = jnp.concatenate(
        [mixed[0]] + [swap(mixed[s], "mp", mp, s) for s in range(1, mp)], axis=1
    )
    branch = dot(mixed_own, out_rows) + output_bias
    residual = token_f + normalize(branch, norm2_gain, norm2_shift)
    ffn_own = normalize(residual, norm3_gain, norm3_shift).astype(bf16)
    ffn_slots = gather_slots(ffn_own, "mp", mp)

    half = mp // 2
    b1, gain, shift = fc1_bias[None], mid_gain[None], mid_shift[None]
    parts = []
    for part in range(2):
        x = jnp.concatenate(ffn_slots[part * half : (part + 1) * half])
        c = jnp.concatenate(cot_slots[part * half : (part + 1) * half])
        parts.append((x, c, *ffn_first(x, c, fc1_weight, b1, gain, fc2_weight)))
    (x_near, c_near, u_near, hg_near, st_near), (x_far, c_far, u_far, hg_far, st_far) = parts
    stats = direct_slots(jnp.concatenate([st_near, st_far], axis=1), "mp", mp)
    hid, fg, back_far, sums_far = ffn_second(
        u_far, hg_far, gain, shift, fc1_weight, stats, tok, half
    )
    hid, fg, back_near, sums_near = ffn_second(
        u_near, hg_near, gain, shift, fc1_weight, stats, tok, 0, (hid, fg)
    )
    back = [back_near[s * tok : (s + 1) * tok] for s in range(half)]
    back += [back_far[s * tok : (s + 1) * tok] for s in range(half)]
    ffn_in_grad = scatter_slots(back, "mp", mp)
    ffn_in = jnp.concatenate([x_near, x_far])
    cot_all = jnp.concatenate([c_near, c_far])

    order = bits_of(dp)
    grad_fc2_weight = group_sum(contract_rows(hid, cot_all), "dp", dp, order)
    grad_fc1_weight = group_sum(contract_rows(ffn_in, fg), "dp", dp, order[1:] + order[:1])
    ffn_out = dot(hid, fc2_weight).astype(bf16)

    _, norm3_pull = jax.vjp(normalize, residual, norm3_gain, norm3_shift)
    residual_from, g_norm3_gain, g_norm3_shift = norm3_pull(ffn_in_grad)
    residual_grad = cotangent + residual_from
    _, norm2_pull = jax.vjp(normalize, branch, norm2_gain, norm2_shift)
    branch_from, g_norm2_gain, g_norm2_shift = norm2_pull(residual_grad)
    branch_low = branch_from.astype(bf16)
    mixed_grad = dot(branch_low, out_rows, 1, 1)
    att_grad = (mixed_grad * scale_slots).astype(bf16)
    att_parts = [att_grad[:, s * width : (s + 1) * width] for s in range(mp)]
    att_grad = jnp.concatenate(
        [att_parts[0]] + [swap(att_parts[s], "mp", mp, s) for s in range(1, mp)]
    )
    dqkv, sums_att = attend_backward(qkv, lengths, me_arr, att_grad, attended, lse, tok, block, block)

    g_out = contract_rows(mixed_own, branch_low)
    g_out = scatter_slots([g_out[s * width : (s + 1) * width] for s in range(mp)], "mp", mp)
    grad_output_weight = group_sum(g_out, "dp", dp, order)

    ffn_out = scatter_slots([ffn_out[s * tok : (s + 1) * tok] for s in range(mp)], "mp", mp)
    output = (residual + ffn_out + fc2_bias).astype(bf16)

    early = jnp.stack(
        [
            g_norm2_gain,
            g_norm2_shift,
            g_norm3_gain,
            g_norm3_shift,
            jnp.sum(branch_low.astype(jnp.float32), 0),
            jnp.sum(cot_low.astype(jnp.float32), 0),
        ]
    )
    early = all_sum(early, [("mp", mp), ("dp", dp)])
    mids = all_sum(sums_near + sums_far, [("dp", dp)])

    normed_back = dot(dqkv, w_qkv, 1, 1).astype(bf16)
    normed_grad = scatter_slots([normed_back[s * tok : (s + 1) * tok] for s in range(mp)], "mp", mp)
    _, norm1_pull = jax.vjp(lambda v: normalize(v, norm1_gain, norm1_shift), token_f)
    token_grad = residual_grad + norm1_pull(normed_grad)[0]

    g_qkv = contract_rows(normed, dqkv)
    wide = w_qkv.astype(jnp.float32)
    sum_qkv = sums_att[:, : 3 * width]
    g_shift1 = jnp.sum(wide * sum_qkv, 1)
    g_gain1 = (jnp.sum(wide * g_qkv, 1) - norm1_shift * g_shift1) / norm1_gain
    grad_qkv = group_sum(g_qkv, "dp", dp, order)
    late = all_sum(jnp.stack([g_gain1, g_shift1]), [("mp", mp)])
    tail = all_sum(
        jnp.concatenate([late.reshape(-1), sums_att.reshape(-1)]).reshape(-1, 128), [("dp", dp)]
    ).reshape(-1)
    d = tokens.shape[1]
    sums_att = tail[tail.shape[0] - 4 * width :]
    return (
        output,
        token_grad,
        tail[:d],
        tail[d : 2 * d],
        grad_qkv[:, :width],
        sums_att[:width],
        grad_qkv[:, width : 2 * width],
        grad_qkv[:, 2 * width :],
        sums_att[2 * width : 3 * width],
        jnp.sum(sums_att[3 * width :].reshape(heads, HEAD_DIM), 1) / head_scale,
        grad_output_weight,
        early[4],
        early[0],
        early[1],
        early[2],
        early[3],
        grad_fc1_weight,
        mids[2],
        mids[0],
        mids[1],
        grad_fc2_weight,
        early[5],
    )


def solution(mesh):
    own = P(("dp", "mp"), None)
    cols, rows, vec, same = P(None, "mp"), P("mp", None), P("mp"), P()
    in_specs = (
        own, P("dp", None), same, same, cols, vec, cols, cols, vec, vec, rows, same, same, same, same, same,
        cols, vec, vec, vec, rows, same, own,
    )
    out_specs = (
        own, own, same, same, cols, vec, cols, cols, vec, vec, rows, same, same, same, same, same,
        cols, vec, vec, vec, rows, same,
    )
    return jax.shard_map(
        functools.partial(on_device, mesh.shape["dp"], mesh.shape["mp"]),
        mesh=mesh, in_specs=in_specs, out_specs=out_specs, check_vma=False,
    )
```

```python
import functools
import math

import jax
import jax.numpy as jnp
from jax import lax
from jax.experimental import pallas as pl
from jax.experimental.pallas import tpu as pltpu
from jax.sharding import PartitionSpec as P

HEAD_DIM = 64
FF = 4096
ROW = 2048
PAIR = 2 * HEAD_DIM
EPSILON = 1e-05
MASKED = -1000000000.0
LOG2E = math.log2(math.e)
SCORE_SCALE = LOG2E * HEAD_DIM**-0.5
SMEM_SPEC = pl.BlockSpec(memory_space=pltpu.SMEM)
VMEM_SPEC = pl.BlockSpec(memory_space=pltpu.VMEM)
BF16 = jnp.bfloat16
F32 = jnp.float32
PARAMS = pltpu.CompilerParams(vmem_limit_bytes=56 * 2**20)


def shape(dims, dtype):
    return jax.ShapeDtypeStruct(dims, dtype)


def cost(us):
    return pl.CostEstimate(flops=0, bytes_accessed=int(us * 1000), transcendentals=0)


def dot(a, b, ca=1, cb=0, precision=None):
    return lax.dot_general(
        a, b, (((ca,), (cb,)), ((), ())), preferred_element_type=F32, precision=precision
    )


def spread_heads(block, heads):
    lane = lax.broadcasted_iota(jnp.int32, (1, block.shape[1]), 1) // HEAD_DIM
    zero = jnp.zeros_like(block)
    return jnp.concatenate([jnp.where(lane == h, block, zero) for h in range(heads)], axis=0)


def seq_ends(len_ref):
    ends = []
    total = jnp.int32(0)
    for j in range(len_ref.shape[-1]):
        total = total + len_ref[0, j]
        ends.append(total)
    return ends


def start_of(ends, pos):
    first = jnp.zeros_like(pos)
    for e in ends:
        first = jnp.maximum(first, jnp.where(e <= pos, e, 0))
    return first


def query_positions(q0, tok, heads):
    lane = lax.broadcasted_iota(jnp.int32, (1, tok), 1) + q0
    return jnp.concatenate([lane] * heads, axis=1)


def hide(scores, k0, pos, first):
    key = lax.broadcasted_iota(jnp.int32, scores.shape, 0) + k0
    return jnp.where((key >= first) & (key <= pos), scores, MASKED)


def slot_rows(place, me, tok):
    return pl.ds(pl.multiple_of((place ^ me) * tok, tok), tok)


def fold_heads(side, heads, tok):
    return jnp.concatenate([side[:, h * tok : (h + 1) * tok] for h in range(heads)], axis=0).T


def key_range(ends, place, tok):
    begin = start_of(ends, place * tok) // tok
    whole = (start_of(ends, place * tok + tok - 1) + tok - 1) // tok
    return begin, jnp.minimum(whole, place)


def forward_kernel(tok, me_ref, len_ref, q_ref, k_ref, v_ref, scale_ref, *refs):
    nslot = ROW // tok
    width = q_ref.shape[1]
    heads = width // HEAD_DIM
    att_ref, lse_ref = refs[:2]
    mix_refs = refs[2 : 2 + nslot]
    vt_ref, mix_ref = refs[2 + nslot :]
    me = me_ref[0]
    ends = seq_ends(len_ref)

    @pl.loop(0, nslot)
    def _(b):
        rows = pl.ds(pl.multiple_of(b * tok, tok), tok)
        vt_ref[b] = v_ref[rows, :].astype(F32).T.astype(BF16)

    @pl.loop(0, nslot)
    def _(place):
        slot = place ^ me
        rows = slot_rows(place, me, tok)
        q4 = spread_heads(q_ref[rows, :], heads)
        pos = query_positions(place * tok, tok, heads)
        first = start_of(ends, pos)

        def tile(ki, state, masked):
            s = dot(k_ref[slot_rows(ki, me, tok), :], q4, 1, 1) * SCORE_SCALE
            if masked:
                s = hide(s, ki * tok, pos, first)
            top = jnp.max(s, 0, keepdims=True)
            vt = vt_ref[ki ^ me]
            if state is not None:
                m, l, acc = state
                top = jnp.maximum(top, m)
            p = jnp.exp2(s - top)
            add = jnp.sum(p, 0, keepdims=True)
            pb = p.astype(BF16)
            out = jnp.concatenate(
                [
                    dot(vt[h * HEAD_DIM : (h + 1) * HEAD_DIM], pb[:, h * tok : (h + 1) * tok])
                    for h in range(heads)
                ],
                axis=1,
            )
            if state is not None:
                fade = jnp.exp2(m - top)
                add = add + l * fade
                out = out + acc * fade
            return top, add, out

        begin, whole = key_range(ends, place, tok)
        state = tile(place, None, True)
        state = lax.fori_loop(begin, whole, lambda ki, st: tile(ki, st, True), state)
        m, l, acc = lax.fori_loop(
            jnp.maximum(whole, begin), place, lambda ki, st: tile(ki, st, False), state
        )
        o = fold_heads(acc / l, heads, tok)
        att_ref[rows, :] = o
        mix_ref[slot] = (o * scale_ref[...]).astype(BF16)
        lse_ref[slot] = m + jnp.log2(l)

    for s in range(nslot):
        mix_refs[s][...] = mix_ref[s]


def pair_blocks(qkv, pair):
    pairs = qkv.shape[1] // (3 * PAIR)
    return [pl.BlockSpec((ROW, PAIR), lambda t, c=j * pairs + pair: (0, c)) for j in range(3)]


def whole_spec(dims):
    return pl.BlockSpec(dims, lambda t: (0,) * len(dims))


def attend_forward(me, lengths, qkv, scale_lanes, tok, pair):
    nslot = ROW // tok
    lanes = PAIR // HEAD_DIM * tok
    made = [((ROW, PAIR), F32), ((nslot, 1, lanes), F32)] + [((tok, PAIR), BF16)] * nslot
    out = pl.pallas_call(
        functools.partial(forward_kernel, tok),
        grid=(1,),
        out_shape=[shape(*m) for m in made],
        in_specs=[SMEM_SPEC, SMEM_SPEC]
        + pair_blocks(qkv, pair)
        + [pl.BlockSpec((1, PAIR), lambda t: (0, pair))],
        out_specs=[whole_spec(m[0]) for m in made],
        scratch_shapes=[
            pltpu.VMEM((nslot, PAIR, tok), BF16),
            pltpu.VMEM((nslot, tok, PAIR), BF16),
        ],
        compiler_params=PARAMS,
        cost_estimate=cost(8),
        name="attend_forward",
    )(me, lengths, qkv, qkv, qkv, scale_lanes)
    return out[0], out[1], list(out[2:])


def end_of(ends, pos):
    last = jnp.full_like(pos, ROW)
    for e in ends:
        last = jnp.where(e > pos, jnp.minimum(last, e), last)
    return last


def backward_kernel(tok, turn, me_ref, len_ref, q_ref, k_ref, v_ref, att_ref, lse_ref, *refs):
    nslot = ROW // tok
    width = q_ref.shape[1]
    heads = width // HEAD_DIM
    do_refs = refs[:nslot]
    if turn == 0:
        dqkv_ref, sum_ref, dqt_ref = refs[nslot : nslot + 3]
    else:
        dqkv_in, sum_in, dqt_in, dqkv_ref, sum_ref, dqt_ref = refs[nslot : nslot + 6]
    do_ref, q4_ref, do4_ref, delta_ref = refs[-4:]
    me = me_ref[0]
    ends = seq_ends(len_ref)
    for s in range(nslot):
        do_ref[s] = do_refs[s][...]
    if turn == 0:
        sum_ref[...] = jnp.zeros_like(sum_ref)
        dqt_ref[...] = jnp.zeros_like(dqt_ref)
    else:
        sum_ref[...] = sum_in[...]
        dqt_ref[...] = dqt_in[...]
    pick = lax.broadcasted_iota(jnp.int32, (8, width), 1) // HEAD_DIM
    pick = (pick == lax.broadcasted_iota(jnp.int32, (8, width), 0)).astype(F32)

    @pl.loop(0, nslot)
    def _(place):
        rows = slot_rows(place, me, tok)
        q4_ref[place] = spread_heads(q_ref[rows, :], heads)
        do = do_ref[place ^ me]
        do4_ref[place] = spread_heads(do, heads)
        both = do.astype(F32) * att_ref[rows, :]
        if turn == 0:
            sum_ref[:, 3 * width :] += jnp.sum(both, 0, keepdims=True)
        d = dot(pick, both, 1, 1, lax.Precision.HIGHEST)
        delta_ref[place] = jnp.concatenate([d[h : h + 1] for h in range(heads)], axis=1)

    @pl.loop(0, nslot // 2)
    def _(j):
        ki = 4 * (j // 2) + (3 * (j % 2) if turn == 0 else 1 + j % 2)
        rows = slot_rows(ki, me, tok)
        k = k_ref[rows, :]
        v = v_ref[rows, :]
        kt = k.astype(F32).T.astype(BF16)

        def tile(qi, state, masked):
            q4 = q4_ref[qi]
            do4 = do4_ref[qi]
            s = dot(k, q4, 1, 1) * SCORE_SCALE
            if masked:
                pos = query_positions(qi * tok, tok, heads)
                s = hide(s, ki * tok, pos, start_of(ends, pos))
            p = jnp.exp2(s - lse_ref[qi ^ me])
            dp = dot(v, do4, 1, 1)
            ds = (p * (dp - delta_ref[qi])).astype(BF16)
            dv = dot(p.astype(BF16), do4)
            dk = dot(ds, q4)
            dqt_ref[qi] += jnp.concatenate(
                [
                    dot(kt[h * HEAD_DIM : (h + 1) * HEAD_DIM], ds[:, h * tok : (h + 1) * tok])
                    for h in range(heads)
                ],
                axis=1,
            )
            if state is None:
                return dk, dv
            return state[0] + dk, state[1] + dv

        state = tile(ki, None, True)
        k0 = ki * tok
        upto = (end_of(ends, k0 + tok - 1) + tok - 1) // tok
        whole = jnp.clip(end_of(ends, k0) // tok, ki + 1, jnp.maximum(upto, ki + 1))
        state = lax.fori_loop(ki + 1, whole, lambda qi, st: tile(qi, st, False), state)
        dk, dv = lax.fori_loop(whole, upto, lambda qi, st: tile(qi, st, True), state)
        dk = (dk * HEAD_DIM**-0.5).astype(BF16)
        dv = dv.astype(BF16)
        dqkv_ref[rows, width : 2 * width] = dk
        dqkv_ref[rows, 2 * width :] = dv
        sum_ref[:, width : 2 * width] += jnp.sum(dk.astype(F32), 0, keepdims=True)
        sum_ref[:, 2 * width : 3 * width] += jnp.sum(dv.astype(F32), 0, keepdims=True)

    if turn == 0:
        return

    @pl.loop(0, nslot // 2)
    def _(j):
        rows = slot_rows(4 * (j // 2) + 3 * (j % 2), me, tok)
        dqkv_ref[rows, width:] = dqkv_in[rows, width:]

    @pl.loop(0, nslot)
    def _(place):
        dq = (fold_heads(dqt_ref[place], heads, tok) * HEAD_DIM**-0.5).astype(BF16)
        dqkv_ref[slot_rows(place, me, tok), :width] = dq
        sum_ref[:, :width] += jnp.sum(dq.astype(F32), 0, keepdims=True)


def attend_backward(me, lengths, qkv, att, lse, grads, tok, pair, turn, held=()):
    nslot = ROW // tok
    lanes = PAIR // HEAD_DIM * tok
    made = [((ROW, 3 * PAIR), BF16), ((1, 4 * PAIR), F32), ((nslot, HEAD_DIM, lanes), F32)]
    return pl.pallas_call(
        functools.partial(backward_kernel, tok, turn),
        grid=(1,),
        out_shape=[shape(*m) for m in made],
        in_specs=[SMEM_SPEC, SMEM_SPEC]
        + pair_blocks(qkv, pair)
        + [whole_spec(att.shape), whole_spec(lse.shape)]
        + [pl.BlockSpec((tok, PAIR), lambda t: (0, pair))] * nslot
        + [whole_spec(v.shape) for v in held],
        out_specs=[whole_spec(m[0]) for m in made],
        scratch_shapes=[
            pltpu.VMEM((nslot, tok, PAIR), BF16),
            pltpu.VMEM((nslot, lanes, PAIR), BF16),
            pltpu.VMEM((nslot, lanes, PAIR), BF16),
            pltpu.VMEM((nslot, 1, lanes), F32),
        ],
        compiler_params=PARAMS,
        cost_estimate=cost(8),
        name="attend_backward",
    )(me, lengths, qkv, qkv, qkv, att, lse, *grads, *held)


def centred(v):
    center = v - jnp.mean(v, -1, keepdims=True)
    inv = lax.rsqrt(jnp.mean(center * center, -1, keepdims=True) + EPSILON)
    return center * inv, inv


def norm_back(unit, inv, e):
    return inv * (e - jnp.mean(e, -1, keepdims=True) - unit * jnp.mean(e * unit, -1, keepdims=True))


def first_norm_kernel(x_ref, gain_ref, shift_ref, out_ref):
    unit, _ = centred(x_ref[...].astype(F32))
    out_ref[...] = (unit * gain_ref[...] + shift_ref[...]).astype(BF16)


def first_norm(x, gain, shift):
    return pl.pallas_call(
        first_norm_kernel,
        out_shape=shape(x.shape, BF16),
        in_specs=[VMEM_SPEC] * 3,
        out_specs=VMEM_SPEC,
        compiler_params=PARAMS,
        cost_estimate=cost(2),
        name="first_norm",
    )(x, gain, shift)


def qkv_kernel(n, *refs):
    slots = refs[:n]
    weights = refs[n : n + 3]
    bias_ref = refs[n + 3]
    out_ref = refs[-1]
    tok = slots[0].shape[0]
    width = weights[0].shape[1]
    for s in range(n):
        for j in range(3):
            cols = slice(j * width, (j + 1) * width)
            made = dot(slots[s][...], weights[j][...]) + bias_ref[:, cols]
            out_ref[s * tok : (s + 1) * tok, cols] = made.astype(BF16)


def qkv_part(slots, weights, bias, part, earlier=None):
    n = len(slots)
    tok = slots[0].shape[0]
    width = weights[0].shape[1]
    args = [*slots, *weights, bias]
    specs = [VMEM_SPEC] * len(args)
    aliases = {}
    if earlier is not None:
        aliases = {len(args): 0}
        args.append(earlier)
        specs.append(pl.BlockSpec(memory_space=pl.ANY))
    return pl.pallas_call(
        functools.partial(qkv_kernel, n),
        grid=(1,),
        out_shape=shape((ROW, 3 * width), BF16),
        in_specs=specs,
        out_specs=pl.BlockSpec((n * tok, 3 * width), lambda t: (part, 0)),
        input_output_aliases=aliases,
        compiler_params=PARAMS,
        cost_estimate=cost(3),
        name="qkv_part",
    )(*args)


def join_lanes(refs):
    return jnp.concatenate([r[...] for r in refs], axis=1) if len(refs) > 1 else refs[0][...]


def after_attention_kernel(n, pairs, *refs):
    mixed = refs[: n * pairs]
    weights = refs[n * pairs : n * pairs + n]
    vectors = refs[n * pairs + n :]
    tok_ref, bias_ref, gain2_ref, shift2_ref, gain3_ref, shift3_ref = vectors[:6]
    branch_ref, residual_ref, ffn_ref = vectors[6:]
    branch = bias_ref[...]
    for s in range(n):
        branch = branch + dot(join_lanes(mixed[s * pairs : (s + 1) * pairs]), weights[s][...])
    branch_ref[...] = branch
    unit, _ = centred(branch)
    residual = tok_ref[...].astype(F32) + (unit * gain2_ref[...] + shift2_ref[...])
    residual_ref[...] = residual
    unit, _ = centred(residual)
    ffn_ref[...] = (unit * gain3_ref[...] + shift3_ref[...]).astype(BF16)


class Window:
    def __init__(self, array, first, rows):
        self.array, self.first, self.shape = array, first, (rows, array.shape[1])
        self.ndim = 2


def array_of(v):
    return v.array if isinstance(v, Window) else v


def row_tiles(rows, cols, tile):
    return pl.BlockSpec((tile, cols), lambda t: (t, 0))


def fixed(array):
    if isinstance(array, Window):
        at = array.first // array.shape[0]
        return pl.BlockSpec(array.shape, lambda *_: (at, 0))
    return pl.BlockSpec(array.shape, lambda *_: (0,) * array.ndim)


def after_attention(mixed, weights, tokens, *vectors, tile=128):
    rows, d = tokens.shape
    tile = min(tile, rows)
    n, pairs = len(mixed), len(mixed[0])
    mixed = [v for slot in mixed for v in slot]
    wide = row_tiles(rows, d, tile)
    return pl.pallas_call(
        functools.partial(after_attention_kernel, n, pairs),
        grid=(rows // tile,),
        in_specs=[row_tiles(rows, PAIR, tile)] * (n * pairs)
        + [fixed(w) for w in weights]
        + [wide]
        + [fixed(v) for v in vectors],
        out_specs=(wide, wide, wide),
        out_shape=(shape((rows, d), F32), shape((rows, d), F32), shape((rows, d), BF16)),
        compiler_params=PARAMS,
        cost_estimate=cost(3),
        name="after_attention",
    )(*mixed, *map(array_of, weights), tokens, *vectors)


def before_attention_kernel(n, adds, *refs):
    came = refs[:adds]
    residual_ref, branch_ref, cot_ref, gain3_ref, gain2_ref, scale_ref = refs[adds : adds + 6]
    weights = refs[adds + 6 : adds + 6 + n]
    outs = refs[adds + 6 + n :]
    grad_ref, low_ref, sum_ref = outs[:3]
    pieces = outs[3:]
    c = came[0][...].astype(F32)
    for r in came[1:]:
        c = c + r[...].astype(F32)
    unit3, inv3 = centred(residual_ref[...])
    cot = cot_ref[...].astype(F32)
    grad = cot + norm_back(unit3, inv3, c * gain3_ref[...])
    grad_ref[...] = grad
    unit2, inv2 = centred(branch_ref[...])
    low = norm_back(unit2, inv2, grad * gain2_ref[...]).astype(BF16)
    low_ref[...] = low

    @pl.when(pl.program_id(0) == 0)
    def _():
        sum_ref[...] = jnp.zeros_like(sum_ref)

    tops = [grad * unit2, grad, c * unit3, c, low.astype(F32), cot]
    sums = [jnp.sum(v, 0, keepdims=True) for v in tops]
    sum_ref[...] += jnp.concatenate(sums + [jnp.zeros_like(sums[0])] * 2, axis=0)
    width = pieces[0].shape[1]
    for s in range(n):
        made = dot(low, weights[s][...], 1, 1) * scale_ref[:, s * width : (s + 1) * width]
        pieces[s][...] = made.astype(BF16)


def before_attention(came, residual, branch, cot, gain3, gain2, scale_slots, weights, tile=128):
    rows, d = residual.shape
    width = weights[0].shape[0]
    tile = min(tile, rows)
    n = len(weights)
    wide = row_tiles(rows, d, tile)
    vectors = [gain3, gain2, scale_slots]
    out = pl.pallas_call(
        functools.partial(before_attention_kernel, n, len(came)),
        grid=(rows // tile,),
        in_specs=[wide] * (len(came) + 3)
        + [fixed(v) for v in vectors]
        + [fixed(w) for w in weights],
        out_specs=(wide, wide, pl.BlockSpec((8, d), lambda t: (0, 0)))
        + (row_tiles(rows, width, tile),) * n,
        out_shape=(shape((rows, d), F32), shape((rows, d), BF16), shape((8, d), F32))
        + (shape((rows, width), BF16),) * n,
        compiler_params=PARAMS,
        cost_estimate=cost(3),
        name="before_attention",
    )(*came, residual, branch, cot, *vectors, *map(array_of, weights))
    return out[0], out[1], out[2], list(out[3:])


def last_norm_kernel(adds, *refs):
    came = refs[:adds]
    x_ref, grad_ref, gain_ref, out_ref = refs[adds:]
    c = came[0][...].astype(F32)
    for r in came[1:]:
        c = c + r[...].astype(F32)
    unit, inv = centred(x_ref[...].astype(F32))
    out_ref[...] = grad_ref[...] + norm_back(unit, inv, c * gain_ref[...])


def last_norm(came, x, grad, gain, tile=128):
    rows, d = x.shape
    tile = min(tile, rows)
    wide = row_tiles(rows, d, tile)
    return pl.pallas_call(
        functools.partial(last_norm_kernel, len(came)),
        grid=(rows // tile,),
        in_specs=[wide] * (len(came) + 2) + [fixed(gain)],
        out_specs=wide,
        out_shape=shape((rows, d), F32),
        compiler_params=PARAMS,
        cost_estimate=cost(2),
        name="last_norm",
    )(*came, x, grad, gain)


def gelu_parts(u):
    k = math.sqrt(2 / math.pi)
    square = u * u
    t = jnp.tanh(u * (k + (k * 0.044715) * square))
    return 0.5 + 0.5 * t, t, square


def pick_piece(refs, places):
    step = pl.program_id(0)
    out = refs[0][...]
    for ref, (first, _, _) in zip(refs[1:], places[1:]):
        out = jnp.where(step >= first, ref[...], out)
    return out


def places_of(pieces, tile):
    places, at = [], 0
    for v in pieces:
        first = v.first // tile if isinstance(v, Window) else 0
        places.append((at, v.shape[0] // tile, first))
        at += v.shape[0] // tile
    return tuple(places)


def piece_tiles(places, tile, cols):
    return [
        pl.BlockSpec((tile, cols), lambda t, f=f, c=c, a=a: (jnp.clip(t - f, 0, c - 1) + a, 0))
        for f, c, a in places
    ]


def ffn_first_kernel(xp, cp, *refs):
    n = len(xp) + len(cp)
    w1_ref, b1_ref, gain_ref, w2_ref = refs[n : n + 4]
    u_ref, hg_ref, stat_ref = refs[n + 4 :]
    units = u_ref.shape[1]
    u = dot(pick_piece(refs[: len(xp)], xp), w1_ref[...]) + b1_ref[...]
    u_ref[...] = u
    half, _, _ = gelu_parts(u)
    a = u * half
    total = jnp.sum(a, 1, keepdims=True)
    d = a - total * (1.0 / units)
    hg = dot(pick_piece(refs[len(xp) : n], cp), w2_ref[...], 1, 1)
    hg_ref[...] = hg
    sg = hg * gain_ref[...]
    cols = [
        total,
        jnp.sum(d * d, 1, keepdims=True),
        jnp.sum(sg, 1, keepdims=True),
        jnp.sum(sg * d, 1, keepdims=True),
    ]
    lane = lax.broadcasted_iota(jnp.int32, (u.shape[0], 128), 1)
    wide = jnp.zeros(lane.shape, F32)
    for j, col in enumerate(cols):
        wide = jnp.where(lane == j, col, wide)
    stat_ref[...] = wide.T[:8]


def ffn_first(xs, cots, w1, b1, gain, w2, tile=256):
    d, units = w1.shape
    tile = min(tile, *(v.shape[0] for v in (*xs, *cots)))
    xp, cp = places_of(xs, tile), places_of(cots, tile)
    rows = sum(v.shape[0] for v in xs)
    return pl.pallas_call(
        functools.partial(ffn_first_kernel, xp, cp),
        grid=(rows // tile,),
        in_specs=piece_tiles(xp, tile, d)
        + piece_tiles(cp, tile, d)
        + [fixed(v) for v in (w1, b1, gain, w2)],
        out_specs=(
            row_tiles(rows, units, tile),
            row_tiles(rows, units, tile),
            pl.BlockSpec((8, tile), lambda t: (0, t)),
        ),
        out_shape=(shape((rows, units), F32), shape((rows, units), F32), shape((8, rows), F32)),
        compiler_params=PARAMS,
        cost_estimate=cost(5),
        name="ffn_first",
    )(*xs, *map(array_of, cots), w1, b1, gain, w2)


def ffn_second_kernel(ndev, n, per, *refs):
    u_ref, hg_ref, gain_ref, shift_ref, w1_ref = refs[:5]
    stats = [r[...] for r in refs[5 : 5 + ndev]]
    hid_ref, fg_ref, sum_ref = refs[-3 - n : -n]
    backs = refs[-n:]
    units = u_ref.shape[1]
    mean = sum(s[0:1] for s in stats) * (1.0 / FF)
    spread = jnp.zeros_like(mean)
    total = jnp.zeros_like(mean)
    cross = jnp.zeros_like(mean)
    for s in stats:
        gap = s[0:1] * (1.0 / units) - mean
        spread += s[1:2] + units * (gap * gap)
        total += s[2:3]
        cross += s[3:4] + gap * s[2:3]
    inv = lax.rsqrt(spread * (1.0 / FF) + EPSILON)
    packed = [mean, inv, total * (1.0 / FF), cross * inv * (1.0 / FF)]
    packed = jnp.concatenate(packed + [jnp.zeros_like(mean)] * 4, axis=0).T
    mean, inv, total, cross = (packed[:, j : j + 1] for j in range(4))
    u = u_ref[...]
    hg = hg_ref[...]
    half, t, square = gelu_parts(u)
    unit = (u * half - mean) * inv
    gain = gain_ref[...]
    hid_ref[...] = (unit * gain + shift_ref[...]).astype(BF16)
    k = math.sqrt(2 / math.pi)
    slope = half + (0.5 * u) * ((1.0 - t * t) * (k + (3 * k * 0.044715) * square))
    fg = (inv * (hg * gain - total - unit * cross) * slope).astype(BF16)
    fg_ref[...] = fg
    back = dot(fg, w1_ref[...], 1, 1).astype(BF16)
    step = pl.program_id(0) // per
    for s in range(n):

        @pl.when(step == s)
        def _(s=s):
            backs[s][...] = back

    @pl.when(pl.program_id(0) == 0)
    def _():
        sum_ref[...] = jnp.zeros_like(sum_ref)

    sums = [jnp.sum(v, 0, keepdims=True) for v in (hg * unit, hg, fg.astype(F32))]
    sum_ref[...] += jnp.concatenate(sums + [jnp.zeros((5, units), F32)], axis=0)


def ffn_second(u, hg, gain, shift, w1, stats, tok, part, earlier=None, tile=256):
    rows, units = u.shape
    d = w1.shape[0]
    tile = min(tile, tok)
    per = tok // tile
    ndev = len(stats)
    n = rows // tok
    skip = part * n * per

    def stat_place(s):
        return lambda t: (0, (((t + skip) // per) ^ s) * per + t % per)

    in_specs = [row_tiles(rows, units, tile)] * 2 + [fixed(v) for v in (gain, shift, w1)]
    in_specs += [pl.BlockSpec((8, tile), stat_place(s)) for s in range(ndev)]
    args = [u, hg, gain, shift, w1, *stats]
    aliases = {}
    if earlier is not None:
        in_specs += [pl.BlockSpec(memory_space=pl.ANY)] * 2
        aliases = {len(args): 0, len(args) + 1: 1}
        args += list(earlier)
    moved = pl.BlockSpec((tile, units), lambda t: (t + skip, 0))
    out = pl.pallas_call(
        functools.partial(ffn_second_kernel, ndev, n, per),
        grid=(rows // tile,),
        in_specs=in_specs,
        out_specs=(moved, moved, pl.BlockSpec((8, units), lambda t: (0, 0)))
        + tuple(piece_tiles([(s * per, per, 0) for s in range(n)], tile, d)),
        out_shape=(shape((ROW, units), BF16), shape((ROW, units), BF16), shape((8, units), F32))
        + (shape((tok, d), BF16),) * n,
        input_output_aliases=aliases,
        compiler_params=PARAMS,
        cost_estimate=cost(5),
        name="ffn_second",
    )(*args)
    return out[0], out[1], out[2], list(out[3:])


def products_kernel(nx, nw, flip, groups, *refs):
    xs, ws, outs = refs[:nx], refs[nx : nx + nw], refs[nx + nw :]
    cols = xs[0].shape[1] // nw
    tok = xs[0].shape[0] // sum(len(g) for g in groups)
    for group, out in zip(groups, outs):
        for at, s in enumerate(group):
            total = None
            for j, w in enumerate(ws):
                left = [x[s * tok : (s + 1) * tok, j * cols : (j + 1) * cols] for x in xs]
                left = jnp.concatenate(left, axis=1) if nx > 1 else left[0]
                made = dot(left, w[...], 1, 1 if flip else 0)
                total = made if total is None else total + made
            out[at * tok : (at + 1) * tok, :] = total.astype(BF16)


def products(xs, weights, flip, tok, first, groups):
    n = sum(len(g) for g in groups)
    d = weights[0].shape[0 if flip else 1]
    out = pl.pallas_call(
        functools.partial(products_kernel, len(xs), len(weights), flip, groups),
        grid=(1,),
        in_specs=[pl.BlockSpec((n * tok, x.shape[1]), lambda t: (first // n, 0)) for x in xs]
        + [fixed(w) for w in weights],
        out_specs=[whole_spec((len(g) * tok, d)) for g in groups],
        out_shape=[shape((len(g) * tok, d), BF16) for g in groups],
        compiler_params=PARAMS,
        cost_estimate=cost(2),
        name="products",
    )(*xs, *weights)
    return list(out)


def head_gradient_kernel(n, pairs, groups, *refs):
    left = refs[n * pairs][...]
    d = left.shape[1]
    for group, out in zip(groups, refs[n * pairs + 1 :]):
        for at, s in enumerate(group):
            made = dot(left, join_lanes(refs[s * pairs : (s + 1) * pairs]), 0, 0)
            out[at * d : (at + 1) * d, :] = made.astype(BF16)


def head_gradient(mixed, low, groups):
    n, pairs = len(mixed), len(mixed[0])
    d = low.shape[1]
    mixed = [v for slot in mixed for v in slot]
    return list(
        pl.pallas_call(
            functools.partial(head_gradient_kernel, n, pairs, groups),
            out_shape=[shape((len(g) * d, pairs * PAIR), BF16) for g in groups],
            in_specs=[VMEM_SPEC] * (n * pairs + 1),
            out_specs=[VMEM_SPEC] * len(groups),
            compiler_params=PARAMS,
            cost_estimate=cost(2),
            name="head_gradient",
        )(*mixed, low)
    )


def gradient_kernel(steps, nl, nr, nj, extra, me_ref, *refs):
    del me_ref
    joins, refs = refs[:nj], refs[nj:]
    lefts, rights = refs[:nl], refs[nl : nl + nr]
    send_ref, keep_ref = refs[nl + nr + extra : nl + nr + extra + 2]
    step = pl.program_id(0)
    pieces = rights if nr > 1 else lefts
    total = None
    at = 0
    for s, piece in enumerate(pieces):
        rows = slice(at, at + piece.shape[0])
        at += piece.shape[0]
        left = lefts[s][...] if nl > 1 else lefts[0][rows, :]
        right = rights[s][...] if nr > 1 else rights[0][rows, :]
        made = dot(left, right, 0, 0)
        total = made if total is None else total + made

    made = total.astype(BF16)
    if nj:
        more = joins[0][...].astype(F32)
        for r in joins[1:]:
            more = more + r[...].astype(F32)
        made = jnp.concatenate([made, more.astype(BF16)], axis=1)

    @pl.when(step < steps // 2)
    def _():
        send_ref[...] = made

    @pl.when(step >= steps // 2)
    def _():
        keep_ref[...] = made

    if extra:
        weights = refs[nl + nr : nl + nr + extra - 1]
        sum_ref = refs[nl + nr + extra - 1]
        width = weights[0].shape[1]
        cross = jnp.zeros((total.shape[0], width), F32)
        plain = cross
        for j, w_ref in enumerate(weights):
            cols = slice(j * width, (j + 1) * width)
            w = w_ref[...].astype(F32)
            cross += w * total[:, cols]
            plain += w * sum_ref[:, cols]
        cross = jnp.sum(cross, 1, keepdims=True)
        plain = jnp.sum(plain, 1, keepdims=True)
        lane = lax.broadcasted_iota(jnp.int32, (total.shape[0], 128), 1)
        wide = jnp.where(lane == 0, cross, jnp.where(lane == 1, plain, 0.0))
        refs[-1][...] = wide.T[:8]


def gradient(side, lefts, rights, weights=(), pair=0, sums=None, joins=(), steps=4):
    m = lefts[0].shape[1]
    steps = min(steps, m // 128)
    size = m // steps
    n = rights[0].shape[1]
    nl, nr = len(lefts), len(rights)
    n += joins[0].shape[1] if joins else 0
    extra = len(weights) + 1 if weights else 0

    def chunk_of(t, side):
        return (t + (1 - side[0]) * (steps // 2)) % steps

    def join_spec(v):
        at = v.first // size if isinstance(v, Window) else 0
        return pl.BlockSpec((size, v.shape[1]), lambda t, me: (chunk_of(t, me) + at, 0))

    in_specs = [join_spec(v) for v in joins]
    in_specs += [pl.BlockSpec((v.shape[0], size), lambda t, me: (0, chunk_of(t, me))) for v in lefts]
    in_specs += [fixed(v) for v in rights]
    in_specs += [pl.BlockSpec((size, PAIR), lambda t, me: (chunk_of(t, me), pair)) for w in weights]
    out_specs = [
        pl.BlockSpec((size, n), lambda t, me: (jnp.minimum(t, steps // 2 - 1), 0)),
        pl.BlockSpec((size, n), lambda t, me: (jnp.maximum(t - steps // 2, 0), 0)),
    ]
    out_shape = [shape((m // 2, n), BF16)] * 2
    args = [side, *map(array_of, joins), *lefts, *map(array_of, rights), *weights]
    if extra:
        args.append(sums)
        in_specs.append(pl.BlockSpec(sums.shape, lambda t, me: (0, 0)))
        out_specs.append(pl.BlockSpec((8, size), lambda t, me: (0, chunk_of(t, me))))
        out_shape.append(shape((8, m), F32))
    return pl.pallas_call(
        functools.partial(gradient_kernel, steps, nl, nr, len(joins), extra),
        grid_spec=pltpu.PrefetchScalarGridSpec(
            num_scalar_prefetch=1, grid=(steps,), in_specs=in_specs, out_specs=out_specs
        ),
        out_shape=out_shape,
        compiler_params=PARAMS,
        cost_estimate=cost(4),
        name="gradient",
    )(*args)


def assemble_kernel(nx, cols, turned, side_ref, *refs):
    mine, came, outs = refs[:nx], refs[nx : 2 * nx], refs[2 * nx :]
    size = mine[0].shape[0]
    side = side_ref[0]
    n = len(outs) - (1 if turned else 0)
    for x in range(nx):
        for ref, first in ((mine[x], side * size), (came[x], (1 - side) * size)):
            first = pl.multiple_of(first, size)
            for j in range(n):
                made = ref[:, j * cols : (j + 1) * cols].astype(F32)
                outs[j][pl.ds(first, size), x * cols : (x + 1) * cols] = made
            if x == 0 and turned:
                outs[n][:, pl.ds(first, size)] = ref[:, n * cols :].astype(F32).T


def assemble(side, mine, came, cols, turned=0):
    size = mine[0].shape[0]
    n = (mine[0].shape[1] - turned) // cols
    out = [shape((2 * size, cols * len(mine)), F32)] * n
    if turned:
        out = out + [shape((turned, 2 * size), F32)]
    return pl.pallas_call(
        functools.partial(assemble_kernel, len(mine), cols, turned),
        out_shape=out,
        in_specs=[SMEM_SPEC] + [VMEM_SPEC] * (2 * len(mine)),
        out_specs=[VMEM_SPEC] * len(out),
        compiler_params=PARAMS,
        cost_estimate=cost(2),
        name="assemble",
    )(side, *mine, *came)


def swap(value, axis, size, bit):
    return lax.ppermute(value, axis, [(i, i ^ bit) for i in range(size)])


def bits_of(size):
    return [1 << b for b in range(size.bit_length() - 1)]


def after(value, *others):
    return lax.optimization_barrier((value, *others))[0]


def spread_low(slots, axis, size, bits):
    slots = dict(slots)
    for bit in bits:
        slots.update({s | bit: swap(v, axis, size, bit) for s, v in slots.items()})
    return slots


def add_low(left, right):
    return (left.astype(F32) + right.astype(F32)).astype(BF16)


def direct_slots(value, axis, size):
    return [value] + [swap(value, axis, size, s) for s in range(1, size)]


class Scatter:
    def __init__(self, size):
        self.size = size
        self.low = bits_of(size)[:-1]
        self.top = size // 2

    def within(self, parts):
        held = {s: [v] for s, v in parts.items()}
        for bit in self.low:
            for s in sorted(held, reverse=True):
                if s & bit:
                    terms = held.pop(s)
                    total = terms[0]
                    for t in terms[1:]:
                        total = add_low(total, t)
                    held[s ^ bit].append(swap(total, "mp", self.size, bit))
        [(_, terms)] = held.items()
        return terms

    def across(self, terms):
        total = terms[0].astype(F32)
        for t in terms[1:]:
            total = total + t.astype(F32)
        total = total.astype(BF16)
        return total, swap(total, "mp", self.size, self.top)


class Stream:
    def __init__(self, dp, bits, send, keep):
        self.dp = dp
        self.index = lax.axis_index("dp")
        self.bits = bits
        self.stage = 0
        self.held = keep
        self.came = swap(send, "dp", dp, bits[0])

    def advance(self, *tie):
        n = len(self.bits)
        if self.stage == 2 * n - 1:
            return self.held
        held, came = after(self.held, *tie), after(self.came, *tie)
        self.stage += 1
        if self.stage <= n:
            cur = add_low(held, came)
            if self.stage == n:
                self.held = send = cur
                bit = self.bits[-1]
            else:
                bit = self.bits[self.stage]
                upper = (self.index & bit) != 0
                low, high = cur[: cur.shape[0] // 2], cur[cur.shape[0] // 2 :]
                send = jnp.where(upper, low, high)
                self.held = jnp.where(upper, high, low)
        else:
            upper = (self.index & self.bits[2 * n - self.stage]) != 0
            low, high = jnp.where(upper, came, held), jnp.where(upper, held, came)
            self.held = send = jnp.concatenate([low, high])
            bit = self.bits[2 * n - self.stage - 1]
        self.came = swap(send, "dp", self.dp, bit)
        return send

    def done(self, *tie):
        while self.stage < 2 * len(self.bits) - 1:
            self.advance(*tie)
        return self


class Direct:
    def __init__(self, dp, send, keep):
        self.dp = dp
        self.index = lax.axis_index("dp")
        self.held = keep
        self.came = swap(send, "dp", dp, 1)
        self.stage = 0

    def others(self, parts):
        return [parts[0]] + [swap(v, "dp", self.dp, 2 * j) for j, v in enumerate(parts) if j]

    def ordered(self, parts):
        bit = 2
        step = 1
        while step < len(parts):
            upper = (self.index & bit) != 0
            parts = [jnp.where(upper, parts[j ^ step], v) for j, v in enumerate(parts)]
            bit, step = 2 * bit, 2 * step
        return parts

    def advance(self, *tie):
        n = self.dp // 2
        self.stage += 1
        if self.stage == 1:
            total = add_low(after(self.held, *tie), after(self.came, *tie))
            size = total.shape[0] // n
            parts = self.ordered([total[j * size : (j + 1) * size] for j in range(n)])
            self.parts = self.others(parts)
            return parts[0]
        if self.stage == 2:
            total = sum(after(v, *tie).astype(F32) for v in self.parts).astype(BF16)
            self.parts = self.others([total] * n)
            return total
        if self.stage == 3:
            parts = [after(v, *tie) for v in self.parts]
            self.held = jnp.concatenate(self.ordered(parts))
            self.came = swap(self.held, "dp", self.dp, 1)
        return self.held

    def done(self, *tie):
        while self.stage < 3:
            self.advance(*tie)
        return self


def on_device(
    dp,
    mp,
    tokens,
    lengths,
    norm1_gain,
    norm1_shift,
    query_weight,
    query_bias,
    key_weight,
    value_weight,
    value_bias,
    head_scale,
    output_weight,
    output_bias,
    norm2_gain,
    norm2_shift,
    norm3_gain,
    norm3_shift,
    fc1_weight,
    fc1_bias,
    mid_gain,
    mid_shift,
    fc2_weight,
    fc2_bias,
    out_grad,
):
    tok, d = tokens.shape
    width = query_weight.shape[1]
    heads = width // HEAD_DIM
    pairs = width // PAIR
    half = mp // 2
    units = fc1_weight.shape[1]
    me = lax.axis_index("mp").astype(jnp.int32)
    me_arr = me[None]
    index = lax.axis_index("dp").astype(jnp.int32)
    plain = bits_of(dp)
    turned = [plain[1], plain[0], *plain[2:]]
    side, side_turned = (index & 1)[None], ((index >> 1) & 1)[None]
    lower = list(reversed(bits_of(mp)[:-1]))
    scatter = Scatter(mp)
    one_by_one = [[s] for s in range(half)]
    merged = [[0], [2], [1, 3]] if mp == 4 else [[s] for s in range(mp)]

    def merged_terms(outs, rows):
        if mp != 4:
            return scatter.within(dict(enumerate(outs[:half]))), scatter.within(
                {half + j: v for j, v in enumerate(outs[half:])}
            )
        came = swap(outs[2], "mp", mp, 1)
        return [outs[0], Window(came, 0, rows)], [outs[1], Window(came, rows, rows)]

    def plain_rows(v):
        return v.array[v.first : v.first + v.shape[0]] if isinstance(v, Window) else v

    def wide_swap(v):
        return swap(v, "mp", mp, half)

    def listed(near, far):
        slots = {**near, **far}
        return [slots[s] for s in range(mp)]

    def row(v):
        return v[None]

    qkv_weights = (query_weight, key_weight, value_weight)
    bias_qkv = jnp.concatenate([query_bias, jnp.zeros_like(query_bias), value_bias])[None]
    scale_lanes = jnp.repeat(head_scale, HEAD_DIM)[None]
    place = me * tok + lax.broadcasted_iota(jnp.int32, (tok, 1), 0)
    cot_low = jnp.where(place < jnp.sum(lengths), out_grad, jnp.zeros_like(out_grad))

    normed_own = first_norm(tokens, row(norm1_gain), row(norm1_shift))
    normed_far = wide_swap(normed_own)
    normed_near = spread_low({0: normed_own}, "mp", mp, lower)
    start = normed_near[half - 1]
    qkv = qkv_part([normed_near[s] for s in range(half)], qkv_weights, bias_qkv, 0)
    cot_low, output_weight = (after(v, start) for v in (cot_low, output_weight))
    cot_near = spread_low({0: cot_low}, "mp", mp, lower)
    out_near = spread_low({0: output_weight}, "mp", mp, lower)
    both = jnp.concatenate([cot_low, output_weight])
    normed_far = after(normed_far, qkv, both, cot_near[half - 1], out_near[half - 1])
    both_far = wide_swap(after(both, normed_far))
    normed_far = spread_low({half: normed_far}, "mp", mp, lower)
    qkv = qkv_part([normed_far[half + s] for s in range(half)], qkv_weights, bias_qkv, 1, qkv)
    normed = listed(normed_near, normed_far)

    far_first = [*range(half, mp), *range(1, half)]
    atts, lses, mixed = [], [], [[] for _ in range(mp)]
    mark = (qkv,)
    for p in range(pairs):
        att, lse, mix = attend_forward(me_arr, lengths, after(qkv, *mark), scale_lanes, tok, p)
        atts.append(att)
        lses.append(lse)
        if p > 0:
            mix = [after(v, *(m[-1] for m in mixed[1:])) for v in mix]
        mixed[0].append(mix[0])
        for s in far_first:
            mixed[s].append(swap(mix[s], "mp", mp, s))
        mark = (mix[0],)
    both_far = spread_low({half: after(both_far, mix[0])}, "mp", mp, lower)
    cot_far = {s: Window(v, 0, tok) for s, v in both_far.items()}
    out_far = {s: Window(v, tok, width) for s, v in both_far.items()}
    out_rows = listed(out_near, out_far)
    branch, residual, ffn_own = after_attention(
        mixed,
        out_rows,
        tokens,
        *(row(v) for v in (output_bias, norm2_gain, norm2_shift, norm3_gain, norm3_shift)),
    )

    ffn_far = wide_swap(ffn_own)
    ffn_near = spread_low({0: ffn_own}, "mp", mp, lower)
    scale_slots = direct_slots(after(scale_lanes, ffn_own), "mp", mp)
    ffn_args = (fc1_weight, row(fc1_bias), row(mid_gain), fc2_weight)
    u_near, hg_near, st_near = ffn_first(
        [ffn_near[s] for s in range(half)], [cot_near[s] for s in range(half)], *ffn_args
    )
    ffn_far = spread_low({half: after(ffn_far, st_near)}, "mp", mp, lower)
    ffn_args = (fc1_weight, after(row(fc1_bias), *scale_slots[1:]), row(mid_gain), fc2_weight)
    cots = listed(cot_near, cot_far)
    ffn_in = listed(ffn_near, ffn_far)
    u_far, hg_far, st_far = ffn_first(ffn_in[half:], cots[half:], *ffn_args)
    stats = direct_slots(jnp.concatenate([st_near, st_far], axis=1), "mp", mp)
    ffn_args = (row(mid_gain), row(mid_shift), fc1_weight, stats, tok)
    hid, fg, mid_far, back_far = ffn_second(u_far, hg_far, *ffn_args, 1)
    back_far = scatter.within({half + j: v for j, v in enumerate(back_far)})
    hid, fg, mid_near, back_near = ffn_second(u_near, hg_near, *ffn_args, 0, (hid, fg))
    scale_slots = jnp.concatenate(scale_slots, axis=1)
    back_far[1:] = [after(v, mid_near) for v in back_far[1:]]
    back_sum, back_far = scatter.across(back_far)
    back_near = scatter.within(dict(enumerate(back_near)))

    send, keep = gradient(side, [after(hid, back_sum)], cots)
    fc2 = Stream(dp, plain, send, keep)
    send, keep = gradient(side_turned, ffn_in, [after(fg, send)])
    fc1 = Stream(dp, turned, send, keep)
    hid = after(hid, send)
    out_near_terms, out_far_terms = merged_terms(
        products([hid], [fc2_weight], False, tok, 0, merged), tok
    )
    came = [after(v, *(t for t in out_far_terms if not isinstance(t, Window))) for v in (*back_near, back_far)]
    residual_grad, branch_low, sums, grads = before_attention(
        came, residual, branch, cot_low, row(norm3_gain), row(norm2_gain), scale_slots, out_rows
    )

    do = {s: swap(grads[s], "mp", mp, s) for s in far_first}
    do = [grads[0]] + [do[s] for s in range(1, mp)]
    mark = fc1.advance(branch_low)
    mark = fc2.advance(mark)
    low = after(branch_low, mark, *do[1:half])
    g_near_terms, g_far_terms = merged_terms(head_gradient(mixed, low, merged), d)
    g_out_sum, g_out_top = scatter.across([plain_rows(v) for v in g_far_terms])
    out_far_terms = [after(plain_rows(v), g_out_sum) for v in out_far_terms]
    out_sum, out_top = scatter.across(out_far_terms)
    mark = after(out_sum, *do[1:])
    mark = fc2.advance(mark)
    mark = fc1.advance(mark)

    dqkvs, sums_att, rows, streams = [], [], [], []

    def between(call):
        nonlocal mark
        if call == 0:
            mark = fc2.advance(mark)
        elif call == 1:
            mark = fc1.advance(after(mark, g_out_top))
            mark = fc2.advance(mark)
        elif call == 2:
            mark = fc1.advance(mark)
            mark = fc2.advance(mark)
            for stream in streams:
                mark = stream.advance(mark)

    call = 0
    for p in range(pairs):
        held = ()
        for turn in range(2):
            held = attend_backward(
                me_arr, lengths, after(qkv, mark), atts[p], lses[p], do, tok, p, turn, held
            )
            mark = held[0]
            between(call)
            call += 1
        dqkv, sum_att, _ = held
        dqkvs.append(dqkv)
        sums_att.append(sum_att)
        if p < pairs - 1:
            joins = [*g_near_terms, g_out_top] if p == 0 else ()
            send, keep, r = gradient(
                side, normed, [after(dqkv, mark)], qkv_weights, p, sum_att, joins
            )
            rows.append(r)
            streams.append(Stream(dp, plain, send, keep))
            mark = send

    mark = after(mark, out_top)
    mark = fc1.advance(mark)
    for stream in streams:
        mark = stream.advance(mark)
    joins = [*g_near_terms, g_out_top] if pairs == 1 else ()
    send, keep, r = gradient(
        side, normed, [after(dqkvs[-1], mark)], qkv_weights, pairs - 1, sums_att[-1], joins
    )
    rows.append(r)
    last = Direct(dp, send, keep)
    far = products(
        [after(v, send) for v in dqkvs], qkv_weights, True, tok, half, one_by_one
    )
    far_terms = scatter.within({half + j: v for j, v in enumerate(far)})
    packed = jnp.concatenate([sums[:6], sum(rows)[:2]])
    packed = jnp.broadcast_to(after(packed, far[0])[None], (mp, *packed.shape))
    packed = lax.all_to_all(packed, "mp", 0, 0)
    near = products([after(v, far[0]) for v in dqkvs], qkv_weights, True, tok, 0, one_by_one)
    far_terms[1:] = [after(v, near[0]) for v in far_terms[1:]]
    far_sum, far_top = scatter.across(far_terms)
    near_terms = scatter.within(dict(enumerate(near)))
    fc2.done(far_sum)
    [grad_fc2_weight] = assemble(side, [after(fc2.held, far_sum)], [fc2.came], fc2.held.shape[1])
    for stream in streams:
        mark = stream.advance(grad_fc2_weight)
    mark = last.advance(mark)
    packed = after(packed, mark).sum(0)
    mids = jnp.pad(mid_near + mid_far, ((0, 0), (0, d - units)))[:4]
    heads_sums = jnp.concatenate(sums_att, axis=1)
    heads_sums = jnp.pad(heads_sums, ((0, 3), (0, d - heads_sums.shape[1])))
    packed = jnp.concatenate([packed, mids, heads_sums])
    packed = jnp.broadcast_to(packed[None], (dp, *packed.shape))
    sent = packed
    packed = lax.all_to_all(packed, "dp", 0, 0)
    fc1.done(sent)
    [grad_fc1_weight] = assemble(
        side_turned, [after(fc1.held, sent)], [fc1.came], fc1.held.shape[1]
    )
    for stream in streams:
        mark = stream.advance(grad_fc1_weight)
    mark = last.advance(mark)
    for stream in streams:
        mark = stream.advance(mark)
    token_grad = last_norm(
        [*near_terms, after(far_top, mark)], tokens, residual_grad, row(norm1_gain)
    )
    mark = last.advance(token_grad)
    output = residual + row(fc2_bias)
    for t in (*out_near_terms, out_top):
        output = output + after(plain_rows(t), mark).astype(F32)
    output = output.astype(BF16)
    packed = after(packed, mark).sum(0)
    streams.append(last)
    for stream in streams:
        stream.done(mark)
    grad_query_weight, grad_key_weight, grad_value_weight, grad_output_weight = assemble(
        side, [v.held for v in streams], [v.came for v in streams], PAIR, width
    )
    shift1 = packed[7]
    gain1 = (packed[6] - norm1_shift * shift1) / norm1_gain
    per_head = packed[12, : 4 * width].reshape(pairs, 4, PAIR)
    return (
        output,
        token_grad,
        gain1,
        shift1,
        grad_query_weight,
        per_head[:, 0].reshape(width),
        grad_key_weight,
        grad_value_weight,
        per_head[:, 2].reshape(width),
        jnp.sum(per_head[:, 3].reshape(heads, HEAD_DIM), 1) / head_scale,
        grad_output_weight,
        packed[4],
        packed[0],
        packed[1],
        packed[2],
        packed[3],
        grad_fc1_weight,
        packed[10, :units],
        packed[8, :units],
        packed[9, :units],
        grad_fc2_weight,
        packed[5],
    )


def solution(mesh):
    own = P(("dp", "mp"), None)
    cols, rows, vec, same = P(None, "mp"), P("mp", None), P("mp"), P()
    ends = (cols, vec, vec, vec, rows, same)
    norms = (same,) * 5
    in_specs = (own, P("dp", None), same, same, cols, vec, cols, cols, vec, vec, rows, *norms, *ends, own)
    out_specs = (own, own, same, same, cols, vec, cols, cols, vec, vec, rows, *norms, *ends)
    return jax.shard_map(
        functools.partial(on_device, mesh.shape["dp"], mesh.shape["mp"]),
        mesh=mesh,
        in_specs=in_specs,
        out_specs=out_specs,
        check_vma=False,
    )
```

```python
import functools
import math

import jax
import jax.numpy as jnp
from jax import lax
from jax.experimental import pallas as pl
from jax.experimental.pallas import tpu as pltpu
from jax.sharding import PartitionSpec as P

HEAD_DIM = 64
FF = 4096
ROW = 2048
PAIR = 2 * HEAD_DIM
EPSILON = 1e-05
MASKED = -1000000000.0
LOG2E = math.log2(math.e)
SCORE_SCALE = LOG2E * HEAD_DIM**-0.5
SMEM_SPEC = pl.BlockSpec(memory_space=pltpu.SMEM)
VMEM_SPEC = pl.BlockSpec(memory_space=pltpu.VMEM)
BF16 = jnp.bfloat16
F32 = jnp.float32
PARAMS = pltpu.CompilerParams(vmem_limit_bytes=56 * 2**20)


def shape(dims, dtype):
    return jax.ShapeDtypeStruct(dims, dtype)


def cost(us):
    return pl.CostEstimate(flops=int(us * 1e10), bytes_accessed=int(us * 3.6e7), transcendentals=0)


def dot(a, b, ca=1, cb=0, precision=None):
    return lax.dot_general(
        a, b, (((ca,), (cb,)), ((), ())), preferred_element_type=F32, precision=precision
    )


def spread_heads(block, heads):
    lane = lax.broadcasted_iota(jnp.int32, (1, block.shape[1]), 1) // HEAD_DIM
    zero = jnp.zeros_like(block)
    return jnp.concatenate([jnp.where(lane == h, block, zero) for h in range(heads)], axis=0)


def seq_ends(len_ref):
    ends = []
    total = jnp.int32(0)
    for j in range(len_ref.shape[-1]):
        total = total + len_ref[0, j]
        ends.append(total)
    return ends


def start_of(ends, pos):
    first = jnp.zeros_like(pos)
    for e in ends:
        first = jnp.maximum(first, jnp.where(e <= pos, e, 0))
    return first


def query_positions(q0, tok, heads):
    lane = lax.broadcasted_iota(jnp.int32, (1, tok), 1) + q0
    return jnp.concatenate([lane] * heads, axis=1)


def hide(scores, k0, pos, first):
    key = lax.broadcasted_iota(jnp.int32, scores.shape, 0) + k0
    return jnp.where((key >= first) & (key <= pos), scores, MASKED)


def slot_rows(place, me, tok):
    return pl.ds(pl.multiple_of((place ^ me) * tok, tok), tok)


def fold_heads(side, heads, tok):
    return jnp.concatenate([side[:, h * tok : (h + 1) * tok] for h in range(heads)], axis=0).T


def key_range(ends, place, tok):
    begin = start_of(ends, place * tok) // tok
    whole = (start_of(ends, place * tok + tok - 1) + tok - 1) // tok
    return begin, jnp.minimum(whole, place)


def forward_kernel(tok, me_ref, len_ref, q_ref, k_ref, v_ref, scale_ref, *refs):
    nslot = ROW // tok
    width = q_ref.shape[1]
    heads = width // HEAD_DIM
    att_ref, lse_ref = refs[:2]
    mix_refs = refs[2 : 2 + nslot]
    vt_ref, mix_ref = refs[2 + nslot :]
    me = me_ref[0]
    ends = seq_ends(len_ref)

    @pl.loop(0, nslot)
    def _(b):
        rows = pl.ds(pl.multiple_of(b * tok, tok), tok)
        vt_ref[b] = v_ref[rows, :].astype(F32).T.astype(BF16)

    @pl.loop(0, nslot)
    def _(place):
        slot = place ^ me
        rows = slot_rows(place, me, tok)
        q4 = spread_heads(q_ref[rows, :], heads)
        pos = query_positions(place * tok, tok, heads)
        first = start_of(ends, pos)

        def tile(ki, state, masked):
            s = dot(k_ref[slot_rows(ki, me, tok), :], q4, 1, 1) * SCORE_SCALE
            if masked:
                s = hide(s, ki * tok, pos, first)
            top = jnp.max(s, 0, keepdims=True)
            vt = vt_ref[ki ^ me]
            if state is not None:
                m, l, acc = state
                top = jnp.maximum(top, m)
            p = jnp.exp2(s - top)
            add = jnp.sum(p, 0, keepdims=True)
            pb = p.astype(BF16)
            out = jnp.concatenate(
                [
                    dot(vt[h * HEAD_DIM : (h + 1) * HEAD_DIM], pb[:, h * tok : (h + 1) * tok])
                    for h in range(heads)
                ],
                axis=1,
            )
            if state is not None:
                fade = jnp.exp2(m - top)
                add = add + l * fade
                out = out + acc * fade
            return top, add, out

        begin, whole = key_range(ends, place, tok)
        state = tile(place, None, True)
        state = lax.fori_loop(begin, whole, lambda ki, st: tile(ki, st, True), state)
        m, l, acc = lax.fori_loop(
            jnp.maximum(whole, begin), place, lambda ki, st: tile(ki, st, False), state
        )
        o = fold_heads(acc / l, heads, tok)
        att_ref[rows, :] = o
        mix_ref[slot] = (o * scale_ref[...]).astype(BF16)
        lse_ref[slot] = m + jnp.log2(l)

    for s in range(nslot):
        mix_refs[s][...] = mix_ref[s]


def pair_blocks(qkv, pair):
    pairs = qkv.shape[1] // (3 * PAIR)
    return [pl.BlockSpec((ROW, PAIR), lambda t, c=j * pairs + pair: (0, c)) for j in range(3)]


def whole_spec(dims):
    return pl.BlockSpec(dims, lambda t: (0,) * len(dims))


def attend_forward(me, lengths, qkv, scale_lanes, tok, pair):
    nslot = ROW // tok
    lanes = PAIR // HEAD_DIM * tok
    made = [((ROW, PAIR), F32), ((nslot, 1, lanes), F32)] + [((tok, PAIR), BF16)] * nslot
    out = pl.pallas_call(
        functools.partial(forward_kernel, tok),
        grid=(1,),
        out_shape=[shape(*m) for m in made],
        in_specs=[SMEM_SPEC, SMEM_SPEC]
        + pair_blocks(qkv, pair)
        + [pl.BlockSpec((1, PAIR), lambda t: (0, pair))],
        out_specs=[whole_spec(m[0]) for m in made],
        scratch_shapes=[
            pltpu.VMEM((nslot, PAIR, tok), BF16),
            pltpu.VMEM((nslot, tok, PAIR), BF16),
        ],
        compiler_params=PARAMS,
        cost_estimate=cost(8),
        name="attend_forward",
    )(me, lengths, qkv, qkv, qkv, scale_lanes)
    return out[0], out[1], list(out[2:])


def end_of(ends, pos):
    last = jnp.full_like(pos, ROW)
    for e in ends:
        last = jnp.where(e > pos, jnp.minimum(last, e), last)
    return last


def backward_kernel(tok, turn, me_ref, len_ref, q_ref, k_ref, v_ref, lse_ref, *refs):
    nslot = ROW // tok
    width = q_ref.shape[1]
    heads = width // HEAD_DIM
    if turn == 0:
        att_ref, refs = refs[0], refs[1:]
    do_refs = refs[:nslot]
    if turn == 0:
        dkv_ref, sum_ref, dqt_ref, delta_ref = refs[nslot : nslot + 4]
    else:
        dkv_in, sum_in, dqt_in, delta_ref, dqkv_ref, sum_ref, dqt_ref = refs[nslot : nslot + 7]
    do_ref, q4_ref, do4_ref = refs[-3:]
    me = me_ref[0]
    ends = seq_ends(len_ref)
    for s in range(nslot):
        do_ref[s] = do_refs[s][...]
    if turn == 0:
        sum_ref[...] = jnp.zeros_like(sum_ref)
        dqt_ref[...] = jnp.zeros_like(dqt_ref)
    else:
        sum_ref[...] = sum_in[...]
        dqt_ref[...] = dqt_in[...]
    pick = lax.broadcasted_iota(jnp.int32, (8, width), 1) // HEAD_DIM
    pick = (pick == lax.broadcasted_iota(jnp.int32, (8, width), 0)).astype(F32)

    @pl.loop(0, nslot)
    def _(place):
        rows = slot_rows(place, me, tok)
        q4_ref[place] = spread_heads(q_ref[rows, :], heads)
        do = do_ref[place ^ me]
        do4_ref[place] = spread_heads(do, heads)
        if turn == 0:
            both = do.astype(F32) * att_ref[rows, :]
            sum_ref[:, 3 * width :] += jnp.sum(both, 0, keepdims=True)
            d = dot(pick, both, 1, 1, lax.Precision.HIGHEST)
            delta_ref[place] = jnp.concatenate([d[h : h + 1] for h in range(heads)], axis=1)

    @pl.loop(0, nslot // 2)
    def _(j):
        ki = 4 * (j // 2) + (3 * (j % 2) if turn == 0 else 1 + j % 2)
        rows = slot_rows(ki, me, tok)
        k = k_ref[rows, :]
        v = v_ref[rows, :]
        kt = k.astype(F32).T.astype(BF16)

        def tile(qi, state, masked):
            q4 = q4_ref[qi]
            do4 = do4_ref[qi]
            s = dot(k, q4, 1, 1) * SCORE_SCALE
            if masked:
                pos = query_positions(qi * tok, tok, heads)
                s = hide(s, ki * tok, pos, start_of(ends, pos))
            p = jnp.exp2(s - lse_ref[qi ^ me])
            dp = dot(v, do4, 1, 1)
            ds = (p * (dp - delta_ref[qi])).astype(BF16)
            dv = dot(p.astype(BF16), do4)
            dk = dot(ds, q4)
            dqt_ref[qi] += jnp.concatenate(
                [
                    dot(kt[h * HEAD_DIM : (h + 1) * HEAD_DIM], ds[:, h * tok : (h + 1) * tok])
                    for h in range(heads)
                ],
                axis=1,
            )
            if state is None:
                return dk, dv
            return state[0] + dk, state[1] + dv

        state = tile(ki, None, True)
        k0 = ki * tok
        upto = (end_of(ends, k0 + tok - 1) + tok - 1) // tok
        whole = jnp.clip(end_of(ends, k0) // tok, ki + 1, jnp.maximum(upto, ki + 1))
        state = lax.fori_loop(ki + 1, whole, lambda qi, st: tile(qi, st, False), state)
        dk, dv = lax.fori_loop(whole, upto, lambda qi, st: tile(qi, st, True), state)
        dk = (dk * HEAD_DIM**-0.5).astype(BF16)
        dv = dv.astype(BF16)
        if turn == 0:
            dkv_ref[j, :, :width] = dk
            dkv_ref[j, :, width:] = dv
        else:
            dqkv_ref[rows, width : 2 * width] = dk
            dqkv_ref[rows, 2 * width :] = dv
        sum_ref[:, width : 2 * width] += jnp.sum(dk.astype(F32), 0, keepdims=True)
        sum_ref[:, 2 * width : 3 * width] += jnp.sum(dv.astype(F32), 0, keepdims=True)

    if turn == 0:
        return

    @pl.loop(0, nslot // 2)
    def _(j):
        rows = slot_rows(4 * (j // 2) + 3 * (j % 2), me, tok)
        dqkv_ref[rows, width:] = dkv_in[j]

    @pl.loop(0, nslot)
    def _(place):
        dq = (fold_heads(dqt_ref[place], heads, tok) * HEAD_DIM**-0.5).astype(BF16)
        dqkv_ref[slot_rows(place, me, tok), :width] = dq
        sum_ref[:, :width] += jnp.sum(dq.astype(F32), 0, keepdims=True)


def attend_backward(me, lengths, qkv, att, lse, grads, tok, pair, turn, held=()):
    nslot = ROW // tok
    lanes = PAIR // HEAD_DIM * tok
    made = [((1, 4 * PAIR), F32), ((nslot, HEAD_DIM, lanes), F32)]
    if turn == 0:
        made = [((nslot // 2, tok, 2 * PAIR), BF16), *made, ((nslot, 1, lanes), F32)]
        first = [att]
    else:
        made = [((ROW, 3 * PAIR), BF16), *made]
        first = []
    return pl.pallas_call(
        functools.partial(backward_kernel, tok, turn),
        grid=(1,),
        out_shape=[shape(*m) for m in made],
        in_specs=[SMEM_SPEC, SMEM_SPEC]
        + pair_blocks(qkv, pair)
        + [whole_spec(v.shape) for v in (lse, *first)]
        + [pl.BlockSpec((tok, PAIR), lambda t: (0, pair))] * nslot
        + [whole_spec(v.shape) for v in held],
        out_specs=[whole_spec(m[0]) for m in made],
        scratch_shapes=[
            pltpu.VMEM((nslot, tok, PAIR), BF16),
            pltpu.VMEM((nslot, lanes, PAIR), BF16),
            pltpu.VMEM((nslot, lanes, PAIR), BF16),
        ],
        compiler_params=PARAMS,
        cost_estimate=cost(8),
        name="attend_backward",
    )(me, lengths, qkv, qkv, qkv, lse, *first, *grads, *held)


def centred(v):
    center = v - jnp.mean(v, -1, keepdims=True)
    inv = lax.rsqrt(jnp.mean(center * center, -1, keepdims=True) + EPSILON)
    return center * inv, inv


def norm_back(unit, inv, e):
    return inv * (e - jnp.mean(e, -1, keepdims=True) - unit * jnp.mean(e * unit, -1, keepdims=True))


def first_norm_kernel(x_ref, gain_ref, shift_ref, out_ref):
    unit, _ = centred(x_ref[...].astype(F32))
    out_ref[...] = (unit * gain_ref[...] + shift_ref[...]).astype(BF16)


def first_norm(x, gain, shift):
    return pl.pallas_call(
        first_norm_kernel,
        out_shape=shape(x.shape, BF16),
        in_specs=[VMEM_SPEC] * 3,
        out_specs=VMEM_SPEC,
        compiler_params=PARAMS,
        cost_estimate=cost(2),
        name="first_norm",
    )(x, gain, shift)


def qkv_kernel(n, *refs):
    slots = refs[:n]
    weights = refs[n : n + 3]
    bias_ref = refs[n + 3]
    out_ref = refs[-1]
    tok = slots[0].shape[0]
    width = weights[0].shape[1]
    for s in range(n):
        for j in range(3):
            cols = slice(j * width, (j + 1) * width)
            made = dot(slots[s][...], weights[j][...]) + bias_ref[:, cols]
            out_ref[s * tok : (s + 1) * tok, cols] = made.astype(BF16)


def qkv_part(slots, weights, bias, part, earlier=None):
    n = len(slots)
    tok = slots[0].shape[0]
    width = weights[0].shape[1]
    args = [*slots, *weights, bias]
    specs = [VMEM_SPEC] * len(args)
    aliases = {}
    if earlier is not None:
        aliases = {len(args): 0}
        args.append(earlier)
        specs.append(pl.BlockSpec(memory_space=pl.ANY))
    return pl.pallas_call(
        functools.partial(qkv_kernel, n),
        grid=(1,),
        out_shape=shape((ROW, 3 * width), BF16),
        in_specs=specs,
        out_specs=pl.BlockSpec((n * tok, 3 * width), lambda t: (part, 0)),
        input_output_aliases=aliases,
        compiler_params=PARAMS,
        cost_estimate=cost(3),
        name="qkv_part",
    )(*args)


def join_lanes(refs):
    return jnp.concatenate([r[...] for r in refs], axis=1) if len(refs) > 1 else refs[0][...]


def after_attention_kernel(n, pairs, *refs):
    mixed = refs[: n * pairs]
    weights = refs[n * pairs : n * pairs + n]
    vectors = refs[n * pairs + n :]
    tok_ref, bias_ref, gain2_ref, shift2_ref, gain3_ref, shift3_ref = vectors[:6]
    branch_ref, residual_ref, ffn_ref = vectors[6:]
    branch = bias_ref[...]
    for s in range(n):
        branch = branch + dot(join_lanes(mixed[s * pairs : (s + 1) * pairs]), weights[s][...])
    branch_ref[...] = branch
    unit, _ = centred(branch)
    residual = tok_ref[...].astype(F32) + (unit * gain2_ref[...] + shift2_ref[...])
    residual_ref[...] = residual
    unit, _ = centred(residual)
    ffn_ref[...] = (unit * gain3_ref[...] + shift3_ref[...]).astype(BF16)


class Window:
    def __init__(self, array, first, rows):
        self.array, self.first, self.shape = array, first, (rows, array.shape[1])
        self.ndim = 2


def array_of(v):
    return v.array if isinstance(v, Window) else v


def row_tiles(rows, cols, tile):
    return pl.BlockSpec((tile, cols), lambda t: (t, 0))


def fixed(array):
    if isinstance(array, Window):
        at = array.first // array.shape[0]
        return pl.BlockSpec(array.shape, lambda *_: (at, 0))
    return pl.BlockSpec(array.shape, lambda *_: (0,) * array.ndim)


def after_attention(mixed, weights, tokens, *vectors, tile=256):
    rows, d = tokens.shape
    tile = min(tile, rows)
    n, pairs = len(mixed), len(mixed[0])
    mixed = [v for slot in mixed for v in slot]
    wide = row_tiles(rows, d, tile)
    return pl.pallas_call(
        functools.partial(after_attention_kernel, n, pairs),
        grid=(rows // tile,),
        in_specs=[row_tiles(rows, PAIR, tile)] * (n * pairs)
        + [fixed(w) for w in weights]
        + [wide]
        + [fixed(v) for v in vectors],
        out_specs=(wide, wide, wide),
        out_shape=(shape((rows, d), F32), shape((rows, d), F32), shape((rows, d), BF16)),
        compiler_params=PARAMS,
        cost_estimate=cost(3),
        name="after_attention",
    )(*mixed, *map(array_of, weights), tokens, *vectors)


def before_attention_kernel(n, adds, *refs):
    came = refs[:adds]
    residual_ref, branch_ref, cot_ref, gain3_ref, gain2_ref, scale_ref = refs[adds : adds + 6]
    weights = refs[adds + 6 : adds + 6 + n]
    outs = refs[adds + 6 + n :]
    grad_ref, low_ref, sum_ref = outs[:3]
    pieces = outs[3:]
    c = came[0][...].astype(F32)
    for r in came[1:]:
        c = c + r[...].astype(F32)
    unit3, inv3 = centred(residual_ref[...])
    cot = cot_ref[...].astype(F32)
    grad = cot + norm_back(unit3, inv3, c * gain3_ref[...])
    grad_ref[...] = grad
    unit2, inv2 = centred(branch_ref[...])
    low = norm_back(unit2, inv2, grad * gain2_ref[...]).astype(BF16)
    low_ref[...] = low

    @pl.when(pl.program_id(0) == 0)
    def _():
        sum_ref[...] = jnp.zeros_like(sum_ref)

    tops = [grad * unit2, grad, c * unit3, c, low.astype(F32), cot]
    sums = [jnp.sum(v, 0, keepdims=True) for v in tops]
    sum_ref[...] += jnp.concatenate(sums + [jnp.zeros_like(sums[0])] * 2, axis=0)
    width = pieces[0].shape[1]
    for s in range(n):
        made = dot(low, weights[s][...], 1, 1) * scale_ref[:, s * width : (s + 1) * width]
        pieces[s][...] = made.astype(BF16)


def before_attention(came, residual, branch, cot, gain3, gain2, scale_slots, weights, tile=256):
    rows, d = residual.shape
    width = weights[0].shape[0]
    tile = min(tile, rows)
    n = len(weights)
    wide = row_tiles(rows, d, tile)
    vectors = [gain3, gain2, scale_slots]
    out = pl.pallas_call(
        functools.partial(before_attention_kernel, n, len(came)),
        grid=(rows // tile,),
        in_specs=[wide] * (len(came) + 3)
        + [fixed(v) for v in vectors]
        + [fixed(w) for w in weights],
        out_specs=(wide, wide, pl.BlockSpec((8, d), lambda t: (0, 0)))
        + (row_tiles(rows, width, tile),) * n,
        out_shape=(shape((rows, d), F32), shape((rows, d), BF16), shape((8, d), F32))
        + (shape((rows, width), BF16),) * n,
        compiler_params=PARAMS,
        cost_estimate=cost(3),
        name="before_attention",
    )(*came, residual, branch, cot, *vectors, *map(array_of, weights))
    return out[0], out[1], out[2], list(out[3:])


def last_norm_kernel(adds, *refs):
    came = refs[:adds]
    x_ref, grad_ref, gain_ref, out_ref = refs[adds:]
    c = came[0][...].astype(F32)
    for r in came[1:]:
        c = c + r[...].astype(F32)
    unit, inv = centred(x_ref[...].astype(F32))
    out_ref[...] = grad_ref[...] + norm_back(unit, inv, c * gain_ref[...])


def last_norm(came, x, grad, gain, tile=256):
    rows, d = x.shape
    tile = min(tile, rows)
    wide = row_tiles(rows, d, tile)
    return pl.pallas_call(
        functools.partial(last_norm_kernel, len(came)),
        grid=(rows // tile,),
        in_specs=[wide] * (len(came) + 2) + [fixed(gain)],
        out_specs=wide,
        out_shape=shape((rows, d), F32),
        compiler_params=PARAMS,
        cost_estimate=cost(2),
        name="last_norm",
    )(*came, x, grad, gain)


def gelu_parts(u):
    k = math.sqrt(2 / math.pi)
    square = u * u
    t = jnp.tanh(u * (k + (k * 0.044715) * square))
    return 0.5 + 0.5 * t, t, square


def pick_piece(refs, places):
    step = pl.program_id(0)
    out = refs[0][...]
    for ref, (first, _, _) in zip(refs[1:], places[1:]):
        out = jnp.where(step >= first, ref[...], out)
    return out


def places_of(pieces, tile):
    places, at = [], 0
    for v in pieces:
        first = v.first // tile if isinstance(v, Window) else 0
        places.append((at, v.shape[0] // tile, first))
        at += v.shape[0] // tile
    return tuple(places)


def piece_tiles(places, tile, cols):
    return [
        pl.BlockSpec((tile, cols), lambda t, f=f, c=c, a=a: (jnp.clip(t - f, 0, c - 1) + a, 0))
        for f, c, a in places
    ]


def hidden_gradient_kernel(cp, *refs):
    refs[-1][...] = dot(pick_piece(refs[: len(cp)], cp), refs[-2][...], 1, 1)


def hidden_gradient(cots, w2, tile=256):
    units, d = w2.shape
    tile = min(tile, *(v.shape[0] for v in cots))
    cp = places_of(cots, tile)
    rows = sum(v.shape[0] for v in cots)
    return pl.pallas_call(
        functools.partial(hidden_gradient_kernel, cp),
        grid=(rows // tile,),
        in_specs=piece_tiles(cp, tile, d) + [fixed(w2)],
        out_specs=row_tiles(rows, units, tile),
        out_shape=shape((rows, units), F32),
        compiler_params=PARAMS,
        cost_estimate=cost(3),
        name="hidden_gradient",
    )(*map(array_of, cots), w2)


def ffn_first_kernel(xp, *refs):
    n = len(xp)
    hg_ref, w1_ref, b1_ref, gain_ref, u_ref, stat_ref = refs[n:]
    units = u_ref.shape[1]
    u = dot(pick_piece(refs[: len(xp)], xp), w1_ref[...]) + b1_ref[...]
    u_ref[...] = u
    half, _, _ = gelu_parts(u)
    a = u * half
    total = jnp.sum(a, 1, keepdims=True)
    d = a - total * (1.0 / units)
    sg = hg_ref[...] * gain_ref[...]
    cols = [
        total,
        jnp.sum(d * d, 1, keepdims=True),
        jnp.sum(sg, 1, keepdims=True),
        jnp.sum(sg * d, 1, keepdims=True),
    ]
    lane = lax.broadcasted_iota(jnp.int32, (u.shape[0], 128), 1)
    wide = jnp.zeros(lane.shape, F32)
    for j, col in enumerate(cols):
        wide = jnp.where(lane == j, col, wide)
    stat_ref[...] = wide.T[:8]


def ffn_first(xs, hg, w1, b1, gain, tile=256):
    d, units = w1.shape
    tile = min(tile, *(v.shape[0] for v in xs))
    xp = places_of(xs, tile)
    rows = sum(v.shape[0] for v in xs)
    return pl.pallas_call(
        functools.partial(ffn_first_kernel, xp),
        grid=(rows // tile,),
        in_specs=piece_tiles(xp, tile, d)
        + [row_tiles(rows, units, tile)]
        + [fixed(v) for v in (w1, b1, gain)],
        out_specs=(row_tiles(rows, units, tile), pl.BlockSpec((8, tile), lambda t: (0, t))),
        out_shape=(shape((rows, units), F32), shape((8, rows), F32)),
        compiler_params=PARAMS,
        cost_estimate=cost(5),
        name="ffn_first",
    )(*xs, hg, w1, b1, gain)


def ffn_second_kernel(ndev, n, per, *refs):
    u_ref, hg_ref, gain_ref, shift_ref, w1_ref = refs[:5]
    stats = [r[...] for r in refs[5 : 5 + ndev]]
    hid_ref, fg_ref, sum_ref = refs[-3 - n : -n]
    backs = refs[-n:]
    units = u_ref.shape[1]
    mean = sum(s[0:1] for s in stats) * (1.0 / FF)
    spread = jnp.zeros_like(mean)
    total = jnp.zeros_like(mean)
    cross = jnp.zeros_like(mean)
    for s in stats:
        gap = s[0:1] * (1.0 / units) - mean
        spread += s[1:2] + units * (gap * gap)
        total += s[2:3]
        cross += s[3:4] + gap * s[2:3]
    inv = lax.rsqrt(spread * (1.0 / FF) + EPSILON)
    packed = [mean, inv, total * (1.0 / FF), cross * inv * (1.0 / FF)]
    packed = jnp.concatenate(packed + [jnp.zeros_like(mean)] * 4, axis=0).T
    mean, inv, total, cross = (packed[:, j : j + 1] for j in range(4))
    u = u_ref[...]
    hg = hg_ref[...]
    half, t, square = gelu_parts(u)
    unit = (u * half - mean) * inv
    gain = gain_ref[...]
    hid_ref[...] = (unit * gain + shift_ref[...]).astype(BF16)
    k = math.sqrt(2 / math.pi)
    slope = half + (0.5 * u) * ((1.0 - t * t) * (k + (3 * k * 0.044715) * square))
    fg = (inv * (hg * gain - total - unit * cross) * slope).astype(BF16)
    fg_ref[...] = fg
    back = dot(fg, w1_ref[...], 1, 1).astype(BF16)
    step = pl.program_id(0) // per
    for s in range(n):

        @pl.when(step == s)
        def _(s=s):
            backs[s][...] = back

    @pl.when(pl.program_id(0) == 0)
    def _():
        sum_ref[...] = jnp.zeros_like(sum_ref)

    sums = [jnp.sum(v, 0, keepdims=True) for v in (hg * unit, hg, fg.astype(F32))]
    sum_ref[...] += jnp.concatenate(sums + [jnp.zeros((5, units), F32)], axis=0)


def ffn_second(u, hg, gain, shift, w1, stats, tok, part, earlier=None, tile=256):
    rows, units = u.shape
    d = w1.shape[0]
    tile = min(tile, tok)
    per = tok // tile
    ndev = len(stats)
    n = rows // tok
    skip = part * n * per

    def stat_place(s):
        return lambda t: (0, (((t + skip) // per) ^ s) * per + t % per)

    in_specs = [row_tiles(rows, units, tile)] * 2 + [fixed(v) for v in (gain, shift, w1)]
    in_specs += [pl.BlockSpec((8, tile), stat_place(s)) for s in range(ndev)]
    args = [u, hg, gain, shift, w1, *stats]
    aliases = {}
    if earlier is not None:
        in_specs += [pl.BlockSpec(memory_space=pl.ANY)] * 2
        aliases = {len(args): 0, len(args) + 1: 1}
        args += list(earlier)
    moved = pl.BlockSpec((tile, units), lambda t: (t + skip, 0))
    out = pl.pallas_call(
        functools.partial(ffn_second_kernel, ndev, n, per),
        grid=(rows // tile,),
        in_specs=in_specs,
        out_specs=(moved, moved, pl.BlockSpec((8, units), lambda t: (0, 0)))
        + tuple(piece_tiles([(s * per, per, 0) for s in range(n)], tile, d)),
        out_shape=(shape((ROW, units), BF16), shape((ROW, units), BF16), shape((8, units), F32))
        + (shape((tok, d), BF16),) * n,
        input_output_aliases=aliases,
        compiler_params=PARAMS,
        cost_estimate=cost(5),
        name="ffn_second",
    )(*args)
    return out[0], out[1], out[2], list(out[3:])


def products_kernel(nx, nw, flip, groups, *refs):
    xs, ws, outs = refs[:nx], refs[nx : nx + nw], refs[nx + nw :]
    cols = xs[0].shape[1] // nw
    tok = xs[0].shape[0] // sum(len(g) for g in groups)
    for group, out in zip(groups, outs):
        for at, s in enumerate(group):
            total = None
            for j, w in enumerate(ws):
                left = [x[s * tok : (s + 1) * tok, j * cols : (j + 1) * cols] for x in xs]
                left = jnp.concatenate(left, axis=1) if nx > 1 else left[0]
                made = dot(left, w[...], 1, 1 if flip else 0)
                total = made if total is None else total + made
            out[at * tok : (at + 1) * tok, :] = total.astype(BF16)


def products(xs, weights, flip, tok, first, groups, us=2):
    n = sum(len(g) for g in groups)
    d = weights[0].shape[0 if flip else 1]
    out = pl.pallas_call(
        functools.partial(products_kernel, len(xs), len(weights), flip, groups),
        grid=(1,),
        in_specs=[pl.BlockSpec((n * tok, x.shape[1]), lambda t: (first // n, 0)) for x in xs]
        + [fixed(w) for w in weights],
        out_specs=[whole_spec((len(g) * tok, d)) for g in groups],
        out_shape=[shape((len(g) * tok, d), BF16) for g in groups],
        compiler_params=PARAMS,
        cost_estimate=cost(us),
        name="products",
    )(*xs, *weights)
    return list(out)


def head_gradient_kernel(n, pairs, groups, *refs):
    left = refs[n * pairs][...]
    d = left.shape[1]
    for group, out in zip(groups, refs[n * pairs + 1 :]):
        for at, s in enumerate(group):
            made = dot(left, join_lanes(refs[s * pairs : (s + 1) * pairs]), 0, 0)
            out[at * d : (at + 1) * d, :] = made.astype(BF16)


def head_gradient(mixed, low, groups):
    n, pairs = len(mixed), len(mixed[0])
    d = low.shape[1]
    mixed = [v for slot in mixed for v in slot]
    return list(
        pl.pallas_call(
            functools.partial(head_gradient_kernel, n, pairs, groups),
            out_shape=[shape((len(g) * d, pairs * PAIR), BF16) for g in groups],
            in_specs=[VMEM_SPEC] * (n * pairs + 1),
            out_specs=[VMEM_SPEC] * len(groups),
            compiler_params=PARAMS,
            cost_estimate=cost(2),
            name="head_gradient",
        )(*mixed, low)
    )


def gradient_kernel(steps, nl, nr, nj, extra, me_ref, *refs):
    del me_ref
    joins, refs = refs[:nj], refs[nj:]
    lefts, rights = refs[:nl], refs[nl : nl + nr]
    send_ref, keep_ref = refs[nl + nr + extra : nl + nr + extra + 2]
    step = pl.program_id(0)
    pieces = rights if nr > 1 else lefts
    total = None
    at = 0
    for s, piece in enumerate(pieces):
        rows = slice(at, at + piece.shape[0])
        at += piece.shape[0]
        left = lefts[s][...] if nl > 1 else lefts[0][rows, :]
        right = rights[s][...] if nr > 1 else rights[0][rows, :]
        made = dot(left, right, 0, 0)
        total = made if total is None else total + made

    made = total.astype(BF16)
    if nj:
        more = joins[0][...].astype(F32)
        for r in joins[1:]:
            more = more + r[...].astype(F32)
        made = jnp.concatenate([made, more.astype(BF16)], axis=1)

    @pl.when(step < steps // 2)
    def _():
        send_ref[...] = made

    @pl.when(step >= steps // 2)
    def _():
        keep_ref[...] = made

    if extra:
        weights = refs[nl + nr : nl + nr + extra - 1]
        sum_ref = refs[nl + nr + extra - 1]
        width = weights[0].shape[1]
        cross = jnp.zeros((total.shape[0], width), F32)
        plain = cross
        for j, w_ref in enumerate(weights):
            cols = slice(j * width, (j + 1) * width)
            w = w_ref[...].astype(F32)
            cross += w * total[:, cols]
            plain += w * sum_ref[:, cols]
        cross = jnp.sum(cross, 1, keepdims=True)
        plain = jnp.sum(plain, 1, keepdims=True)
        lane = lax.broadcasted_iota(jnp.int32, (total.shape[0], 128), 1)
        wide = jnp.where(lane == 0, cross, jnp.where(lane == 1, plain, 0.0))
        refs[-1][...] = wide.T[:8]


def gradient(side, lefts, rights, weights=(), pair=0, sums=None, joins=(), steps=4):
    m = lefts[0].shape[1]
    steps = min(steps, m // 128)
    size = m // steps
    n = rights[0].shape[1]
    nl, nr = len(lefts), len(rights)
    n += joins[0].shape[1] if joins else 0
    extra = len(weights) + 1 if weights else 0

    def chunk_of(t, side):
        return (t + (1 - side[0]) * (steps // 2)) % steps

    def join_spec(v):
        at = v.first // size if isinstance(v, Window) else 0
        return pl.BlockSpec((size, v.shape[1]), lambda t, me: (chunk_of(t, me) + at, 0))

    in_specs = [join_spec(v) for v in joins]
    in_specs += [pl.BlockSpec((v.shape[0], size), lambda t, me: (0, chunk_of(t, me))) for v in lefts]
    in_specs += [fixed(v) for v in rights]
    in_specs += [pl.BlockSpec((size, PAIR), lambda t, me: (chunk_of(t, me), pair)) for w in weights]
    out_specs = [
        pl.BlockSpec((size, n), lambda t, me: (jnp.minimum(t, steps // 2 - 1), 0)),
        pl.BlockSpec((size, n), lambda t, me: (jnp.maximum(t - steps // 2, 0), 0)),
    ]
    out_shape = [shape((m // 2, n), BF16)] * 2
    args = [side, *map(array_of, joins), *lefts, *map(array_of, rights), *weights]
    if extra:
        args.append(sums)
        in_specs.append(pl.BlockSpec(sums.shape, lambda t, me: (0, 0)))
        out_specs.append(pl.BlockSpec((8, size), lambda t, me: (0, chunk_of(t, me))))
        out_shape.append(shape((8, m), F32))
    return pl.pallas_call(
        functools.partial(gradient_kernel, steps, nl, nr, len(joins), extra),
        grid_spec=pltpu.PrefetchScalarGridSpec(
            num_scalar_prefetch=1, grid=(steps,), in_specs=in_specs, out_specs=out_specs
        ),
        out_shape=out_shape,
        compiler_params=PARAMS,
        cost_estimate=cost(4),
        name="gradient",
    )(*args)


def assemble_kernel(nx, cols, turned, side_ref, *refs):
    mine, came, outs = refs[:nx], refs[nx : 2 * nx], refs[2 * nx :]
    size = mine[0].shape[0]
    side = side_ref[0]
    n = len(outs) - (1 if turned else 0)
    for x in range(nx):
        for ref, first in ((mine[x], side * size), (came[x], (1 - side) * size)):
            first = pl.multiple_of(first, size)
            for j in range(n):
                made = ref[:, j * cols : (j + 1) * cols].astype(F32)
                outs[j][pl.ds(first, size), x * cols : (x + 1) * cols] = made
            if x == 0 and turned:
                outs[n][:, pl.ds(first, size)] = ref[:, n * cols :].astype(F32).T


def assemble(side, mine, came, cols, turned=0):
    size = mine[0].shape[0]
    n = (mine[0].shape[1] - turned) // cols
    out = [shape((2 * size, cols * len(mine)), F32)] * n
    if turned:
        out = out + [shape((turned, 2 * size), F32)]
    return pl.pallas_call(
        functools.partial(assemble_kernel, len(mine), cols, turned),
        out_shape=out,
        in_specs=[SMEM_SPEC] + [VMEM_SPEC] * (2 * len(mine)),
        out_specs=[VMEM_SPEC] * len(out),
        compiler_params=PARAMS,
        cost_estimate=cost(0),
        name="assemble",
    )(side, *mine, *came)


def swap(value, axis, size, bit):
    return lax.ppermute(value, axis, [(i, i ^ bit) for i in range(size)])


def bits_of(size):
    return [1 << b for b in range(size.bit_length() - 1)]


def after(value, *others):
    return lax.optimization_barrier((value, *others))[0]


def spread_low(slots, axis, size, bits):
    slots = dict(slots)
    for bit in bits:
        slots.update({s | bit: swap(v, axis, size, bit) for s, v in slots.items()})
    return slots


def add_low(left, right):
    return (left.astype(F32) + right.astype(F32)).astype(BF16)


def direct_slots(value, axis, size):
    return [value] + [swap(value, axis, size, s) for s in range(1, size)]


class Scatter:
    def __init__(self, size):
        self.size = size
        self.low = bits_of(size)[:-1]
        self.top = size // 2

    def within(self, parts):
        held = {s: [v] for s, v in parts.items()}
        for bit in self.low:
            for s in sorted(held, reverse=True):
                if s & bit:
                    terms = held.pop(s)
                    total = terms[0]
                    for t in terms[1:]:
                        total = add_low(total, t)
                    held[s ^ bit].append(swap(total, "mp", self.size, bit))
        [(_, terms)] = held.items()
        return terms

    def across(self, terms):
        total = terms[0].astype(F32)
        for t in terms[1:]:
            total = total + t.astype(F32)
        total = total.astype(BF16)
        return total, swap(total, "mp", self.size, self.top)


class Stream:
    def __init__(self, dp, bits, send, keep):
        self.dp = dp
        self.index = lax.axis_index("dp")
        self.bits = bits
        self.stage = 0
        self.held = keep
        self.came = swap(send, "dp", dp, bits[0])

    def advance(self, *tie):
        n = len(self.bits)
        if self.stage == 2 * n - 1:
            return self.held
        held, came = after(self.held, *tie), after(self.came, *tie)
        self.stage += 1
        if self.stage <= n:
            cur = add_low(held, came)
            if self.stage == n:
                self.held = send = cur
                bit = self.bits[-1]
            else:
                bit = self.bits[self.stage]
                upper = (self.index & bit) != 0
                low, high = cur[: cur.shape[0] // 2], cur[cur.shape[0] // 2 :]
                send = jnp.where(upper, low, high)
                self.held = jnp.where(upper, high, low)
        else:
            upper = (self.index & self.bits[2 * n - self.stage]) != 0
            low, high = jnp.where(upper, came, held), jnp.where(upper, held, came)
            self.held = send = jnp.concatenate([low, high])
            bit = self.bits[2 * n - self.stage - 1]
        self.came = swap(send, "dp", self.dp, bit)
        return send

    def done(self, *tie):
        while self.stage < 2 * len(self.bits) - 1:
            self.advance(*tie)
        return self


class Direct:
    def __init__(self, dp, send, keep):
        self.dp = dp
        self.index = lax.axis_index("dp")
        self.held = keep
        self.came = swap(send, "dp", dp, 1)
        self.stage = 0

    def others(self, parts):
        return [parts[0]] + [swap(v, "dp", self.dp, 2 * j) for j, v in enumerate(parts) if j]

    def ordered(self, parts):
        bit = 2
        step = 1
        while step < len(parts):
            upper = (self.index & bit) != 0
            parts = [jnp.where(upper, parts[j ^ step], v) for j, v in enumerate(parts)]
            bit, step = 2 * bit, 2 * step
        return parts

    def advance(self, *tie):
        n = self.dp // 2
        self.stage += 1
        if self.stage == 1:
            total = add_low(after(self.held, *tie), after(self.came, *tie))
            size = total.shape[0] // n
            parts = self.ordered([total[j * size : (j + 1) * size] for j in range(n)])
            self.parts = self.others(parts)
            return parts[0]
        if self.stage == 2:
            total = sum(after(v, *tie).astype(F32) for v in self.parts).astype(BF16)
            self.parts = self.others([total] * n)
            return total
        if self.stage == 3:
            parts = [after(v, *tie) for v in self.parts]
            self.held = jnp.concatenate(self.ordered(parts))
            self.came = swap(self.held, "dp", self.dp, 1)
        return self.held

    def done(self, *tie):
        while self.stage < 3:
            self.advance(*tie)
        return self


def on_device(
    dp,
    mp,
    tokens,
    lengths,
    norm1_gain,
    norm1_shift,
    query_weight,
    query_bias,
    key_weight,
    value_weight,
    value_bias,
    head_scale,
    output_weight,
    output_bias,
    norm2_gain,
    norm2_shift,
    norm3_gain,
    norm3_shift,
    fc1_weight,
    fc1_bias,
    mid_gain,
    mid_shift,
    fc2_weight,
    fc2_bias,
    out_grad,
):
    tok, d = tokens.shape
    width = query_weight.shape[1]
    heads = width // HEAD_DIM
    pairs = width // PAIR
    half = mp // 2
    units = fc1_weight.shape[1]
    me = lax.axis_index("mp").astype(jnp.int32)
    me_arr = me[None]
    index = lax.axis_index("dp").astype(jnp.int32)
    plain = bits_of(dp)
    turned = [plain[1], plain[0], *plain[2:]]
    side, side_turned = (index & 1)[None], ((index >> 1) & 1)[None]
    lower = list(reversed(bits_of(mp)[:-1]))
    scatter = Scatter(mp)
    one_by_one = [[s] for s in range(half)]
    merged = [[0], [2], [1, 3]] if mp == 4 else [[s] for s in range(mp)]

    def merged_terms(outs, rows):
        if mp != 4:
            return scatter.within(dict(enumerate(outs[:half]))), scatter.within(
                {half + j: v for j, v in enumerate(outs[half:])}
            )
        came = swap(outs[2], "mp", mp, 1)
        return [outs[0], Window(came, 0, rows)], [outs[1], Window(came, rows, rows)]

    def plain_rows(v):
        return v.array[v.first : v.first + v.shape[0]] if isinstance(v, Window) else v

    def wide_swap(v):
        return swap(v, "mp", mp, half)

    def listed(near, far):
        slots = {**near, **far}
        return [slots[s] for s in range(mp)]

    def row(v):
        return v[None]

    qkv_weights = (query_weight, key_weight, value_weight)
    bias_qkv = jnp.concatenate([query_bias, jnp.zeros_like(query_bias), value_bias])[None]
    scale_lanes = jnp.repeat(head_scale, HEAD_DIM)[None]
    place = me * tok + lax.broadcasted_iota(jnp.int32, (tok, 1), 0)
    cot_low = jnp.where(place < jnp.sum(lengths), out_grad, jnp.zeros_like(out_grad))

    normed_own = first_norm(tokens, row(norm1_gain), row(norm1_shift))
    normed_far = wide_swap(normed_own)
    normed_near = spread_low({0: normed_own}, "mp", mp, lower)
    start = normed_near[half - 1]
    qkv = qkv_part([normed_near[s] for s in range(half)], qkv_weights, bias_qkv, 0)
    cot_low, output_weight = (after(v, start) for v in (cot_low, output_weight))
    cot_near = spread_low({0: cot_low}, "mp", mp, lower)
    out_near = spread_low({0: output_weight}, "mp", mp, lower)
    both = jnp.concatenate([cot_low, output_weight])
    hg_near = hidden_gradient([after(cot_near[s], qkv) for s in range(half)], fc2_weight)
    normed_far = after(normed_far, hg_near, both, out_near[half - 1])
    both_far = wide_swap(after(both, normed_far))
    normed_far = spread_low({half: normed_far}, "mp", mp, lower)
    qkv = qkv_part([normed_far[half + s] for s in range(half)], qkv_weights, bias_qkv, 1, qkv)
    normed = listed(normed_near, normed_far)

    far_first = [*range(half, mp), *range(1, half)]
    atts, lses, mixed = [], [], [[] for _ in range(mp)]
    mark = (qkv,)
    for p in range(pairs):
        att, lse, mix = attend_forward(me_arr, lengths, after(qkv, *mark), scale_lanes, tok, p)
        atts.append(att)
        lses.append(lse)
        if p > 0:
            mix = [after(v, *(m[-1] for m in mixed[1:])) for v in mix]
        mixed[0].append(mix[0])
        for s in far_first:
            mixed[s].append(swap(mix[s], "mp", mp, s))
        mark = (mix[0],)
    both_far = spread_low({half: after(both_far, mix[0])}, "mp", mp, lower)
    cot_far = {s: Window(v, 0, tok) for s, v in both_far.items()}
    out_far = {s: Window(v, tok, width) for s, v in both_far.items()}
    out_rows = listed(out_near, out_far)
    branch, residual, ffn_own = after_attention(
        mixed,
        out_rows,
        tokens,
        *(row(v) for v in (output_bias, norm2_gain, norm2_shift, norm3_gain, norm3_shift)),
    )

    ffn_far = wide_swap(ffn_own)
    ffn_near = spread_low({0: ffn_own}, "mp", mp, lower)
    scale_slots = direct_slots(after(scale_lanes, ffn_own), "mp", mp)
    cots, ffn_near = listed(cot_near, cot_far), [ffn_near[s] for s in range(half)]
    ffn_args = (fc1_weight, row(fc1_bias), row(mid_gain))
    u_near, st_near = ffn_first(ffn_near, hg_near, *ffn_args)
    cot_ready = Window(after(cots[half].array, st_near), 0, tok)
    hg_far = hidden_gradient([cot_ready, *cots[half + 1 :]], fc2_weight)
    ffn_far = spread_low({half: after(ffn_far, hg_far)}, "mp", mp, lower)
    ffn_in = ffn_near + [ffn_far[half + s] for s in range(half)]
    ffn_args = (fc1_weight, after(row(fc1_bias), *scale_slots[1:]), row(mid_gain))
    u_far, st_far = ffn_first(ffn_in[half:], hg_far, *ffn_args)
    stats = direct_slots(jnp.concatenate([st_near, st_far], axis=1), "mp", mp)
    ffn_args = (row(mid_gain), row(mid_shift), fc1_weight, stats, tok)
    hid, fg, mid_far, back_far = ffn_second(u_far, hg_far, *ffn_args, 1)
    back_far = scatter.within({half + j: v for j, v in enumerate(back_far)})
    hid, fg, mid_near, back_near = ffn_second(u_near, hg_near, *ffn_args, 0, (hid, fg))
    scale_slots = jnp.concatenate(scale_slots, axis=1)
    back_far[1:] = [after(v, mid_near) for v in back_far[1:]]
    back_sum, back_far = scatter.across(back_far)
    back_near = scatter.within(dict(enumerate(back_near)))

    send, keep = gradient(side, [after(hid, back_sum)], cots)
    fc2 = Stream(dp, plain, send, keep)
    send, keep = gradient(side_turned, ffn_in, [after(fg, send)])
    fc1 = Stream(dp, turned, send, keep)
    came = [after(v, send) for v in (*back_near, back_far)]
    residual_grad, branch_low, sums, grads = before_attention(
        came, residual, branch, cot_low, row(norm3_gain), row(norm2_gain), scale_slots, out_rows
    )

    do = {s: swap(grads[s], "mp", mp, s) for s in far_first}
    do = [grads[0]] + [do[s] for s in range(1, mp)]
    mark = fc2.advance(branch_low)
    low = after(branch_low, mark, *do[1:half])
    g_near_terms, g_far_terms = merged_terms(head_gradient(mixed, low, merged), d)
    outs = products([after(hid, g_near_terms[0])], [fc2_weight], False, tok, half, one_by_one)
    out_far_terms = scatter.within({half + j: v for j, v in enumerate(outs)})
    mark = fc1.advance(outs[0])
    do[half:] = [after(v, mark) for v in do[half:]]
    mark = do[-1]
    g_far_terms = [after(plain_rows(v), mark) for v in g_far_terms]
    g_out_sum, g_out_top = scatter.across(g_far_terms)
    mark = fc2.advance(g_out_sum)

    dqkvs, sums_att, rows, streams = [], [], [], []

    def between(call):
        nonlocal mark
        nonlocal out_top
        if call == 0:
            mark = fc2.advance(mark)
            mark = fc1.advance(mark)
            out_sum, out_top = scatter.across([after(v, mark) for v in out_far_terms])
            mark = out_sum
        elif call == 1:
            mark = fc2.advance(after(mark, g_out_top))
        elif call == 2:
            mark = fc1.advance(mark)
            mark = fc2.advance(mark)
            for stream in streams:
                mark = stream.advance(mark)

    call, out_top = 0, None
    for p in range(pairs):
        held = ()
        for turn in range(2):
            held = attend_backward(
                me_arr, lengths, after(qkv, mark), atts[p], lses[p], do, tok, p, turn, held
            )
            mark = held[0]
            between(call)
            call += 1
        dqkv, sum_att, _ = held
        dqkvs.append(dqkv)
        sums_att.append(sum_att)
        if p < pairs - 1:
            joins = [*g_near_terms, g_out_top] if p == 0 else ()
            send, keep, r = gradient(
                side, normed, [after(dqkv, mark)], qkv_weights, p, sum_att, joins
            )
            rows.append(r)
            streams.append(Stream(dp, plain, send, keep))
            mark = fc1.advance(send)

    mark = after(mark, out_top)
    for stream in streams:
        mark = stream.advance(mark)
    joins = [*g_near_terms, g_out_top] if pairs == 1 else ()
    send, keep, r = gradient(
        side, normed, [after(dqkvs[-1], mark)], qkv_weights, pairs - 1, sums_att[-1], joins
    )
    rows.append(r)
    last = Direct(dp, send, keep)
    mark = send
    for stream in streams:
        mark = stream.advance(mark)
    packed = jnp.concatenate([sums[:6], sum(rows)[:2]])
    packed = jnp.broadcast_to(after(packed, mark)[None], (mp, *packed.shape))
    sent = packed
    packed = lax.all_to_all(packed, "mp", 0, 0)
    far = products([after(v, sent) for v in dqkvs], qkv_weights, True, tok, half, one_by_one)
    far_terms = scatter.within({half + j: v for j, v in enumerate(far)})
    mark = far[0]
    for stream in streams:
        mark = stream.advance(mark)
    near = products([after(v, mark) for v in dqkvs], qkv_weights, True, tok, 0, one_by_one)
    far_terms[1:] = [after(v, near[0]) for v in far_terms[1:]]
    far_sum, far_top = scatter.across(far_terms)
    near_terms = scatter.within(dict(enumerate(near)))
    mark = last.advance(far_sum)
    fc2.done(mark)
    [grad_fc2_weight] = assemble(side, [after(fc2.held, mark)], [fc2.came], fc2.held.shape[1])
    mark = fc1.advance(grad_fc2_weight)
    for stream in streams:
        mark = stream.advance(mark)
    mark = last.advance(mark)
    packed = after(packed, mark).sum(0)
    mids = jnp.pad(mid_near + mid_far, ((0, 0), (0, d - units)))[:4]
    heads_sums = jnp.concatenate(sums_att, axis=1)
    heads_sums = jnp.pad(heads_sums, ((0, 3), (0, d - heads_sums.shape[1])))
    packed = jnp.concatenate([packed, mids, heads_sums])
    packed = jnp.broadcast_to(packed[None], (dp, *packed.shape))
    sent = packed
    packed = lax.all_to_all(packed, "dp", 0, 0)
    mark = last.advance(sent)
    outs = products([after(hid, mark)], [fc2_weight], False, tok, 0, one_by_one, 0)
    out_near_terms = scatter.within(dict(enumerate(outs)))
    token_grad = last_norm(
        [*near_terms, after(far_top, outs[0], *(v.came for v in streams))], tokens, residual_grad, row(norm1_gain)
    )
    output = residual + row(fc2_bias)
    for t in (*out_near_terms, out_top):
        output = output + after(t, token_grad).astype(F32)
    output = output.astype(BF16)
    packed = after(packed, output).sum(0)
    fc1.done(output)
    for stream in (*streams, last):
        stream.done(output)
    streams.append(last)
    grad_query_weight, grad_key_weight, grad_value_weight, grad_output_weight = assemble(
        side, [after(v.held, packed) for v in streams], [v.came for v in streams], PAIR, width
    )
    [grad_fc1_weight] = assemble(
        side_turned, [after(fc1.held, grad_query_weight)], [fc1.came], fc1.held.shape[1]
    )
    shift1 = packed[7]
    gain1 = (packed[6] - norm1_shift * shift1) / norm1_gain
    per_head = packed[12, : 4 * width].reshape(pairs, 4, PAIR)
    return (
        output,
        token_grad,
        gain1,
        shift1,
        grad_query_weight,
        per_head[:, 0].reshape(width),
        grad_key_weight,
        grad_value_weight,
        per_head[:, 2].reshape(width),
        jnp.sum(per_head[:, 3].reshape(heads, HEAD_DIM), 1) / head_scale,
        grad_output_weight,
        packed[4],
        packed[0],
        packed[1],
        packed[2],
        packed[3],
        grad_fc1_weight,
        packed[10, :units],
        packed[8, :units],
        packed[9, :units],
        grad_fc2_weight,
        packed[5],
    )


def solution(mesh):
    own = P(("dp", "mp"), None)
    cols, rows, vec, same = P(None, "mp"), P("mp", None), P("mp"), P()
    ends = (cols, vec, vec, vec, rows, same)
    norms = (same,) * 5
    in_specs = (own, P("dp", None), same, same, cols, vec, cols, cols, vec, vec, rows, *norms, *ends, own)
    out_specs = (own, own, same, same, cols, vec, cols, cols, vec, vec, rows, *norms, *ends)
    return jax.shard_map(
        functools.partial(on_device, mesh.shape["dp"], mesh.shape["mp"]),
        mesh=mesh,
        in_specs=in_specs,
        out_specs=out_specs,
        check_vma=False,
    )
```

```python
import functools
import math

import jax
import jax.numpy as jnp
from jax import lax
from jax.experimental import pallas as pl
from jax.experimental.pallas import tpu as pltpu
from jax.sharding import PartitionSpec as P

HEAD_DIM = 64
FF = 4096
ROW = 2048
PAIR = 2 * HEAD_DIM
EPSILON = 1e-05
MASKED = -1000000000.0
LOG2E = math.log2(math.e)
SCORE_SCALE = LOG2E * HEAD_DIM**-0.5
SMEM_SPEC = pl.BlockSpec(memory_space=pltpu.SMEM)
VMEM_SPEC = pl.BlockSpec(memory_space=pltpu.VMEM)
BF16 = jnp.bfloat16
F32 = jnp.float32
PARAMS = pltpu.CompilerParams(vmem_limit_bytes=56 * 2**20)


def shape(dims, dtype):
    return jax.ShapeDtypeStruct(dims, dtype)


def cost(us):
    return pl.CostEstimate(flops=int(us * 1e10), bytes_accessed=int(us * 3.6e7), transcendentals=0)


def dot(a, b, ca=1, cb=0, precision=None):
    return lax.dot_general(
        a, b, (((ca,), (cb,)), ((), ())), preferred_element_type=F32, precision=precision
    )


def spread_heads(block, heads):
    lane = lax.broadcasted_iota(jnp.int32, (1, block.shape[1]), 1) // HEAD_DIM
    zero = jnp.zeros_like(block)
    return jnp.concatenate([jnp.where(lane == h, block, zero) for h in range(heads)], axis=0)


def seq_ends(len_ref):
    ends = []
    total = jnp.int32(0)
    for j in range(len_ref.shape[-1]):
        total = total + len_ref[0, j]
        ends.append(total)
    return ends


def start_of(ends, pos):
    first = jnp.zeros_like(pos)
    for e in ends:
        first = jnp.maximum(first, jnp.where(e <= pos, e, 0))
    return first


def query_positions(q0, tok, heads):
    lane = lax.broadcasted_iota(jnp.int32, (1, tok), 1) + q0
    return jnp.concatenate([lane] * heads, axis=1)


def hide(scores, k0, pos, first):
    key = lax.broadcasted_iota(jnp.int32, scores.shape, 0) + k0
    return jnp.where((key >= first) & (key <= pos), scores, MASKED)


def slot_rows(place, me, tok):
    return pl.ds(pl.multiple_of((place ^ me) * tok, tok), tok)


def fold_heads(side, heads, tok):
    return jnp.concatenate([side[:, h * tok : (h + 1) * tok] for h in range(heads)], axis=0).T


def key_range(ends, place, tok):
    begin = start_of(ends, place * tok) // tok
    whole = (start_of(ends, place * tok + tok - 1) + tok - 1) // tok
    return begin, jnp.minimum(whole, place)


def forward_kernel(tok, me_ref, len_ref, q_ref, k_ref, v_ref, scale_ref, *refs):
    nslot = ROW // tok
    width = q_ref.shape[1]
    heads = width // HEAD_DIM
    att_ref, lse_ref = refs[:2]
    mix_refs = refs[2 : 2 + nslot]
    vt_ref, mix_ref = refs[2 + nslot :]
    me = me_ref[0]
    ends = seq_ends(len_ref)

    @pl.loop(0, nslot)
    def _(b):
        rows = pl.ds(pl.multiple_of(b * tok, tok), tok)
        vt_ref[b] = v_ref[rows, :].astype(F32).T.astype(BF16)

    @pl.loop(0, nslot)
    def _(place):
        slot = place ^ me
        rows = slot_rows(place, me, tok)
        q4 = spread_heads(q_ref[rows, :], heads)
        pos = query_positions(place * tok, tok, heads)
        first = start_of(ends, pos)

        def tile(ki, state, masked):
            s = dot(k_ref[slot_rows(ki, me, tok), :], q4, 1, 1) * SCORE_SCALE
            if masked:
                s = hide(s, ki * tok, pos, first)
            top = jnp.max(s, 0, keepdims=True)
            vt = vt_ref[ki ^ me]
            if state is not None:
                m, l, acc = state
                top = jnp.maximum(top, m)
            p = jnp.exp2(s - top)
            add = jnp.sum(p, 0, keepdims=True)
            pb = p.astype(BF16)
            out = jnp.concatenate(
                [
                    dot(vt[h * HEAD_DIM : (h + 1) * HEAD_DIM], pb[:, h * tok : (h + 1) * tok])
                    for h in range(heads)
                ],
                axis=1,
            )
            if state is not None:
                fade = jnp.exp2(m - top)
                add = add + l * fade
                out = out + acc * fade
            return top, add, out

        begin, whole = key_range(ends, place, tok)
        state = tile(place, None, True)
        state = lax.fori_loop(begin, whole, lambda ki, st: tile(ki, st, True), state)
        m, l, acc = lax.fori_loop(
            jnp.maximum(whole, begin), place, lambda ki, st: tile(ki, st, False), state
        )
        o = fold_heads(acc / l, heads, tok)
        att_ref[rows, :] = o
        mix_ref[slot] = (o * scale_ref[...]).astype(BF16)
        lse_ref[slot] = m + jnp.log2(l)

    for s in range(nslot):
        mix_refs[s][...] = mix_ref[s]


def pair_blocks(qkv, pair):
    pairs = qkv.shape[1] // (3 * PAIR)
    return [pl.BlockSpec((ROW, PAIR), lambda t, c=j * pairs + pair: (0, c)) for j in range(3)]


def whole_spec(dims):
    return pl.BlockSpec(dims, lambda t: (0,) * len(dims))


def attend_forward(me, lengths, qkv, scale_lanes, tok, pair):
    nslot = ROW // tok
    lanes = PAIR // HEAD_DIM * tok
    made = [((ROW, PAIR), F32), ((nslot, 1, lanes), F32)] + [((tok, PAIR), BF16)] * nslot
    out = pl.pallas_call(
        functools.partial(forward_kernel, tok),
        grid=(1,),
        out_shape=[shape(*m) for m in made],
        in_specs=[SMEM_SPEC, SMEM_SPEC]
        + pair_blocks(qkv, pair)
        + [pl.BlockSpec((1, PAIR), lambda t: (0, pair))],
        out_specs=[whole_spec(m[0]) for m in made],
        scratch_shapes=[
            pltpu.VMEM((nslot, PAIR, tok), BF16),
            pltpu.VMEM((nslot, tok, PAIR), BF16),
        ],
        compiler_params=PARAMS,
        cost_estimate=cost(8),
        name="attend_forward",
    )(me, lengths, qkv, qkv, qkv, scale_lanes)
    return out[0], out[1], list(out[2:])


def end_of(ends, pos):
    last = jnp.full_like(pos, ROW)
    for e in ends:
        last = jnp.where(e > pos, jnp.minimum(last, e), last)
    return last


def backward_kernel(tok, turn, me_ref, len_ref, q_ref, k_ref, v_ref, lse_ref, *refs):
    nslot = ROW // tok
    width = q_ref.shape[1]
    heads = width // HEAD_DIM
    if turn == 0:
        att_ref, refs = refs[0], refs[1:]
    do_refs = refs[:nslot]
    if turn == 0:
        dkv_ref, sum_ref, dqt_ref, delta_ref = refs[nslot : nslot + 4]
    else:
        dkv_in, sum_in, dqt_in, delta_ref, dqkv_ref, sum_ref, dqt_ref = refs[nslot : nslot + 7]
    do_ref, q4_ref, do4_ref = refs[-3:]
    me = me_ref[0]
    ends = seq_ends(len_ref)
    for s in range(nslot):
        do_ref[s] = do_refs[s][...]
    if turn == 0:
        sum_ref[...] = jnp.zeros_like(sum_ref)
        dqt_ref[...] = jnp.zeros_like(dqt_ref)
    else:
        sum_ref[...] = sum_in[...]
        dqt_ref[...] = dqt_in[...]
    pick = lax.broadcasted_iota(jnp.int32, (8, width), 1) // HEAD_DIM
    pick = (pick == lax.broadcasted_iota(jnp.int32, (8, width), 0)).astype(F32)

    @pl.loop(0, nslot)
    def _(place):
        rows = slot_rows(place, me, tok)
        q4_ref[place] = spread_heads(q_ref[rows, :], heads)
        do = do_ref[place ^ me]
        do4_ref[place] = spread_heads(do, heads)
        if turn == 0:
            both = do.astype(F32) * att_ref[rows, :]
            sum_ref[:, 3 * width :] += jnp.sum(both, 0, keepdims=True)
            d = dot(pick, both, 1, 1, lax.Precision.HIGHEST)
            delta_ref[place] = jnp.concatenate([d[h : h + 1] for h in range(heads)], axis=1)

    @pl.loop(0, nslot // 2)
    def _(j):
        ki = 4 * (j // 2) + (3 * (j % 2) if turn == 0 else 1 + j % 2)
        rows = slot_rows(ki, me, tok)
        k = k_ref[rows, :]
        v = v_ref[rows, :]
        kt = k.astype(F32).T.astype(BF16)

        def tile(qi, state, masked):
            q4 = q4_ref[qi]
            do4 = do4_ref[qi]
            s = dot(k, q4, 1, 1) * SCORE_SCALE
            if masked:
                pos = query_positions(qi * tok, tok, heads)
                s = hide(s, ki * tok, pos, start_of(ends, pos))
            p = jnp.exp2(s - lse_ref[qi ^ me])
            dp = dot(v, do4, 1, 1)
            ds = (p * (dp - delta_ref[qi])).astype(BF16)
            dv = dot(p.astype(BF16), do4)
            dk = dot(ds, q4)
            dqt_ref[qi] += jnp.concatenate(
                [
                    dot(kt[h * HEAD_DIM : (h + 1) * HEAD_DIM], ds[:, h * tok : (h + 1) * tok])
                    for h in range(heads)
                ],
                axis=1,
            )
            if state is None:
                return dk, dv
            return state[0] + dk, state[1] + dv

        state = tile(ki, None, True)
        k0 = ki * tok
        upto = (end_of(ends, k0 + tok - 1) + tok - 1) // tok
        whole = jnp.clip(end_of(ends, k0) // tok, ki + 1, jnp.maximum(upto, ki + 1))
        state = lax.fori_loop(ki + 1, whole, lambda qi, st: tile(qi, st, False), state)
        dk, dv = lax.fori_loop(whole, upto, lambda qi, st: tile(qi, st, True), state)
        dk = (dk * HEAD_DIM**-0.5).astype(BF16)
        dv = dv.astype(BF16)
        if turn == 0:
            dkv_ref[j, :, :width] = dk
            dkv_ref[j, :, width:] = dv
        else:
            dqkv_ref[rows, width : 2 * width] = dk
            dqkv_ref[rows, 2 * width :] = dv
        sum_ref[:, width : 2 * width] += jnp.sum(dk.astype(F32), 0, keepdims=True)
        sum_ref[:, 2 * width : 3 * width] += jnp.sum(dv.astype(F32), 0, keepdims=True)

    if turn == 0:
        return

    @pl.loop(0, nslot // 2)
    def _(j):
        rows = slot_rows(4 * (j // 2) + 3 * (j % 2), me, tok)
        dqkv_ref[rows, width:] = dkv_in[j]

    @pl.loop(0, nslot)
    def _(place):
        dq = (fold_heads(dqt_ref[place], heads, tok) * HEAD_DIM**-0.5).astype(BF16)
        dqkv_ref[slot_rows(place, me, tok), :width] = dq
        sum_ref[:, :width] += jnp.sum(dq.astype(F32), 0, keepdims=True)


def attend_backward(me, lengths, qkv, att, lse, grads, tok, pair, turn, held=()):
    nslot = ROW // tok
    lanes = PAIR // HEAD_DIM * tok
    made = [((1, 4 * PAIR), F32), ((nslot, HEAD_DIM, lanes), F32)]
    if turn == 0:
        made = [((nslot // 2, tok, 2 * PAIR), BF16), *made, ((nslot, 1, lanes), F32)]
        first = [att]
    else:
        made = [((ROW, 3 * PAIR), BF16), *made]
        first = []
    return pl.pallas_call(
        functools.partial(backward_kernel, tok, turn),
        grid=(1,),
        out_shape=[shape(*m) for m in made],
        in_specs=[SMEM_SPEC, SMEM_SPEC]
        + pair_blocks(qkv, pair)
        + [whole_spec(v.shape) for v in (lse, *first)]
        + [pl.BlockSpec((tok, PAIR), lambda t: (0, pair))] * nslot
        + [whole_spec(v.shape) for v in held],
        out_specs=[whole_spec(m[0]) for m in made],
        scratch_shapes=[
            pltpu.VMEM((nslot, tok, PAIR), BF16),
            pltpu.VMEM((nslot, lanes, PAIR), BF16),
            pltpu.VMEM((nslot, lanes, PAIR), BF16),
        ],
        compiler_params=PARAMS,
        cost_estimate=cost(8),
        name="attend_backward",
    )(me, lengths, qkv, qkv, qkv, lse, *first, *grads, *held)


def centred(v):
    center = v - jnp.mean(v, -1, keepdims=True)
    inv = lax.rsqrt(jnp.mean(center * center, -1, keepdims=True) + EPSILON)
    return center * inv, inv


def norm_back(unit, inv, e):
    return inv * (e - jnp.mean(e, -1, keepdims=True) - unit * jnp.mean(e * unit, -1, keepdims=True))


def first_norm_kernel(x_ref, gain_ref, shift_ref, out_ref):
    unit, _ = centred(x_ref[...].astype(F32))
    out_ref[...] = (unit * gain_ref[...] + shift_ref[...]).astype(BF16)


def first_norm(x, gain, shift):
    return pl.pallas_call(
        first_norm_kernel,
        out_shape=shape(x.shape, BF16),
        in_specs=[VMEM_SPEC] * 3,
        out_specs=VMEM_SPEC,
        compiler_params=PARAMS,
        cost_estimate=cost(2),
        name="first_norm",
    )(x, gain, shift)


def qkv_kernel(n, *refs):
    slots = refs[:n]
    weights = refs[n : n + 3]
    bias_ref = refs[n + 3]
    out_ref = refs[-1]
    tok = slots[0].shape[0]
    width = weights[0].shape[1]
    for s in range(n):
        for j in range(3):
            cols = slice(j * width, (j + 1) * width)
            made = dot(slots[s][...], weights[j][...]) + bias_ref[:, cols]
            out_ref[s * tok : (s + 1) * tok, cols] = made.astype(BF16)


def qkv_part(slots, weights, bias, part, earlier=None):
    n = len(slots)
    tok = slots[0].shape[0]
    width = weights[0].shape[1]
    args = [*slots, *weights, bias]
    specs = [VMEM_SPEC] * len(args)
    aliases = {}
    if earlier is not None:
        aliases = {len(args): 0}
        args.append(earlier)
        specs.append(pl.BlockSpec(memory_space=pl.ANY))
    return pl.pallas_call(
        functools.partial(qkv_kernel, n),
        grid=(1,),
        out_shape=shape((ROW, 3 * width), BF16),
        in_specs=specs,
        out_specs=pl.BlockSpec((n * tok, 3 * width), lambda t: (part, 0)),
        input_output_aliases=aliases,
        compiler_params=PARAMS,
        cost_estimate=cost(3),
        name="qkv_part",
    )(*args)


def join_lanes(refs):
    return jnp.concatenate([r[...] for r in refs], axis=1) if len(refs) > 1 else refs[0][...]


def after_attention_kernel(n, pairs, *refs):
    mixed = refs[: n * pairs]
    weights = refs[n * pairs : n * pairs + n]
    vectors = refs[n * pairs + n :]
    tok_ref, bias_ref, gain2_ref, shift2_ref, gain3_ref, shift3_ref = vectors[:6]
    branch_ref, residual_ref, ffn_ref = vectors[6:]
    branch = bias_ref[...]
    for s in range(n):
        branch = branch + dot(join_lanes(mixed[s * pairs : (s + 1) * pairs]), weights[s][...])
    branch_ref[...] = branch
    unit, _ = centred(branch)
    residual = tok_ref[...].astype(F32) + (unit * gain2_ref[...] + shift2_ref[...])
    residual_ref[...] = residual
    unit, _ = centred(residual)
    ffn_ref[...] = (unit * gain3_ref[...] + shift3_ref[...]).astype(BF16)


class Window:
    def __init__(self, array, first, rows):
        self.array, self.first, self.shape = array, first, (rows, array.shape[1])
        self.ndim = 2


def array_of(v):
    return v.array if isinstance(v, Window) else v


def row_tiles(rows, cols, tile):
    return pl.BlockSpec((tile, cols), lambda t: (t, 0))


def fixed(array):
    if isinstance(array, Window):
        at = array.first // array.shape[0]
        return pl.BlockSpec(array.shape, lambda *_: (at, 0))
    return pl.BlockSpec(array.shape, lambda *_: (0,) * array.ndim)


def after_attention(mixed, weights, tokens, *vectors, tile=256):
    rows, d = tokens.shape
    tile = min(tile, rows)
    n, pairs = len(mixed), len(mixed[0])
    mixed = [v for slot in mixed for v in slot]
    wide = row_tiles(rows, d, tile)
    return pl.pallas_call(
        functools.partial(after_attention_kernel, n, pairs),
        grid=(rows // tile,),
        in_specs=[row_tiles(rows, PAIR, tile)] * (n * pairs)
        + [fixed(w) for w in weights]
        + [wide]
        + [fixed(v) for v in vectors],
        out_specs=(wide, wide, wide),
        out_shape=(shape((rows, d), F32), shape((rows, d), F32), shape((rows, d), BF16)),
        compiler_params=PARAMS,
        cost_estimate=cost(3),
        name="after_attention",
    )(*mixed, *map(array_of, weights), tokens, *vectors)


def before_attention_kernel(n, adds, *refs):
    came = refs[:adds]
    residual_ref, branch_ref, cot_ref, gain3_ref, gain2_ref, scale_ref = refs[adds : adds + 6]
    weights = refs[adds + 6 : adds + 6 + n]
    outs = refs[adds + 6 + n :]
    grad_ref, low_ref, sum_ref = outs[:3]
    pieces = outs[3:]
    c = came[0][...].astype(F32)
    for r in came[1:]:
        c = c + r[...].astype(F32)
    unit3, inv3 = centred(residual_ref[...])
    cot = cot_ref[...].astype(F32)
    grad = cot + norm_back(unit3, inv3, c * gain3_ref[...])
    grad_ref[...] = grad
    unit2, inv2 = centred(branch_ref[...])
    low = norm_back(unit2, inv2, grad * gain2_ref[...]).astype(BF16)
    low_ref[...] = low

    @pl.when(pl.program_id(0) == 0)
    def _():
        sum_ref[...] = jnp.zeros_like(sum_ref)

    tops = [grad * unit2, grad, c * unit3, c, low.astype(F32), cot]
    sums = [jnp.sum(v, 0, keepdims=True) for v in tops]
    sum_ref[...] += jnp.concatenate(sums + [jnp.zeros_like(sums[0])] * 2, axis=0)
    width = pieces[0].shape[1]
    for s in range(n):
        made = dot(low, weights[s][...], 1, 1) * scale_ref[:, s * width : (s + 1) * width]
        pieces[s][...] = made.astype(BF16)


def before_attention(came, residual, branch, cot, gain3, gain2, scale_slots, weights, tile=256):
    rows, d = residual.shape
    width = weights[0].shape[0]
    tile = min(tile, rows)
    n = len(weights)
    wide = row_tiles(rows, d, tile)
    vectors = [gain3, gain2, scale_slots]
    out = pl.pallas_call(
        functools.partial(before_attention_kernel, n, len(came)),
        grid=(rows // tile,),
        in_specs=[wide] * (len(came) + 3)
        + [fixed(v) for v in vectors]
        + [fixed(w) for w in weights],
        out_specs=(wide, wide, pl.BlockSpec((8, d), lambda t: (0, 0)))
        + (row_tiles(rows, width, tile),) * n,
        out_shape=(shape((rows, d), F32), shape((rows, d), BF16), shape((8, d), F32))
        + (shape((rows, width), BF16),) * n,
        compiler_params=PARAMS,
        cost_estimate=cost(3),
        name="before_attention",
    )(*came, residual, branch, cot, *vectors, *map(array_of, weights))
    return out[0], out[1], out[2], list(out[3:])


def last_norm_kernel(adds, *refs):
    came = refs[:adds]
    x_ref, grad_ref, gain_ref, out_ref = refs[adds:]
    c = came[0][...].astype(F32)
    for r in came[1:]:
        c = c + r[...].astype(F32)
    unit, inv = centred(x_ref[...].astype(F32))
    out_ref[...] = grad_ref[...] + norm_back(unit, inv, c * gain_ref[...])


def last_norm(came, x, grad, gain, tile=256):
    rows, d = x.shape
    tile = min(tile, rows)
    wide = row_tiles(rows, d, tile)
    return pl.pallas_call(
        functools.partial(last_norm_kernel, len(came)),
        grid=(rows // tile,),
        in_specs=[wide] * (len(came) + 2) + [fixed(gain)],
        out_specs=wide,
        out_shape=shape((rows, d), F32),
        compiler_params=PARAMS,
        cost_estimate=cost(2),
        name="last_norm",
    )(*came, x, grad, gain)


def gelu_parts(u):
    k = math.sqrt(2 / math.pi)
    square = u * u
    t = jnp.tanh(u * (k + (k * 0.044715) * square))
    return 0.5 + 0.5 * t, t, square


def pick_piece(refs, places):
    step = pl.program_id(0)
    out = refs[0][...]
    for ref, (first, _, _) in zip(refs[1:], places[1:]):
        out = jnp.where(step >= first, ref[...], out)
    return out


def places_of(pieces, tile):
    places, at = [], 0
    for v in pieces:
        first = v.first // tile if isinstance(v, Window) else 0
        places.append((at, v.shape[0] // tile, first))
        at += v.shape[0] // tile
    return tuple(places)


def piece_tiles(places, tile, cols):
    return [
        pl.BlockSpec((tile, cols), lambda t, f=f, c=c, a=a: (jnp.clip(t - f, 0, c - 1) + a, 0))
        for f, c, a in places
    ]


def hidden_gradient_kernel(cp, *refs):
    refs[-1][...] = dot(pick_piece(refs[: len(cp)], cp), refs[-2][...], 1, 1)


def hidden_gradient(cots, w2, tile=256):
    units, d = w2.shape
    tile = min(tile, *(v.shape[0] for v in cots))
    cp = places_of(cots, tile)
    rows = sum(v.shape[0] for v in cots)
    return pl.pallas_call(
        functools.partial(hidden_gradient_kernel, cp),
        grid=(rows // tile,),
        in_specs=piece_tiles(cp, tile, d) + [fixed(w2)],
        out_specs=row_tiles(rows, units, tile),
        out_shape=shape((rows, units), F32),
        compiler_params=PARAMS,
        cost_estimate=cost(3),
        name="hidden_gradient",
    )(*map(array_of, cots), w2)


def ffn_first_kernel(xp, *refs):
    n = len(xp)
    hg_ref, w1_ref, b1_ref, gain_ref, u_ref, stat_ref = refs[n:]
    units = u_ref.shape[1]
    u = dot(pick_piece(refs[: len(xp)], xp), w1_ref[...]) + b1_ref[...]
    u_ref[...] = u
    half, _, _ = gelu_parts(u)
    a = u * half
    total = jnp.sum(a, 1, keepdims=True)
    d = a - total * (1.0 / units)
    sg = hg_ref[...] * gain_ref[...]
    cols = [
        total,
        jnp.sum(d * d, 1, keepdims=True),
        jnp.sum(sg, 1, keepdims=True),
        jnp.sum(sg * d, 1, keepdims=True),
    ]
    lane = lax.broadcasted_iota(jnp.int32, (u.shape[0], 128), 1)
    wide = jnp.zeros(lane.shape, F32)
    for j, col in enumerate(cols):
        wide = jnp.where(lane == j, col, wide)
    stat_ref[...] = wide.T[:8]


def ffn_first(xs, hg, w1, b1, gain, tile=256):
    d, units = w1.shape
    tile = min(tile, *(v.shape[0] for v in xs))
    xp = places_of(xs, tile)
    rows = sum(v.shape[0] for v in xs)
    return pl.pallas_call(
        functools.partial(ffn_first_kernel, xp),
        grid=(rows // tile,),
        in_specs=piece_tiles(xp, tile, d)
        + [row_tiles(rows, units, tile)]
        + [fixed(v) for v in (w1, b1, gain)],
        out_specs=(row_tiles(rows, units, tile), pl.BlockSpec((8, tile), lambda t: (0, t))),
        out_shape=(shape((rows, units), F32), shape((8, rows), F32)),
        compiler_params=PARAMS,
        cost_estimate=cost(5),
        name="ffn_first",
    )(*xs, hg, w1, b1, gain)


def ffn_second_kernel(ndev, n, per, *refs):
    u_ref, hg_ref, gain_ref, shift_ref, w1_ref = refs[:5]
    stats = [r[...] for r in refs[5 : 5 + ndev]]
    hid_ref, fg_ref, sum_ref = refs[-3 - n : -n]
    backs = refs[-n:]
    units = u_ref.shape[1]
    mean = sum(s[0:1] for s in stats) * (1.0 / FF)
    spread = jnp.zeros_like(mean)
    total = jnp.zeros_like(mean)
    cross = jnp.zeros_like(mean)
    for s in stats:
        gap = s[0:1] * (1.0 / units) - mean
        spread += s[1:2] + units * (gap * gap)
        total += s[2:3]
        cross += s[3:4] + gap * s[2:3]
    inv = lax.rsqrt(spread * (1.0 / FF) + EPSILON)
    packed = [mean, inv, total * (1.0 / FF), cross * inv * (1.0 / FF)]
    packed = jnp.concatenate(packed + [jnp.zeros_like(mean)] * 4, axis=0).T
    mean, inv, total, cross = (packed[:, j : j + 1] for j in range(4))
    u = u_ref[...]
    hg = hg_ref[...]
    half, t, square = gelu_parts(u)
    unit = (u * half - mean) * inv
    gain = gain_ref[...]
    hid_ref[...] = (unit * gain + shift_ref[...]).astype(BF16)
    k = math.sqrt(2 / math.pi)
    slope = half + (0.5 * u) * ((1.0 - t * t) * (k + (3 * k * 0.044715) * square))
    fg = (inv * (hg * gain - total - unit * cross) * slope).astype(BF16)
    fg_ref[...] = fg
    back = dot(fg, w1_ref[...], 1, 1).astype(BF16)
    step = pl.program_id(0) // per
    for s in range(n):

        @pl.when(step == s)
        def _(s=s):
            backs[s][...] = back

    @pl.when(pl.program_id(0) == 0)
    def _():
        sum_ref[...] = jnp.zeros_like(sum_ref)

    sums = [jnp.sum(v, 0, keepdims=True) for v in (hg * unit, hg, fg.astype(F32))]
    sum_ref[...] += jnp.concatenate(sums + [jnp.zeros((5, units), F32)], axis=0)


def ffn_second(u, hg, gain, shift, w1, stats, tok, part, earlier=None, tile=256):
    rows, units = u.shape
    d = w1.shape[0]
    tile = min(tile, tok)
    per = tok // tile
    ndev = len(stats)
    n = rows // tok
    skip = part * n * per

    def stat_place(s):
        return lambda t: (0, (((t + skip) // per) ^ s) * per + t % per)

    in_specs = [row_tiles(rows, units, tile)] * 2 + [fixed(v) for v in (gain, shift, w1)]
    in_specs += [pl.BlockSpec((8, tile), stat_place(s)) for s in range(ndev)]
    args = [u, hg, gain, shift, w1, *stats]
    aliases = {}
    if earlier is not None:
        in_specs += [pl.BlockSpec(memory_space=pl.ANY)] * 2
        aliases = {len(args): 0, len(args) + 1: 1}
        args += list(earlier)
    moved = pl.BlockSpec((tile, units), lambda t: (t + skip, 0))
    out = pl.pallas_call(
        functools.partial(ffn_second_kernel, ndev, n, per),
        grid=(rows // tile,),
        in_specs=in_specs,
        out_specs=(moved, moved, pl.BlockSpec((8, units), lambda t: (0, 0)))
        + tuple(piece_tiles([(s * per, per, 0) for s in range(n)], tile, d)),
        out_shape=(shape((ROW, units), BF16), shape((ROW, units), BF16), shape((8, units), F32))
        + (shape((tok, d), BF16),) * n,
        input_output_aliases=aliases,
        compiler_params=PARAMS,
        cost_estimate=cost(5),
        name="ffn_second",
    )(*args)
    return out[0], out[1], out[2], list(out[3:])


def products_kernel(nx, nw, flip, groups, *refs):
    xs, ws, outs = refs[:nx], refs[nx : nx + nw], refs[nx + nw :]
    cols = xs[0].shape[1] // nw
    tok = xs[0].shape[0] // sum(len(g) for g in groups)
    for group, out in zip(groups, outs):
        for at, s in enumerate(group):
            total = None
            for j, w in enumerate(ws):
                left = [x[s * tok : (s + 1) * tok, j * cols : (j + 1) * cols] for x in xs]
                left = jnp.concatenate(left, axis=1) if nx > 1 else left[0]
                made = dot(left, w[...], 1, 1 if flip else 0)
                total = made if total is None else total + made
            out[at * tok : (at + 1) * tok, :] = total.astype(BF16)


def products(xs, weights, flip, tok, first, groups, us=2):
    n = sum(len(g) for g in groups)
    d = weights[0].shape[0 if flip else 1]
    out = pl.pallas_call(
        functools.partial(products_kernel, len(xs), len(weights), flip, groups),
        grid=(1,),
        in_specs=[pl.BlockSpec((n * tok, x.shape[1]), lambda t: (first // n, 0)) for x in xs]
        + [fixed(w) for w in weights],
        out_specs=[whole_spec((len(g) * tok, d)) for g in groups],
        out_shape=[shape((len(g) * tok, d), BF16) for g in groups],
        compiler_params=PARAMS,
        cost_estimate=cost(us),
        name="products",
    )(*xs, *weights)
    return list(out)


def head_gradient_kernel(n, pairs, groups, *refs):
    left = refs[n * pairs][...]
    d = left.shape[1]
    for group, out in zip(groups, refs[n * pairs + 1 :]):
        for at, s in enumerate(group):
            made = dot(left, join_lanes(refs[s * pairs : (s + 1) * pairs]), 0, 0)
            out[at * d : (at + 1) * d, :] = made.astype(BF16)


def head_gradient(mixed, low, groups):
    n, pairs = len(mixed), len(mixed[0])
    d = low.shape[1]
    mixed = [v for slot in mixed for v in slot]
    return list(
        pl.pallas_call(
            functools.partial(head_gradient_kernel, n, pairs, groups),
            out_shape=[shape((len(g) * d, pairs * PAIR), BF16) for g in groups],
            in_specs=[VMEM_SPEC] * (n * pairs + 1),
            out_specs=[VMEM_SPEC] * len(groups),
            compiler_params=PARAMS,
            cost_estimate=cost(2),
            name="head_gradient",
        )(*mixed, low)
    )


def gradient_kernel(steps, nl, nr, nj, extra, me_ref, *refs):
    del me_ref
    joins, refs = refs[:nj], refs[nj:]
    lefts, rights = refs[:nl], refs[nl : nl + nr]
    send_ref, keep_ref = refs[nl + nr + extra : nl + nr + extra + 2]
    step = pl.program_id(0)
    pieces = rights if nr > 1 else lefts
    total = None
    at = 0
    for s, piece in enumerate(pieces):
        rows = slice(at, at + piece.shape[0])
        at += piece.shape[0]
        left = lefts[s][...] if nl > 1 else lefts[0][rows, :]
        right = rights[s][...] if nr > 1 else rights[0][rows, :]
        made = dot(left, right, 0, 0)
        total = made if total is None else total + made

    made = total.astype(BF16)
    if nj:
        more = joins[0][...].astype(F32)
        for r in joins[1:]:
            more = more + r[...].astype(F32)
        made = jnp.concatenate([made, more.astype(BF16)], axis=1)

    @pl.when(step < steps // 2)
    def _():
        send_ref[...] = made

    @pl.when(step >= steps // 2)
    def _():
        keep_ref[...] = made

    if extra:
        weights = refs[nl + nr : nl + nr + extra - 1]
        sum_ref = refs[nl + nr + extra - 1]
        width = weights[0].shape[1]
        cross = jnp.zeros((total.shape[0], width), F32)
        plain = cross
        for j, w_ref in enumerate(weights):
            cols = slice(j * width, (j + 1) * width)
            w = w_ref[...].astype(F32)
            cross += w * total[:, cols]
            plain += w * sum_ref[:, cols]
        cross = jnp.sum(cross, 1, keepdims=True)
        plain = jnp.sum(plain, 1, keepdims=True)
        lane = lax.broadcasted_iota(jnp.int32, (total.shape[0], 128), 1)
        wide = jnp.where(lane == 0, cross, jnp.where(lane == 1, plain, 0.0))
        refs[-1][...] = wide.T[:8]


def gradient(side, lefts, rights, weights=(), pair=0, sums=None, joins=(), steps=4):
    m = lefts[0].shape[1]
    steps = min(steps, m // 128)
    size = m // steps
    n = rights[0].shape[1]
    nl, nr = len(lefts), len(rights)
    n += joins[0].shape[1] if joins else 0
    extra = len(weights) + 1 if weights else 0

    def chunk_of(t, side):
        return (t + (1 - side[0]) * (steps // 2)) % steps

    def join_spec(v):
        at = v.first // size if isinstance(v, Window) else 0
        return pl.BlockSpec((size, v.shape[1]), lambda t, me: (chunk_of(t, me) + at, 0))

    in_specs = [join_spec(v) for v in joins]
    in_specs += [pl.BlockSpec((v.shape[0], size), lambda t, me: (0, chunk_of(t, me))) for v in lefts]
    in_specs += [fixed(v) for v in rights]
    in_specs += [pl.BlockSpec((size, PAIR), lambda t, me: (chunk_of(t, me), pair)) for w in weights]
    out_specs = [
        pl.BlockSpec((size, n), lambda t, me: (jnp.minimum(t, steps // 2 - 1), 0)),
        pl.BlockSpec((size, n), lambda t, me: (jnp.maximum(t - steps // 2, 0), 0)),
    ]
    out_shape = [shape((m // 2, n), BF16)] * 2
    args = [side, *map(array_of, joins), *lefts, *map(array_of, rights), *weights]
    if extra:
        args.append(sums)
        in_specs.append(pl.BlockSpec(sums.shape, lambda t, me: (0, 0)))
        out_specs.append(pl.BlockSpec((8, size), lambda t, me: (0, chunk_of(t, me))))
        out_shape.append(shape((8, m), F32))
    return pl.pallas_call(
        functools.partial(gradient_kernel, steps, nl, nr, len(joins), extra),
        grid_spec=pltpu.PrefetchScalarGridSpec(
            num_scalar_prefetch=1, grid=(steps,), in_specs=in_specs, out_specs=out_specs
        ),
        out_shape=out_shape,
        compiler_params=PARAMS,
        cost_estimate=cost(4),
        name="gradient",
    )(*args)


def assemble_kernel(nx, cols, turned, side_ref, *refs):
    mine, came, outs = refs[:nx], refs[nx : 2 * nx], refs[2 * nx :]
    size = mine[0].shape[0]
    side = side_ref[0]
    n = len(outs) - (1 if turned else 0)
    for x in range(nx):
        for ref, first in ((mine[x], side * size), (came[x], (1 - side) * size)):
            first = pl.multiple_of(first, size)
            for j in range(n):
                made = ref[:, j * cols : (j + 1) * cols].astype(F32)
                outs[j][pl.ds(first, size), x * cols : (x + 1) * cols] = made
            if x == 0 and turned:
                outs[n][:, pl.ds(first, size)] = ref[:, n * cols :].astype(F32).T


def assemble(side, mine, came, cols, turned=0):
    size = mine[0].shape[0]
    n = (mine[0].shape[1] - turned) // cols
    out = [shape((2 * size, cols * len(mine)), F32)] * n
    if turned:
        out = out + [shape((turned, 2 * size), F32)]
    return pl.pallas_call(
        functools.partial(assemble_kernel, len(mine), cols, turned),
        out_shape=out,
        in_specs=[SMEM_SPEC] + [VMEM_SPEC] * (2 * len(mine)),
        out_specs=[VMEM_SPEC] * len(out),
        compiler_params=PARAMS,
        cost_estimate=cost(0),
        name="assemble",
    )(side, *mine, *came)


def place_half_kernel(side_ref, v_ref, *refs):
    del side_ref
    refs[-1][...] = v_ref[...].astype(F32)


def place_half(side, v, earlier=None, steps=2):
    size, n = v.shape
    tile = size // steps
    args, specs, aliases = [side, v], [pl.BlockSpec((tile, n), lambda t, side: (t, 0))], {}
    if earlier is not None:
        args.append(earlier)
        specs.append(pl.BlockSpec(memory_space=pl.ANY))
        aliases = {2: 0}
    return pl.pallas_call(
        place_half_kernel,
        grid_spec=pltpu.PrefetchScalarGridSpec(
            num_scalar_prefetch=1,
            grid=(steps,),
            in_specs=specs,
            out_specs=pl.BlockSpec((tile, n), lambda t, side: (side[0] * steps + t, 0)),
        ),
        out_shape=shape((2 * size, n), F32),
        input_output_aliases=aliases,
        compiler_params=PARAMS,
        cost_estimate=cost(0),
        name="place_half",
    )(*args)


def swap(value, axis, size, bit):
    return lax.ppermute(value, axis, [(i, i ^ bit) for i in range(size)])


def bits_of(size):
    return [1 << b for b in range(size.bit_length() - 1)]


def after(value, *others):
    return lax.optimization_barrier((value, *others))[0]


def spread_low(slots, axis, size, bits):
    slots = dict(slots)
    for bit in bits:
        slots.update({s | bit: swap(v, axis, size, bit) for s, v in slots.items()})
    return slots


def add_low(left, right):
    return (left.astype(F32) + right.astype(F32)).astype(BF16)


def direct_slots(value, axis, size):
    return [value] + [swap(value, axis, size, s) for s in range(1, size)]


class Scatter:
    def __init__(self, size):
        self.size = size
        self.low = bits_of(size)[:-1]
        self.top = size // 2

    def within(self, parts):
        held = {s: [v] for s, v in parts.items()}
        for bit in self.low:
            for s in sorted(held, reverse=True):
                if s & bit:
                    terms = held.pop(s)
                    total = terms[0]
                    for t in terms[1:]:
                        total = add_low(total, t)
                    held[s ^ bit].append(swap(total, "mp", self.size, bit))
        [(_, terms)] = held.items()
        return terms

    def across(self, terms):
        total = terms[0].astype(F32)
        for t in terms[1:]:
            total = total + t.astype(F32)
        total = total.astype(BF16)
        return total, swap(total, "mp", self.size, self.top)


class Stream:
    def __init__(self, dp, bits, send, keep):
        self.dp = dp
        self.index = lax.axis_index("dp")
        self.bits = bits
        self.stage = 0
        self.held = keep
        self.came = swap(send, "dp", dp, bits[0])

    def advance(self, *tie):
        n = len(self.bits)
        if self.stage == 2 * n - 1:
            return self.held
        held, came = after(self.held, *tie), after(self.came, *tie)
        self.stage += 1
        if self.stage <= n:
            cur = add_low(held, came)
            if self.stage == n:
                self.held = send = cur
                bit = self.bits[-1]
            else:
                bit = self.bits[self.stage]
                upper = (self.index & bit) != 0
                low, high = cur[: cur.shape[0] // 2], cur[cur.shape[0] // 2 :]
                send = jnp.where(upper, low, high)
                self.held = jnp.where(upper, high, low)
        else:
            upper = (self.index & self.bits[2 * n - self.stage]) != 0
            low, high = jnp.where(upper, came, held), jnp.where(upper, held, came)
            self.held = send = jnp.concatenate([low, high])
            bit = self.bits[2 * n - self.stage - 1]
        self.came = swap(send, "dp", self.dp, bit)
        return send

    def done(self, *tie):
        while self.stage < 2 * len(self.bits) - 1:
            self.advance(*tie)
        return self


class Direct:
    def __init__(self, dp, send, keep):
        self.dp = dp
        self.index = lax.axis_index("dp")
        self.held = keep
        self.came = swap(send, "dp", dp, 1)
        self.stage = 0

    def others(self, parts):
        return [parts[0]] + [swap(v, "dp", self.dp, 2 * j) for j, v in enumerate(parts) if j]

    def ordered(self, parts):
        bit = 2
        step = 1
        while step < len(parts):
            upper = (self.index & bit) != 0
            parts = [jnp.where(upper, parts[j ^ step], v) for j, v in enumerate(parts)]
            bit, step = 2 * bit, 2 * step
        return parts

    def advance(self, *tie):
        n = self.dp // 2
        self.stage += 1
        if self.stage == 1:
            total = add_low(after(self.held, *tie), after(self.came, *tie))
            size = total.shape[0] // n
            parts = self.ordered([total[j * size : (j + 1) * size] for j in range(n)])
            self.parts = self.others(parts)
            return parts[0]
        if self.stage == 2:
            total = sum(after(v, *tie).astype(F32) for v in self.parts).astype(BF16)
            self.parts = self.others([total] * n)
            return total
        if self.stage == 3:
            parts = [after(v, *tie) for v in self.parts]
            self.held = jnp.concatenate(self.ordered(parts))
            self.came = swap(self.held, "dp", self.dp, 1)
        return self.held

    def done(self, *tie):
        while self.stage < 3:
            self.advance(*tie)
        return self


def on_device(
    dp,
    mp,
    tokens,
    lengths,
    norm1_gain,
    norm1_shift,
    query_weight,
    query_bias,
    key_weight,
    value_weight,
    value_bias,
    head_scale,
    output_weight,
    output_bias,
    norm2_gain,
    norm2_shift,
    norm3_gain,
    norm3_shift,
    fc1_weight,
    fc1_bias,
    mid_gain,
    mid_shift,
    fc2_weight,
    fc2_bias,
    out_grad,
):
    tok, d = tokens.shape
    width = query_weight.shape[1]
    heads = width // HEAD_DIM
    pairs = width // PAIR
    half = mp // 2
    units = fc1_weight.shape[1]
    me = lax.axis_index("mp").astype(jnp.int32)
    me_arr = me[None]
    index = lax.axis_index("dp").astype(jnp.int32)
    plain = bits_of(dp)
    turned = [plain[1], plain[0], *plain[2:]]
    side, side_turned = (index & 1)[None], ((index >> 1) & 1)[None]
    lower = list(reversed(bits_of(mp)[:-1]))
    scatter = Scatter(mp)
    one_by_one = [[s] for s in range(half)]
    merged = [[0], [2], [1, 3]] if mp == 4 else [[s] for s in range(mp)]

    def merged_terms(outs, rows):
        if mp != 4:
            return scatter.within(dict(enumerate(outs[:half]))), scatter.within(
                {half + j: v for j, v in enumerate(outs[half:])}
            )
        came = swap(outs[2], "mp", mp, 1)
        return [outs[0], Window(came, 0, rows)], [outs[1], Window(came, rows, rows)]

    def plain_rows(v):
        return v.array[v.first : v.first + v.shape[0]] if isinstance(v, Window) else v

    def wide_swap(v):
        return swap(v, "mp", mp, half)

    def listed(near, far):
        slots = {**near, **far}
        return [slots[s] for s in range(mp)]

    def row(v):
        return v[None]

    qkv_weights = (query_weight, key_weight, value_weight)
    bias_qkv = jnp.concatenate([query_bias, jnp.zeros_like(query_bias), value_bias])[None]
    scale_lanes = jnp.repeat(head_scale, HEAD_DIM)[None]
    place = me * tok + lax.broadcasted_iota(jnp.int32, (tok, 1), 0)
    cot_low = jnp.where(place < jnp.sum(lengths), out_grad, jnp.zeros_like(out_grad))

    normed_own = first_norm(tokens, row(norm1_gain), row(norm1_shift))
    normed_far = wide_swap(normed_own)
    normed_near = spread_low({0: normed_own}, "mp", mp, lower)
    start = normed_near[half - 1]
    qkv = qkv_part([normed_near[s] for s in range(half)], qkv_weights, bias_qkv, 0)
    cot_low, output_weight = (after(v, start) for v in (cot_low, output_weight))
    cot_near = spread_low({0: cot_low}, "mp", mp, lower)
    out_near = spread_low({0: output_weight}, "mp", mp, lower)
    both = jnp.concatenate([cot_low, output_weight])
    hg_near = hidden_gradient([after(cot_near[s], qkv) for s in range(half)], fc2_weight)
    normed_far = after(normed_far, hg_near, both, out_near[half - 1])
    both_far = wide_swap(after(both, normed_far))
    normed_far = spread_low({half: normed_far}, "mp", mp, lower)
    qkv = qkv_part([normed_far[half + s] for s in range(half)], qkv_weights, bias_qkv, 1, qkv)
    normed = listed(normed_near, normed_far)

    far_first = [*range(half, mp), *range(1, half)]
    atts, lses, mixed = [], [], [[] for _ in range(mp)]
    mark = (qkv,)
    for p in range(pairs):
        att, lse, mix = attend_forward(me_arr, lengths, after(qkv, *mark), scale_lanes, tok, p)
        atts.append(att)
        lses.append(lse)
        if p > 0:
            mix = [after(v, *(m[-1] for m in mixed[1:])) for v in mix]
        mixed[0].append(mix[0])
        for s in far_first:
            mixed[s].append(swap(mix[s], "mp", mp, s))
        mark = (mix[0],)
    both_far = spread_low({half: after(both_far, mix[0])}, "mp", mp, lower)
    cot_far = {s: Window(v, 0, tok) for s, v in both_far.items()}
    out_far = {s: Window(v, tok, width) for s, v in both_far.items()}
    out_rows = listed(out_near, out_far)
    branch, residual, ffn_own = after_attention(
        mixed,
        out_rows,
        tokens,
        *(row(v) for v in (output_bias, norm2_gain, norm2_shift, norm3_gain, norm3_shift)),
    )

    ffn_far = wide_swap(ffn_own)
    ffn_near = spread_low({0: ffn_own}, "mp", mp, lower)
    scale_slots = direct_slots(after(scale_lanes, ffn_own), "mp", mp)
    cots, ffn_near = listed(cot_near, cot_far), [ffn_near[s] for s in range(half)]
    ffn_args = (fc1_weight, row(fc1_bias), row(mid_gain))
    u_near, st_near = ffn_first(ffn_near, hg_near, *ffn_args)
    cot_ready = Window(after(cots[half].array, st_near), 0, tok)
    hg_far = hidden_gradient([cot_ready, *cots[half + 1 :]], fc2_weight)
    ffn_far = spread_low({half: after(ffn_far, hg_far)}, "mp", mp, lower)
    ffn_in = ffn_near + [ffn_far[half + s] for s in range(half)]
    ffn_args = (fc1_weight, after(row(fc1_bias), *scale_slots[1:]), row(mid_gain))
    u_far, st_far = ffn_first(ffn_in[half:], hg_far, *ffn_args)
    stats = direct_slots(jnp.concatenate([st_near, st_far], axis=1), "mp", mp)
    ffn_args = (row(mid_gain), row(mid_shift), fc1_weight, stats, tok)
    hid, fg, mid_far, back_far = ffn_second(u_far, hg_far, *ffn_args, 1)
    back_far = scatter.within({half + j: v for j, v in enumerate(back_far)})
    hid, fg, mid_near, back_near = ffn_second(u_near, hg_near, *ffn_args, 0, (hid, fg))
    scale_slots = jnp.concatenate(scale_slots, axis=1)
    back_far[1:] = [after(v, mid_near) for v in back_far[1:]]
    back_sum, back_far = scatter.across(back_far)
    back_near = scatter.within(dict(enumerate(back_near)))

    send, keep = gradient(side, [after(hid, back_sum)], cots)
    fc2 = Stream(dp, plain, send, keep)
    send, keep = gradient(side_turned, ffn_in, [after(fg, send)])
    fc1 = Stream(dp, turned, send, keep)
    came = [after(v, send) for v in (*back_near, back_far)]
    residual_grad, branch_low, sums, grads = before_attention(
        came, residual, branch, cot_low, row(norm3_gain), row(norm2_gain), scale_slots, out_rows
    )

    do = {s: swap(grads[s], "mp", mp, s) for s in far_first}
    do = [grads[0]] + [do[s] for s in range(1, mp)]
    mark = fc2.advance(branch_low)
    low = after(branch_low, mark, *do[1:half])
    g_near_terms, g_far_terms = merged_terms(head_gradient(mixed, low, merged), d)
    outs = products([after(hid, g_near_terms[0])], [fc2_weight], False, tok, half, one_by_one)
    out_far_terms = scatter.within({half + j: v for j, v in enumerate(outs)})
    mark = fc1.advance(outs[0])
    do[half:] = [after(v, mark) for v in do[half:]]
    mark = do[-1]
    g_far_terms = [after(plain_rows(v), mark) for v in g_far_terms]
    g_out_sum, g_out_top = scatter.across(g_far_terms)
    mark = fc2.advance(g_out_sum)

    dqkvs, sums_att, rows, streams = [], [], [], []

    def between(call):
        nonlocal mark
        nonlocal out_top
        if call == 0:
            mark = fc2.advance(mark)
            mark = fc1.advance(mark)
            out_sum, out_top = scatter.across([after(v, mark) for v in out_far_terms])
            mark = out_sum
        elif call == 1:
            mark = fc2.advance(after(mark, g_out_top))
        elif call == 2:
            mark = fc1.advance(mark)
            mark = fc2.advance(mark)
            for stream in streams:
                mark = stream.advance(mark)

    call, out_top = 0, None
    for p in range(pairs):
        held = ()
        for turn in range(2):
            held = attend_backward(
                me_arr, lengths, after(qkv, mark), atts[p], lses[p], do, tok, p, turn, held
            )
            mark = held[0]
            between(call)
            call += 1
        dqkv, sum_att, _ = held
        dqkvs.append(dqkv)
        sums_att.append(sum_att)
        if p < pairs - 1:
            joins = [*g_near_terms, g_out_top] if p == 0 else ()
            send, keep, r = gradient(
                side, normed, [after(dqkv, mark)], qkv_weights, p, sum_att, joins
            )
            rows.append(r)
            streams.append(Stream(dp, plain, send, keep))
            mark = fc1.advance(send)

    mark = after(mark, out_top)
    for stream in streams:
        mark = stream.advance(mark)
    mark = fc1.advance(mark)
    joins = [*g_near_terms, g_out_top] if pairs == 1 else ()
    send, keep, r = gradient(
        side, normed, [after(dqkvs[-1], mark)], qkv_weights, pairs - 1, sums_att[-1], joins
    )
    rows.append(r)
    last = Direct(dp, send, keep)
    mark = send
    for stream in streams:
        mark = stream.advance(mark)
    packed = jnp.concatenate([sums[:6], sum(rows)[:2]])
    packed = jnp.broadcast_to(after(packed, mark)[None], (mp, *packed.shape))
    sent = packed
    packed = lax.all_to_all(packed, "mp", 0, 0)
    far = products([after(v, sent) for v in dqkvs], qkv_weights, True, tok, half, one_by_one)
    far_terms = scatter.within({half + j: v for j, v in enumerate(far)})
    mark = far[0]
    for stream in streams:
        mark = stream.advance(mark)
    near = products([after(v, mark) for v in dqkvs], qkv_weights, True, tok, 0, one_by_one)
    far_terms[1:] = [after(v, near[0]) for v in far_terms[1:]]
    far_sum, far_top = scatter.across(far_terms)
    near_terms = scatter.within(dict(enumerate(near)))
    mark = last.advance(far_sum)
    fc2.done(mark)
    [grad_fc2_weight] = assemble(side, [after(fc2.held, mark)], [fc2.came], fc2.held.shape[1])
    mark = grad_fc2_weight
    for stream in streams:
        mark = stream.advance(mark)
    mark = last.advance(mark)
    packed = after(packed, mark).sum(0)
    mids = jnp.pad(mid_near + mid_far, ((0, 0), (0, d - units)))[:4]
    heads_sums = jnp.concatenate(sums_att, axis=1)
    heads_sums = jnp.pad(heads_sums, ((0, 3), (0, d - heads_sums.shape[1])))
    packed = jnp.concatenate([packed, mids, heads_sums])
    packed = jnp.broadcast_to(packed[None], (dp, *packed.shape))
    sent = packed
    packed = lax.all_to_all(packed, "dp", 0, 0)
    mark = last.advance(sent)
    outs = products([after(hid, mark)], [fc2_weight], False, tok, 0, one_by_one, 0)
    out_near_terms = scatter.within(dict(enumerate(outs)))
    token_grad = last_norm(
        [*near_terms, after(far_top, outs[0], *(v.came for v in streams))], tokens, residual_grad, row(norm1_gain)
    )
    output = residual + row(fc2_bias)
    for t in (*out_near_terms, out_top):
        output = output + after(t, token_grad).astype(F32)
    output = output.astype(BF16)
    packed = after(packed, output).sum(0)
    fc1.done(output)
    for stream in (*streams, last):
        stream.done(output)
    streams.append(last)
    grad_query_weight, grad_key_weight, grad_value_weight, grad_output_weight = assemble(
        side, [after(v.held, packed) for v in streams], [v.came for v in streams], PAIR, width
    )
    own_half = place_half(side_turned, after(fc1.held, grad_query_weight))
    came = after(fc1.came, own_half)
    grad_fc1_weight = place_half(1 - side_turned, came, own_half)
    shift1 = packed[7]
    gain1 = (packed[6] - norm1_shift * shift1) / norm1_gain
    per_head = packed[12, : 4 * width].reshape(pairs, 4, PAIR)
    return (
        output,
        token_grad,
        gain1,
        shift1,
        grad_query_weight,
        per_head[:, 0].reshape(width),
        grad_key_weight,
        grad_value_weight,
        per_head[:, 2].reshape(width),
        jnp.sum(per_head[:, 3].reshape(heads, HEAD_DIM), 1) / head_scale,
        grad_output_weight,
        packed[4],
        packed[0],
        packed[1],
        packed[2],
        packed[3],
        grad_fc1_weight,
        packed[10, :units],
        packed[8, :units],
        packed[9, :units],
        grad_fc2_weight,
        packed[5],
    )


def solution(mesh):
    own = P(("dp", "mp"), None)
    cols, rows, vec, same = P(None, "mp"), P("mp", None), P("mp"), P()
    ends = (cols, vec, vec, vec, rows, same)
    norms = (same,) * 5
    in_specs = (own, P("dp", None), same, same, cols, vec, cols, cols, vec, vec, rows, *norms, *ends, own)
    out_specs = (own, own, same, same, cols, vec, cols, cols, vec, vec, rows, *norms, *ends)
    return jax.shard_map(
        functools.partial(on_device, mesh.shape["dp"], mesh.shape["mp"]),
        mesh=mesh,
        in_specs=in_specs,
        out_specs=out_specs,
        check_vma=False,
    )
```
